32 devices in a mesh: dp: 4 (over z), fsdp: 8 (over y, x, core).
Axes of the slice: x: 2, y: 2, z: 4, core: 2. Of those that a mesh axis runs over, the one named last changes fastest.
Arguments:
- tokens: bfloat16 [32768, 512], P(('dp', 'fsdp')), may hold values from -6 to 6
- chain_ids: int32 [32, 1024], P(('dp', 'fsdp')), may hold values from 0 to 127, as said below
- qkv_weight: bfloat16 [512, 1536], P(('dp', 'fsdp')), may hold values from -0.25 to 0.25
- mix_weight: bfloat16 [512, 512], P(('dp', 'fsdp')), may hold values from -0.75 to 0.75
- up_weight: bfloat16 [512, 2048], P(('dp', 'fsdp')), may hold values from -0.25 to 0.25
- down_weight: bfloat16 [2048, 512], P(('dp', 'fsdp')), may hold values from -0.125 to 0.125
- norm_gain: bfloat16 [2, 512], P(None, ('dp', 'fsdp')), may hold values from 0.5 to 1.5
- norm_bias: bfloat16 [2, 512], P(None, ('dp', 'fsdp')), may hold values from -1.796875 to 1.796875
- qv_bias: bfloat16 [2, 512], P(None, ('dp', 'fsdp')), may hold values from -1.796875 to 1.796875
- proj_bias: bfloat16 [2, 512], P(None, ('dp', 'fsdp')), may hold values from -1.796875 to 1.796875
- up_bias: bfloat16 [2048], P(('dp', 'fsdp')), may hold values from -1.796875 to 1.796875
- cotangent: bfloat16 [32768, 512], P(('dp', 'fsdp')), may hold values from -6 to 6
Outputs:
- output: bfloat16 [32768, 512], P(('dp', 'fsdp'))
- input_grad: float32 [32768, 512], P(('dp', 'fsdp'))
- qkv_grad: float32 [512, 1536], P(('dp', 'fsdp'))
- mix_grad: float32 [512, 512], P(('dp', 'fsdp'))
- up_grad: float32 [512, 2048], P(('dp', 'fsdp'))
- down_grad: float32 [2048, 512], P(('dp', 'fsdp'))
- norm_gain_grad: float32 [2, 512], P(None, ('dp', 'fsdp'))
- norm_bias_grad: float32 [2, 512], P(None, ('dp', 'fsdp'))
- qv_bias_grad: float32 [2, 512], P(None, ('dp', 'fsdp'))
- proj_bias_grad: float32 [2, 512], P(None, ('dp', 'fsdp'))
- up_bias_grad: float32 [2048], P(('dp', 'fsdp'))
The draws below stay inside these ranges and needn't reach their ends.
Inputs may be any that keep to these rules, and one draw needn't show every extreme that they name: `chain_ids`: in each row (the residues of one device) the chain numbers start at 0 and never fall; residues with one number form one chain, and a new chain begins only at a position that is a multiple of 8. In every draw some device holds a single chain of all 1024 residues.
All inputs are finite; a program needn't handle non-finite values.
Results may differ from the reference program's by a relative error of at most 0.0093.
Values may be sent and summed in bfloat16 or wider, within the bound.
No kernel may reach another device: no remote copies, remote signals or barrier semaphores. Data moves between devices by JAX's collectives and lax.ppermute only.
A program may use at most 256 MiB of HBM per device.

```python
import jax
import jax.numpy as jnp
from jax import lax

D = 512
HEADS = 8
FF = 2048
TOK_DEV = 1024
TOKENS = 32768
DEVICES = 32


def draw_chain_ids(key, part):
    first_key, second_key, third_key, fourth_key = jax.random.split(jax.random.fold_in(key, 17), 4)
    exponent = jax.random.randint(first_key, (DEVICES, 1), 0, 7)
    random_bits = jax.random.randint(second_key, (DEVICES, TOK_DEV), 0, 1048576)
    period = jnp.left_shift(jnp.ones((DEVICES, 1), jnp.int32), exponent)
    row_index = lax.broadcasted_iota(jnp.int32, (DEVICES, TOK_DEV), 0)
    col_index = lax.broadcasted_iota(jnp.int32, (DEVICES, TOK_DEV), 1)
    single = jax.random.randint(third_key, (), 0, DEVICES)
    regular = (single + 1 + jax.random.randint(fourth_key, (), 0, DEVICES - 1)) % DEVICES
    on_grid = col_index % 8 == 0
    starts = on_grid & ((random_bits % period == 0) | (row_index == regular))
    starts = starts & (row_index != single) & (col_index > 0)
    return jnp.cumsum(starts.astype(jnp.int32), axis=1).astype(jnp.int32)


def levels(own_key, extent, shards, smallest, high):
    def one(position, blocks):
        heights = jax.random.uniform(jax.random.fold_in(jax.random.fold_in(own_key, 6), position), (blocks,), jnp.float32, smallest / len(shards), high / len(shards))
        return jnp.repeat(jnp.exp(heights), extent[position] // blocks).reshape((-1,) + (1,) * (len(extent) - position - 1))

    factor_of = one(*shards[0])
    for cut in shards[1:]:
        factor_of = factor_of * one(*cut)
    return factor_of


def bell_draw(rng, shape, scale, bound, shards=(), dtype=jnp.bfloat16):
    gain = levels(rng, shape, shards, -0.22, 0.18) if shards else 1.0
    values = jax.random.normal(rng, shape, jnp.float32) * scale * gain
    return jnp.minimum(jnp.maximum(values, -bound), bound).astype(dtype)


def setup_inputs(seed: int = 0) -> dict:
    splits = jax.random.split(jax.random.key(seed), 13)
    return {
        "tokens": bell_draw(splits[0], (TOKENS, D), 1.0, 6.0, ((0, 32),)),
        "chain_ids": draw_chain_ids(jax.random.fold_in(splits[12], 71), 0),
        "qkv_weight": bell_draw(splits[2], (D, 3 * D), D ** -0.5, 0.25, ((0, 32),)),
        "mix_weight": bell_draw(splits[3], (D, D), (D // 8) ** -0.5, 0.75, ((0, 32),)),
        "up_weight": bell_draw(splits[4], (D, FF), D ** -0.5, 0.25, ((0, 32),)),
        "down_weight": bell_draw(splits[5], (FF, D), FF ** -0.5, 0.125, ((0, 32),)),
        "norm_gain": jnp.clip(1.0 + 0.1 * jax.random.normal(splits[6], (2, D), jnp.float32), 0.5, 1.5).astype(jnp.bfloat16),
        "norm_bias": bell_draw(splits[7], (2, D), 0.3, 1.796875, ((1, 32),)),
        "qv_bias": bell_draw(splits[8], (2, D), 0.3, 1.796875, ((1, 32),)),
        "proj_bias": bell_draw(splits[9], (2, D), 0.3, 1.796875, ((1, 32),)),
        "up_bias": bell_draw(splits[10], (FF,), 0.3, 1.796875, ((0, 32),)),
        "cotangent": bell_draw(splits[11], (TOKENS, D), 1.0, 6.0, ((0, 32),)),
    }


NEG = -1e+30
EPS = 1e-05

@jax.custom_vjp
def low(v):
    return lax.optimization_barrier(v.astype(jnp.bfloat16)).astype(jnp.float32)

@jax.custom_vjp
def low_back(v):
    return v

def low_keep(v):
    return (low(v), None)

def low_pass(kept, grad):
    return (grad,)

def back_keep(v):
    return (v, None)

def back_low(kept, grad):
    return (low(grad),)
low.defvjp(low_keep, low_pass)
low_back.defvjp(back_keep, back_low)

def normalize(rows_in, gain_row, shift_row):
    row_mean = lax.optimization_barrier(jnp.mean(rows_in, axis=-1, keepdims=True))
    centred = rows_in - row_mean
    spread = lax.optimization_barrier(jnp.mean(centred * centred, axis=-1, keepdims=True))
    return centred * lax.rsqrt(spread + EPS) * gain_row + shift_row

def layer(stream, chains, params):
    qkv_weight, mix_weight, up_weight, down_weight, norm_gain, norm_bias, qv_bias, proj_bias, up_bias = params
    high = lax.Precision.HIGHEST
    head_size = D // HEADS
    normed = low(normalize(stream, norm_gain[0], norm_bias[0]))
    mixed_rows = jnp.dot(normed, qkv_weight, precision=high)
    queries = low(low_back(mixed_rows[:, :D] + qv_bias[0])).reshape(TOK_DEV, HEADS, head_size)
    key_rows = low(low_back(mixed_rows[:, D:2 * D])).reshape(TOK_DEV, HEADS, head_size)
    values = low(low_back(mixed_rows[:, 2 * D:] + qv_bias[1])).reshape(TOK_DEV, HEADS, head_size)
    scores = low_back(jnp.einsum('qhe,khe->hqk', queries, key_rows, precision=high) * 0.125)
    allowed = (chains[:, None] == chains[None, :])[None]
    masked = jnp.where(allowed, scores, NEG)
    log_total = jax.nn.logsumexp(masked, axis=-1, keepdims=True)
    attn_probs = low(jnp.where(allowed, jnp.exp(masked - log_total), 0.0))
    attended = jnp.einsum('hqk,khe->qhe', attn_probs, values, precision=high).reshape(TOK_DEV, D)
    attended = low(low_back(attended))
    middle = stream + low_back(jnp.dot(attended, mix_weight, precision=high) + proj_bias[0])
    normed_two = low(normalize(middle, norm_gain[1], norm_bias[1]))
    pre_act = low_back(jnp.dot(normed_two, up_weight, precision=high) + up_bias)
    activated = low(jax.nn.gelu(pre_act, approximate=False))
    return middle + low_back(jnp.dot(activated, down_weight, precision=high) + proj_bias[1])

def reference(tokens, chain_ids, qkv_weight, mix_weight, up_weight, down_weight, norm_gain, norm_bias, qv_bias, proj_bias, up_bias, cotangent):
    params = (qkv_weight.astype(jnp.float32), mix_weight.astype(jnp.float32), up_weight.astype(jnp.float32), down_weight.astype(jnp.float32), norm_gain.astype(jnp.float32), norm_bias.astype(jnp.float32), qv_bias.astype(jnp.float32), proj_bias.astype(jnp.float32), up_bias.astype(jnp.float32))
    stream_all = tokens.astype(jnp.float32).reshape(DEVICES, TOK_DEV, D)

    def forward(stream_in, param_set):

        def one_block(paired):
            return layer(paired[0], paired[1], param_set)
        return lax.map(jax.checkpoint(one_block), (stream_in, chain_ids))
    result, pullback = jax.vjp(forward, stream_all, params)
    grad_stream, grad_params = pullback(cotangent.astype(jnp.float32).reshape(DEVICES, TOK_DEV, D))
    qkv_grad, mix_grad, up_grad, down_grad, gain_grad, shift_grad, qv_grad, proj_grad, up_bias_grad = grad_params
    return (result.reshape(TOKENS, D).astype(jnp.bfloat16), grad_stream.reshape(TOKENS, D), qkv_grad, mix_grad, up_grad, down_grad, gain_grad, shift_grad, qv_grad, proj_grad, up_bias_grad)
```

```python
import math

import jax
import jax.numpy as jnp
from jax import lax
from jax.experimental import pallas as pl
from jax.experimental.pallas import tpu as pltpu
from jax.sharding import PartitionSpec as P

AXES = ("dp", "fsdp")
HEADS = 8
EPS = 1e-05
SCALE = 0.125
EXP_SCALE = SCALE * math.log2(math.e)
HIDE = -(2.0**60)
MIB = 2**20

BF = jnp.bfloat16
F32 = jnp.float32
NN = (((1,), (0,)), ((), ()))
NT = (((1,), (1,)), ((), ()))
TN = (((0,), (0,)), ((), ()))


def dot(a, b, dims=NN):
    return lax.dot_general(a, b, dims, preferred_element_type=F32)


def vmem():
    return pl.BlockSpec(memory_space=pltpu.VMEM)


def smem():
    return pl.BlockSpec(memory_space=pltpu.SMEM)


def shape(dims, dtype):
    return jax.ShapeDtypeStruct(dims, dtype)


def slots():
    return [(c, j, i) for c in range(2) for j in range(4) for i in range(4)]


def block_row(me, c, j, i, rows):
    return pl.multiple_of((me ^ (c | (j << 1) | (i << 3))) * rows, rows)


def row_stats(rows_in):
    mean = jnp.mean(rows_in, axis=-1, keepdims=True)
    centred = rows_in - mean
    spread = jnp.mean(centred * centred, axis=-1, keepdims=True)
    return centred, lax.rsqrt(spread + EPS)


def split_three(row):
    first = row.astype(BF).astype(F32)
    rest = row - first
    second = rest.astype(BF).astype(F32)
    return first, second, rest - second


def pack_kernel(qkv, mix, up, down, gain, shift, qv, proj, up_bias, a0, a1, b0, b1, rows128):
    for pair in range(4):
        target, base = (a0, a1)[pair // 2], (pair % 2) * 384
        for part in range(3):
            target[:, base + 128 * part : base + 128 * part + 128] = qkv[
                :, 512 * part + 128 * pair : 512 * part + 128 * pair + 128
            ]
    rows128[...] = jnp.zeros_like(rows128)
    for index, ref in enumerate((gain, shift, qv, proj)):
        rows128[2 * index : 2 * index + 2, :] = ref[...].astype(F32)
    eye = (
        lax.broadcasted_iota(jnp.int32, (16, 16), 0) == lax.broadcasted_iota(jnp.int32, (16, 16), 1)
    ).astype(F32)
    columns = dot(eye.astype(BF), rows128[...].astype(BF), NT)
    bias = jnp.concatenate([jnp.zeros((1, 64), F32), up_bias[...].astype(F32)], axis=1)
    row = lax.broadcasted_iota(jnp.int32, (16, 128), 0)
    lane = lax.broadcasted_iota(jnp.int32, (16, 128), 1)
    a0[:, 768:896] = jnp.where((row == 0) & (lane >= 64), bias, columns).astype(BF)
    b0[:, 0:512] = mix[...]
    b0[:, 512:2560] = up[...]
    for part in range(4):
        b1[:, 512 * part : 512 * part + 512] = down[16 * part : 16 * part + 16, :]


def pack(qkv, mix, up, down, gain, shift, qv, proj, up_bias):
    return pl.pallas_call(
        pack_kernel,
        in_specs=[vmem()] * 9,
        out_specs=[vmem()] * 4,
        out_shape=[
            shape((16, 896), BF),
            shape((16, 768), BF),
            shape((16, 2560), BF),
            shape((16, 2048), BF),
        ],
        scratch_shapes=[pltpu.VMEM((128, 16), F32)],
        name="pack",
    )(qkv, mix, up, down, gain, shift, qv, proj, up_bias.reshape(1, 64))


def aux_rows(chain):
    row = lax.broadcasted_iota(jnp.int32, (128, chain.shape[1]), 0)
    low_bits = jnp.where(row < 7, (chain >> jnp.minimum(row, 6)) & 1, 0)
    high_bits = jnp.where(
        (row >= 7) & (row < 14), 1 - ((chain >> jnp.minimum(jnp.maximum(row - 7, 0), 6)) & 1), 0
    )
    bits = low_bits + high_bits
    query_side = bits.astype(F32) * HIDE
    key_side = jnp.where(row < 14, 1 - bits, jnp.where(row < 17, 1, 0)).astype(F32)
    return query_side.astype(BF), key_side.T.astype(BF)


def pair_forward(normed, weight, bias_q, bias_v, key_aux, qa, ot, outs, pair, block):
    q_out, k_out, v_out, o_out, ot_out, lse_out = outs
    rows = normed.shape[0]
    cols = slice(128 * pair, 128 * pair + 128)
    q2 = (dot(normed, weight[:, 0:128]) + bias_q).astype(BF)
    k2 = dot(normed, weight[:, 128:256]).astype(BF)
    v2 = (dot(normed, weight[:, 256:384]) + bias_v).astype(BF)
    q_out[:, cols] = q2
    k_out[:, cols] = k2
    v_out[:, cols] = v2
    qa[0:128, :] = q2.T
    vt = v2.T
    ones = (lax.broadcasted_iota(jnp.int32, (16, rows), 0) == 0).astype(F32).astype(BF)
    lane = lax.broadcasted_iota(jnp.int32, k2.shape, 1)
    zero = jnp.zeros_like(k2)
    keys = [
        jnp.concatenate([jnp.where((lane >= 64) == bool(h), k2, zero), key_aux], axis=1)
        for h in range(2)
    ]
    vts = [jnp.concatenate([vt[64 * h : 64 * h + 64], ones], axis=0) for h in range(2)]
    count = rows // block

    def score(index):
        q_cols = qa[:, block * index : block * index + block]
        return [dot(keys[h], q_cols) for h in range(2)]

    ahead = score(0)
    for index in range(count):
        scores = ahead
        if index + 1 < count:
            ahead = score(index + 1)
        span = slice(block * index, block * index + block)
        for h in range(2):
            peak = jnp.max(scores[h], axis=0, keepdims=True)
            probs = jnp.exp2((scores[h] - peak) * EXP_SCALE).astype(BF)
            mixed = dot(vts[h], probs)
            total = mixed[64:65]
            ot[64 * h : 64 * h + 64, span] = mixed[:64] * (1.0 / total)
            lse_out[2 * pair + h : 2 * pair + h + 1, span] = peak + jnp.log(total) * (1.0 / SCALE)
    ot_out[128 * pair : 128 * pair + 128, :] = ot[...].astype(BF)
    o_out[:, cols] = ot[...].T.astype(BF)


def assemble(me, mine, other, target, width):
    for c, j, i in slots():
        source = (mine, other)[c]
        target[pl.ds(block_row(me, c, j, i, 16), 16), :] = source[4 * j + i, :, 0:width]


def forward_first_kernel(
    me_ref, tokens, chain, mine, other,
    q_out, k_out, v_out, o_out, ot_out, lse_out, weight, normed_out, normed_t, smalls, up_row,
    key_aux_out, query_aux_out, qa, ot, columns,
):
    me = me_ref[0]
    assemble(me, mine, other, weight, 768)
    for c, j, i in slots():
        source = (mine, other)[c]
        columns[pl.ds(block_row(me, c, j, i, 16), 16), :] = source[4 * j + i, :, 768:896].astype(F32)
    smalls[...] = columns[...].T[0:8, :]
    lane = lax.broadcasted_iota(jnp.int32, (1, 128), 1)
    for a in range(16):
        even = pltpu.roll(columns[32 * a : 32 * a + 8, :], 64, 1)[0:1, :]
        odd = columns[32 * a + 16 : 32 * a + 17, :]
        up_row[:, 128 * a : 128 * a + 128] = jnp.where(lane < 64, even, odd)
    query_side, key_side = aux_rows(chain[...])
    qa[128:256, :] = query_side
    query_aux_out[...] = query_side
    key_aux_out[...] = key_side

    def norm_block(index, carry):
        span = pl.ds(pl.multiple_of(index * 256, 256), 256)
        centred, scale = row_stats(tokens[span, :].astype(F32))
        normed_out[span, :] = (centred * scale * smalls[0:1, :] + smalls[2:3, :]).astype(BF)
        return carry

    lax.fori_loop(0, tokens.shape[0] // 256, norm_block, 0)
    normed = normed_out[...]
    normed_t[0:512, :] = normed.T
    ones_row = lax.broadcasted_iota(jnp.int32, (16, normed.shape[0]), 0) == 0
    normed_t[512:528, :] = ones_row.astype(F32).astype(BF)
    outs = (q_out, k_out, v_out, o_out, ot_out, lse_out)
    for pair in range(2):
        cols = slice(128 * pair, 128 * pair + 128)
        pair_forward(
            normed, weight[:, 384 * pair : 384 * pair + 384], smalls[4:5, cols], smalls[5:6, cols],
            key_side, qa, ot, outs, pair, 512,
        )


def forward_second_kernel(
    me_ref, normed_in, mine, other, smalls, key_aux, query_aux,
    q_out, k_out, v_out, o_out, ot_out, lse_out, weight, qa, ot,
):
    me = me_ref[0]
    assemble(me, mine, other, weight, 768)
    qa[128:256, :] = query_aux[...]
    normed = normed_in[...]
    outs = (q_out, k_out, v_out, o_out, ot_out, lse_out)
    for pair in range(2):
        cols = slice(256 + 128 * pair, 256 + 128 * pair + 128)
        pair_forward(
            normed, weight[:, 384 * pair : 384 * pair + 384], smalls[4:5, cols], smalls[5:6, cols],
            key_aux[...], qa, ot, outs, pair, 512,
        )


def forward_shapes(rows):
    return [shape((rows, 256), BF)] * 4 + [
        shape((256, rows), BF),
        shape((4, rows), F32),
        shape((512, 768), BF),
    ]


def forward_scratch(rows):
    return [pltpu.VMEM((256, rows), BF), pltpu.VMEM((128, rows), F32)]


def forward_first(me, tokens, chain, mine, other):
    rows = tokens.shape[0]
    return pl.pallas_call(
        forward_first_kernel,
        in_specs=[smem()] + [vmem()] * 4,
        out_specs=[vmem()] * 13,
        out_shape=forward_shapes(rows)
        + [
            shape((rows, 512), BF),
            shape((528, rows), BF),
            shape((8, 512), F32),
            shape((1, 2048), F32),
            shape((rows, 128), BF),
            shape((128, rows), BF),
        ],
        scratch_shapes=forward_scratch(rows) + [pltpu.VMEM((512, 128), F32)],
        compiler_params=pltpu.CompilerParams(vmem_limit_bytes=40 * MIB),
        name="attend_first",
    )(me, tokens, chain, mine, other)


def forward_second(me, normed, mine, other, smalls, key_aux, query_aux):
    rows = normed.shape[0]
    return pl.pallas_call(
        forward_second_kernel,
        in_specs=[smem()] + [vmem()] * 6,
        out_specs=[vmem()] * 7,
        out_shape=forward_shapes(rows),
        scratch_shapes=forward_scratch(rows),
        compiler_params=pltpu.CompilerParams(vmem_limit_bytes=40 * MIB),
        name="attend_second",
    )(me, normed, mine, other, smalls, key_aux, query_aux)


def gelu_parts(u):
    half_cdf = 0.5 + 0.5 * lax.erf(u * math.sqrt(0.5))
    density = jnp.exp2(u * u * (-0.5 * math.log2(math.e))) * (1.0 / math.sqrt(2.0 * math.pi))
    return u * half_cdf, half_cdf + u * density


def scatter_blocks(me, source, rows, base_block, blocks, send, keep, span):
    core = me & 1
    for half in range(blocks // 2):
        first = base_block + 2 * half
        row = 2 * half * rows
        r = (me ^ first) >> 1
        place = ((r & 3) << 2) | (r >> 2)
        kept = source[pl.ds(pl.multiple_of(row + core * rows, rows), rows), :]
        sent = source[pl.ds(pl.multiple_of(row + (1 - core) * rows, rows), rows), :]
        keep[place, :, span] = kept
        send[place, :, span] = sent.astype(BF)


def feed_kernel(
    me_ref, tokens, o_first, o_second, ot_first, ot_second, mine_a, other_a, mine_b, other_b,
    smalls, up_row, cot,
    output, grad_middle, grad_att, d_send, d_keep, u_send, u_keep, m_send, m_keep, small_grads,
    up_bias_grad, mix, up, down, middle, normed, normed_t, total, back, stage_d, stage_u, stats,
):
    me = me_ref[0]
    for c, j, i in slots():
        first, second = ((mine_a, mine_b), (other_a, other_b))[c]
        row = block_row(me, c, j, i, 16)
        mix[pl.ds(row, 16), :] = first[4 * j + i, :, 0:512]
        up[pl.ds(row, 16), :] = first[4 * j + i, :, 512:2560]
        for part in range(4):
            row4 = pl.multiple_of(block_row(me, c, j, i, 64) + 16 * part, 16)
            down[pl.ds(row4, 16), :] = second[4 * j + i, :, 512 * part : 512 * part + 512]
    rows = tokens.shape[0]
    block = 256
    count = rows // block

    def ahead(index, carry):
        span = pl.ds(pl.multiple_of(index * block, block), block)
        att = jnp.concatenate([o_first[span, :], o_second[span, :]], axis=1)
        mid = tokens[span, :].astype(F32) + dot(att, mix[...]) + smalls[6:7, :]
        middle[span, :] = mid
        centred, scale = row_stats(mid)
        normed[span, :] = (centred * scale * smalls[1:2, :] + smalls[3:4, :]).astype(BF)
        total[span, :] = mid + smalls[7:8, :]
        return carry

    lax.fori_loop(0, count, ahead, 0)
    back[...] = jnp.zeros_like(back)
    normed_t[0:512, :] = normed[...].T
    ones_row = lax.broadcasted_iota(jnp.int32, (16, rows), 0) == 0
    normed_t[512:528, :] = ones_row.astype(F32).astype(BF)

    width = 512
    for chunk in range(2048 // width):
        span = slice(chunk * width, chunk * width + width)
        up_part = up[:, span]
        down_part = down[span, :]
        act_parts = []
        pre = dot(normed[...], up_part) + up_row[:, span]
        act, slope = gelu_parts(pre)
        act_low = act.astype(BF)
        grad_pre = (dot(cot[...], down_part, NT) * slope).astype(BF)
        total[...] += dot(act_low, down_part)
        stage_d[...] = dot(act_low, cot[...], TN)
        back[...] += dot(grad_pre, up_part, NT)
        stage_u[...] = dot(normed_t[...], grad_pre)
        up_bias_grad[:, span] = stage_u[512:513, :]
        scatter_blocks(me, stage_d, 64, chunk * width // 64, width // 64, d_send, d_keep, slice(None))
        scatter_blocks(me, stage_u, 16, 0, 32, u_send, u_keep, span)
    output[...] = total[...].astype(BF)

    def behind(index, carry):
        gain_sum, shift_sum, branch_sum, cot_sum = carry
        span = pl.ds(pl.multiple_of(index * block, block), block)
        centred, scale = row_stats(middle[span, :])
        xh = centred * scale
        h = back[span, :]
        hg = h * smalls[1:2, :]
        cot_rows = cot[span, :].astype(F32)
        grad = cot_rows + scale * (
            hg
            - jnp.mean(hg, axis=-1, keepdims=True)
            - xh * jnp.mean(hg * xh, axis=-1, keepdims=True)
        )
        grad_middle[span, :] = grad
        low = grad.astype(BF)
        normed[span, :] = low
        grad_att[span, :] = dot(low, mix[...], NT).astype(BF)
        return (
            gain_sum + jnp.sum(h * xh, axis=0, keepdims=True),
            shift_sum + jnp.sum(h, axis=0, keepdims=True),
            branch_sum + jnp.sum(low.astype(F32), axis=0, keepdims=True),
            cot_sum + jnp.sum(cot_rows, axis=0, keepdims=True),
        )

    zero = jnp.zeros((1, 512), F32)
    sums = lax.fori_loop(0, count, behind, (zero, zero, zero, zero))
    for index in range(4):
        small_grads[index : index + 1, :] = sums[index]
    small_grads[4:8, :] = jnp.zeros((4, 512), F32)
    stage_d[0:256, :] = dot(ot_first[...], normed[...])
    stage_d[256:512, :] = dot(ot_second[...], normed[...])
    scatter_blocks(me, stage_d, 16, 0, 32, m_send, m_keep, slice(None))


def feed(me, tokens, o_pair, ot_pair, a_pair, b_pair, smalls, up_row, cot):
    rows = tokens.shape[0]
    return pl.pallas_call(
        feed_kernel,
        in_specs=[smem()] + [vmem()] * 12,
        out_specs=[vmem()] * 11,
        out_shape=[
            shape((rows, 512), BF),
            shape((rows, 512), F32),
            shape((rows, 512), BF),
            shape((16, 64, 512), BF),
            shape((16, 64, 512), F32),
            shape((16, 16, 2048), BF),
            shape((16, 16, 2048), F32),
            shape((16, 16, 512), BF),
            shape((16, 16, 512), F32),
            shape((8, 512), F32),
            shape((1, 2048), F32),
        ],
        scratch_shapes=[
            pltpu.VMEM((512, 512), BF),
            pltpu.VMEM((512, 2048), BF),
            pltpu.VMEM((2048, 512), BF),
            pltpu.VMEM((rows, 512), F32),
            pltpu.VMEM((rows, 512), BF),
            pltpu.VMEM((528, rows), BF),
            pltpu.VMEM((rows, 512), F32),
            pltpu.VMEM((rows, 512), F32),
            pltpu.VMEM((512, 512), F32),
            pltpu.VMEM((528, 512), F32),
            pltpu.VMEM((8, 128), F32),
        ],
        compiler_params=pltpu.CompilerParams(vmem_limit_bytes=56 * MIB),
        name="feed",
    )(me, tokens, *o_pair, *ot_pair, *a_pair, *b_pair, smalls, up_row, cot)


def pair_backward(q, k, v, do, ot_in, lse, key_aux, qa, da, dqt, acc_k, acc_v, gm, pair, block):
    cols = slice(128 * pair, 128 * pair + 128)
    k2 = k[:, cols]
    v2 = v[:, cols]
    rows = k2.shape[0]
    kt = k2.T
    lane = lax.broadcasted_iota(jnp.int32, k2.shape, 1)
    zero = jnp.zeros_like(k2)
    keys = []
    vals = []
    for h in range(2):
        own = (lane >= 64) == bool(h)
        keys.append(jnp.concatenate([jnp.where(own, k2, zero), key_aux], axis=1))
        vals.append(jnp.concatenate([jnp.where(own, v2, zero), key_aux], axis=1))
    qt = q[:, cols].T
    dt = do[:, cols].T
    product = dt.astype(F32) * ot_in[cols, :].astype(F32)
    row = lax.broadcasted_iota(jnp.int32, (16, rows), 0)
    for h in range(2):
        qa[h, 0:128, :] = qt
        da[h, 0:128, :] = dt
        delta = jnp.sum(product[64 * h : 64 * h + 64], axis=0, keepdims=True)
        base = qa[h, 128:144, :].astype(F32)
        one, two, three = split_three(-lse[2 * pair + h : 2 * pair + h + 1, :])
        base = jnp.where(row == 14, one, jnp.where(row == 15, two, base))
        qa[h, 128:144, :] = base.astype(BF)
        qa[h, 144:160, :] = jnp.where(row == 0, three, 0.0).astype(BF)
        one, two, three = split_three(-delta)
        base = jnp.where(row == 14, one, jnp.where(row == 15, two, 0.0))
        da[h, 128:144, :] = base.astype(BF)
        da[h, 144:160, :] = jnp.where(row == 0, three, 0.0).astype(BF)
    small_lane = lax.broadcasted_iota(jnp.int32, (block, 128), 1)
    for index in range(rows // block):
        span = slice(block * index, block * index + block)
        do_rows = do[span, cols]
        q_rows = q[span, cols]
        blank = jnp.zeros_like(do_rows)
        sum_k = None
        sum_v = None
        for h in range(2):
            own = (small_lane >= 64) == bool(h)
            probs = jnp.exp2(dot(keys[h], qa[h, :, span]) * EXP_SCALE)
            grad = (probs * dot(vals[h], da[h, :, span])).astype(BF)
            probs = probs.astype(BF)
            dqt[64 * h : 64 * h + 64, span] = dot(kt[64 * h : 64 * h + 64, :], grad)
            part_k = dot(grad, jnp.where(own, q_rows, blank))
            part_v = dot(probs, jnp.where(own, do_rows, blank))
            sum_k = part_k if sum_k is None else sum_k + part_k
            sum_v = part_v if sum_v is None else sum_v + part_v
        if index == 0:
            acc_k[...] = sum_k
            acc_v[...] = sum_v
        else:
            acc_k[...] += sum_k
            acc_v[...] += sum_v
    base = 384 * pair
    gm[:, base : base + 128] = (dqt[...].T * SCALE).astype(BF)
    gm[:, base + 128 : base + 256] = (acc_k[...] * SCALE).astype(BF)
    gm[:, base + 256 : base + 384] = acc_v[...].astype(BF)


def backward_group(
    me, q, k, v, do, ot_in, lse, key_aux, query_aux, normed_t, q_send, q_keep, sums, scratch
):
    qa, da, dqt, acc_k, acc_v, gm, stage = scratch
    for h in range(2):
        qa[h, 128:256, :] = query_aux[...]
        da[h, 128:256, :] = jnp.zeros((128, da.shape[2]), BF)
    for pair in range(2):
        pair_backward(
            q, k, v, do, ot_in, lse, key_aux[...], qa, da, dqt, acc_k, acc_v, gm, pair, 256
        )
    stage[...] = dot(normed_t[...], gm[...])
    sums[...] = stage[512:520, :]
    scatter_blocks(me, stage, 16, 0, 32, q_send, q_keep, slice(0, 768))


def backward_first_kernel(
    me_ref, q, k, v, do, ot_in, lse, key_aux, query_aux, normed_t, weight,
    q_send, q_keep, sums, partial, *scratch,
):
    backward_group(
        me_ref[0], q, k, v, do, ot_in, lse, key_aux, query_aux, normed_t, q_send, q_keep, sums,
        scratch,
    )
    gm = scratch[5]
    partial[...] = dot(gm[...], weight[...], NT)


def backward_second_kernel(
    me_ref, q, k, v, do, ot_in, lse, key_aux, query_aux, normed_t, weight, partial, tokens,
    smalls, grad_middle, small_grads, up_bias_grad, sums_first,
    q_send, q_keep, input_grad, *scratch,
):
    me = me_ref[0]
    sums, columns = scratch[7], scratch[8]
    backward_group(
        me, q, k, v, do, ot_in, lse, key_aux, query_aux, normed_t, q_send, q_keep, sums,
        scratch[:7],
    )
    gm = scratch[5]
    block = 256

    def behind(index, carry):
        gain_sum, shift_sum = carry
        span = pl.ds(pl.multiple_of(index * block, block), block)
        centred, scale = row_stats(tokens[span, :].astype(F32))
        xh = centred * scale
        h = partial[span, :] + dot(gm[span, :], weight[...], NT)
        hg = h * smalls[0:1, :]
        input_grad[span, :] = grad_middle[span, :] + scale * (
            hg
            - jnp.mean(hg, axis=-1, keepdims=True)
            - xh * jnp.mean(hg * xh, axis=-1, keepdims=True)
        )
        return (
            gain_sum + jnp.sum(h * xh, axis=0, keepdims=True),
            shift_sum + jnp.sum(h, axis=0, keepdims=True),
        )

    zero = jnp.zeros((1, 512), F32)
    gain_sum, shift_sum = lax.fori_loop(0, tokens.shape[0] // block, behind, (zero, zero))
    columns[...] = jnp.zeros_like(columns)
    columns[0:1, :] = gain_sum
    columns[1:2, :] = small_grads[0:1, :]
    columns[2:3, :] = shift_sum
    columns[3:4, :] = small_grads[1:2, :]
    for pair in range(4):
        source = (sums_first, sums)[pair // 2]
        base = (pair % 2) * 384
        span = slice(128 * pair, 128 * pair + 128)
        columns[4:5, span] = source[0:1, base : base + 128]
        columns[5:6, span] = source[0:1, base + 256 : base + 384]
    columns[6:7, :] = small_grads[2:3, :]
    columns[7:8, :] = small_grads[3:4, :]
    stage = scratch[6]
    stage[0:512, 0:128] = columns[...].T
    lane = lax.broadcasted_iota(jnp.int32, (1, 128), 1)
    for a in range(16):
        piece = up_bias_grad[:, 128 * a : 128 * a + 128]
        rolled = pltpu.roll(jnp.broadcast_to(piece, (8, 128)), 64, 1)[0:1, :]
        for half, values in enumerate((rolled, piece)):
            row = 32 * a + 16 * half
            stage[row : row + 1, 0:128] = jnp.where(lane < 64, stage[row : row + 1, 0:128], values)
    core = me & 1
    for half in range(16):
        r = (me ^ (2 * half)) >> 1
        place = ((r & 3) << 2) | (r >> 2)
        kept = pl.multiple_of(32 * half + core * 16, 16)
        sent = pl.multiple_of(32 * half + (1 - core) * 16, 16)
        q_keep[place, :, 768:896] = stage[pl.ds(kept, 16), 0:128]
        q_send[place, :, 768:896] = stage[pl.ds(sent, 16), 0:128].astype(BF)


def backward_scratch(rows):
    return [
        pltpu.VMEM((2, 256, rows), BF),
        pltpu.VMEM((2, 256, rows), BF),
        pltpu.VMEM((128, rows), F32),
        pltpu.VMEM((rows, 128), F32),
        pltpu.VMEM((rows, 128), F32),
        pltpu.VMEM((rows, 768), BF),
        pltpu.VMEM((528, 768), F32),
    ]


def backward_first(me, *operands):
    rows = operands[0].shape[0]
    return pl.pallas_call(
        backward_first_kernel,
        in_specs=[smem(), vmem(), vmem(), vmem(), pl.BlockSpec((rows, 256), lambda i: (0, 0))]
        + [vmem()] * 6,
        grid=(1,),
        out_specs=[vmem()] * 4,
        out_shape=[
            shape((16, 16, 768), BF),
            shape((16, 16, 768), F32),
            shape((8, 768), F32),
            shape((rows, 512), F32),
        ],
        scratch_shapes=backward_scratch(rows),
        compiler_params=pltpu.CompilerParams(vmem_limit_bytes=48 * MIB),
        name="attend_back_first",
    )(me, *operands)


def backward_second(me, *operands):
    rows = operands[0].shape[0]
    return pl.pallas_call(
        backward_second_kernel,
        in_specs=[smem(), vmem(), vmem(), vmem(), pl.BlockSpec((rows, 256), lambda i: (0, 1))]
        + [vmem()] * 13,
        grid=(1,),
        out_specs=[vmem()] * 3,
        out_shape=[
            shape((16, 16, 896), BF),
            shape((16, 16, 896), F32),
            shape((rows, 512), F32),
        ],
        scratch_shapes=backward_scratch(rows)
        + [pltpu.VMEM((8, 768), F32), pltpu.VMEM((128, 512), F32)],
        compiler_params=pltpu.CompilerParams(vmem_limit_bytes=48 * MIB),
        name="attend_back_second",
    )(me, *operands)


def swap(value, mask, count):
    return lax.ppermute(value, AXES, [(d, d ^ mask) for d in range(count)])


def spread(part, count):
    column = jnp.stack([part] + [swap(part, i << 3, count) for i in range(1, 4)])
    plane = jnp.stack([column] + [swap(column, j << 1, count) for j in range(1, 4)])
    mine = plane.reshape((16,) + part.shape)
    return mine, swap(mine, 1, count)


def collect(send, keep, count):
    rows, width = send.shape[1:]
    total = (keep + swap(send, 1, count).astype(F32)).reshape(4, 4, rows, width)
    plane = total[0]
    for j in range(1, 4):
        plane = plane + swap(total[j].astype(BF), j << 1, count).astype(F32)
    own = plane[0]
    for i in range(1, 4):
        own = own + swap(plane[i].astype(BF), i << 3, count).astype(F32)
    return own


def pack_whole(qkv, mix, up, down, gain, shift, qv, proj, up_bias):
    pieces = []
    for pair in range(4):
        for part in range(3):
            base = 512 * part + 128 * pair
            pieces.append(qkv[:, base : base + 128])
    rows = jnp.concatenate([gain, shift, qv, proj], axis=0)
    tile = jnp.pad(rows.T, ((0, 0), (0, 120))).reshape(32, 16, 128)
    tile = tile.at[:, 0, 64:128].set(up_bias.reshape(32, 64))
    a0 = jnp.concatenate([jnp.concatenate(pieces[:6], 1).reshape(32, 16, 768), tile], axis=2)
    a1 = jnp.concatenate(pieces[6:], 1).reshape(32, 16, 768)
    b0 = jnp.concatenate([mix, up], axis=1).reshape(32, 16, 2560)
    b1 = down.reshape(32, 4, 16, 512).swapaxes(1, 2).reshape(32, 16, 2048)
    return a0, a1, b0, b1


def relative_halves(blocks):
    parts = blocks.reshape((4, 4, 2) + blocks.shape[1:])
    parts = parts.transpose((2, 1, 0) + tuple(range(3, parts.ndim)))
    return parts[0].reshape((16,) + blocks.shape[1:]), parts[1].reshape((16,) + blocks.shape[1:])


def whole_blocks(send, keep):
    parts = jnp.stack([keep, send.astype(F32)]).reshape((2, 4, 4) + keep.shape[1:])
    parts = parts.transpose((2, 1, 0) + tuple(range(3, parts.ndim)))
    return parts.reshape((32,) + keep.shape[1:])


def body(cubic, count, tokens, chain_ids, qkv, mix, up, down, gain, shift, qv, proj, up_bias, cot):
    params = (qkv, mix, up, down, gain, shift, qv, proj, up_bias)
    if cubic:
        index = lax.axis_index("dp") * (count // lax.axis_size("dp")) + lax.axis_index("fsdp")
        me = index.astype(jnp.int32).reshape(1)
        parts = pack(*params)
        a0, a1, b0, b1 = [spread(part, count) for part in parts]
    else:
        me = jnp.zeros((1,), jnp.int32)
        dims = (0, 0, 0, 0, 1, 1, 1, 1, 0)
        whole = [
            lax.all_gather(value, AXES, axis=dim, tiled=True)
            for value, dim in zip(params, dims, strict=True)
        ]
        a0, a1, b0, b1 = [relative_halves(part) for part in pack_whole(*whole)]
    q0, k0, v0, o0, ot0, lse0, w0, normed, normed_t, smalls, up_row, key_aux, query_aux = (
        forward_first(me, tokens, chain_ids, *a0)
    )
    q1, k1, v1, o1, ot1, lse1, w1 = forward_second(me, normed, *a1, smalls, key_aux, query_aux)
    (
        output, grad_middle, grad_att, d_send, d_keep, u_send, u_keep, m_send, m_keep,
        small_grads, up_bias_grad,
    ) = feed(me, tokens, (o0, o1), (ot0, ot1), b0, b1, smalls, up_row, cot)
    s0, r0, sums0, partial = backward_first(
        me, q0, k0, v0, grad_att, ot0, lse0, key_aux, query_aux, normed_t, w0
    )
    s1, r1, input_grad = backward_second(
        me, q1, k1, v1, grad_att, ot1, lse1, key_aux, query_aux, normed_t, w1, partial, tokens,
        smalls, grad_middle, small_grads, up_bias_grad, sums0,
    )
    pairs = ((d_send, d_keep), (u_send, u_keep), (m_send, m_keep), (s0, r0), (s1, r1))
    if cubic:
        down_grad, up_grad, mix_grad, first, second = [collect(s, r, count) for s, r in pairs]
        tile = second[:, 768:896]
        vectors = tile[:, 0:8].T
        bias_grad = tile[0, 64:128]
        joined = [first, second[:, :768]]
        qkv_grad = unpack_columns(joined)
    else:
        blocks = [whole_blocks(s, r) for s, r in pairs]
        tiles = blocks[4][:, :, 768:896]
        wholes = (
            blocks[0].reshape(2048, 512),
            blocks[1].reshape(512, 2048),
            blocks[2].reshape(512, 512),
            unpack_columns(
                [blocks[3].reshape(512, 768), blocks[4][:, :, :768].reshape(512, 768)]
            ),
            tiles[:, 0, 64:128].reshape(2048),
        )
        down_grad, up_grad, mix_grad, qkv_grad, bias_grad = [
            lax.psum_scatter(value, AXES, scatter_dimension=0, tiled=True) for value in wholes
        ]
        vectors = lax.psum_scatter(
            tiles[:, :, 0:8].reshape(512, 8).T, AXES, scatter_dimension=1, tiled=True
        )
    return (
        output, input_grad, qkv_grad, mix_grad, up_grad, down_grad,
        vectors[0:2], vectors[2:4], vectors[4:6], vectors[6:8], bias_grad,
    )


def unpack_columns(halves):
    pieces = []
    for part in range(3):
        for pair in range(4):
            base = (pair % 2) * 384 + 128 * part
            pieces.append(halves[pair // 2][:, base : base + 128])
    return jnp.concatenate(pieces, axis=1)


def solution(mesh):
    count = mesh.shape["dp"] * mesh.shape["fsdp"]
    cubic = count == 32

    def entry(*operands):
        return body(cubic, count, *operands)

    rows = P(AXES, None)
    columns = P(None, AXES)
    flat = P(AXES)
    return jax.shard_map(
        entry,
        mesh=mesh,
        in_specs=(rows,) * 6 + (columns,) * 4 + (flat, rows),
        out_specs=(rows,) * 6 + (columns,) * 4 + (flat,),
        check_vma=False,
    )
```

```python
import functools
import math

import jax
import jax.numpy as jnp
from jax import lax
from jax.experimental import pallas as pl
from jax.experimental.pallas import tpu as pltpu
from jax.sharding import PartitionSpec as P

AXES = ("dp", "fsdp")
HEADS = 8
EPS = 1e-05
SCALE = 0.125
EXP_SCALE = SCALE * math.log2(math.e)
HIDE = -(2.0**60)
MIB = 2**20

BF = jnp.bfloat16
F32 = jnp.float32
NN = (((1,), (0,)), ((), ()))
NT = (((1,), (1,)), ((), ()))
TN = (((0,), (0,)), ((), ()))


def dot(a, b, dims=NN):
    return lax.dot_general(a, b, dims, preferred_element_type=F32)


def vmem():
    return pl.BlockSpec(memory_space=pltpu.VMEM)


def smem():
    return pl.BlockSpec(memory_space=pltpu.SMEM)


def shape(dims, dtype):
    return jax.ShapeDtypeStruct(dims, dtype)


def cost(us):
    return pl.CostEstimate(flops=int(us * 1.1e9), bytes_accessed=0, transcendentals=0)


def slots():
    return [(c, j, i) for c in range(2) for j in range(4) for i in range(4)]


def block_row(me, c, j, i, rows):
    return pl.multiple_of((me ^ (c | (j << 1) | (i << 3))) * rows, rows)


def row_stats(rows_in):
    mean = jnp.mean(rows_in, axis=-1, keepdims=True)
    centred = rows_in - mean
    spread = jnp.mean(centred * centred, axis=-1, keepdims=True)
    return centred, lax.rsqrt(spread + EPS)


def split_three(row):
    first = row.astype(BF).astype(F32)
    rest = row - first
    second = rest.astype(BF).astype(F32)
    return first, second, rest - second


def pack_kernel(qkv, mix, up, down, gain, shift, qv, proj, up_bias, a0, b0, b1, rows128):
    for pair in range(4):
        for part in range(3):
            base = 384 * pair + 128 * part
            a0[:, base : base + 128] = qkv[:, 512 * part + 128 * pair : 512 * part + 128 * pair + 128]
    rows128[...] = jnp.zeros_like(rows128)
    for index, ref in enumerate((gain, shift, qv, proj)):
        rows128[2 * index : 2 * index + 2, :] = ref[...].astype(F32)
    eye = (
        lax.broadcasted_iota(jnp.int32, (16, 16), 0) == lax.broadcasted_iota(jnp.int32, (16, 16), 1)
    ).astype(F32)
    columns = dot(eye.astype(BF), rows128[...].astype(BF), NT)
    bias = jnp.concatenate([jnp.zeros((1, 64), F32), up_bias[...].astype(F32)], axis=1)
    row = lax.broadcasted_iota(jnp.int32, (16, 128), 0)
    lane = lax.broadcasted_iota(jnp.int32, (16, 128), 1)
    a0[:, 1536:1664] = jnp.where((row == 0) & (lane >= 64), bias, columns).astype(BF)
    b0[:, 0:512] = mix[...]
    b0[:, 512:2560] = up[...]
    for part in range(4):
        b1[:, 512 * part : 512 * part + 512] = down[16 * part : 16 * part + 16, :]


def pack(qkv, mix, up, down, gain, shift, qv, proj, up_bias):
    return pl.pallas_call(
        pack_kernel,
        in_specs=[vmem()] * 9,
        out_specs=[vmem()] * 3,
        out_shape=[
            shape((16, 1664), BF),
            shape((16, 2560), BF),
            shape((16, 2048), BF),
        ],
        scratch_shapes=[pltpu.VMEM((128, 16), F32)],
        cost_estimate=cost(1.5),
        name="pack",
    )(qkv, mix, up, down, gain, shift, qv, proj, up_bias.reshape(1, 64))


def aux_rows(chain):
    row = lax.broadcasted_iota(jnp.int32, (128, chain.shape[1]), 0)
    low_bits = jnp.where(row < 7, (chain >> jnp.minimum(row, 6)) & 1, 0)
    high_bits = jnp.where(
        (row >= 7) & (row < 14), 1 - ((chain >> jnp.minimum(jnp.maximum(row - 7, 0), 6)) & 1), 0
    )
    bits = low_bits + high_bits
    query_side = bits.astype(F32) * HIDE
    key_side = jnp.where(row < 14, 1 - bits, jnp.where(row < 17, 1, 0)).astype(F32)
    return query_side.astype(BF), key_side.T.astype(BF)


def pair_forward(normed, weight, bias_q, bias_v, key_aux, qa, ot, outs, pair, block):
    q_out, k_out, v_out, o_out, ot_out, lse_out = outs
    rows = normed.shape[0]
    cols = slice(128 * pair, 128 * pair + 128)
    q2 = (dot(normed, weight[:, 0:128]) + bias_q).astype(BF)
    k2 = dot(normed, weight[:, 128:256]).astype(BF)
    v2 = (dot(normed, weight[:, 256:384]) + bias_v).astype(BF)
    q_out[:, cols] = q2
    k_out[:, cols] = k2
    v_out[:, cols] = v2
    qa[0:128, :] = q2.T
    vt = v2.T
    ones = (lax.broadcasted_iota(jnp.int32, (16, rows), 0) == 0).astype(F32).astype(BF)
    lane = lax.broadcasted_iota(jnp.int32, k2.shape, 1)
    zero = jnp.zeros_like(k2)
    keys = [
        jnp.concatenate([jnp.where((lane >= 64) == bool(h), k2, zero), key_aux], axis=1)
        for h in range(2)
    ]
    vts = [jnp.concatenate([vt[64 * h : 64 * h + 64], ones], axis=0) for h in range(2)]
    count = rows // block

    def score(index):
        q_cols = qa[:, block * index : block * index + block]
        return [dot(keys[h], q_cols) for h in range(2)]

    ahead = score(0)
    for index in range(count):
        scores = ahead
        if index + 1 < count:
            ahead = score(index + 1)
        span = slice(block * index, block * index + block)
        for h in range(2):
            peak = jnp.max(scores[h], axis=0, keepdims=True)
            probs = jnp.exp2((scores[h] - peak) * EXP_SCALE).astype(BF)
            mixed = dot(vts[h], probs)
            total = mixed[64:65]
            ot[64 * h : 64 * h + 64, span] = mixed[:64] * (1.0 / total)
            lse_out[2 * pair + h : 2 * pair + h + 1, span] = peak + jnp.log(total) * (1.0 / SCALE)
    ot_out[128 * pair : 128 * pair + 128, :] = ot[...].astype(BF)
    o_out[:, cols] = ot[...].T.astype(BF)


def forward_kernel(
    me_ref, tokens, chain, mine, other,
    q_out, k_out, v_out, o_out, ot_out, lse_out, weight, normed_out, normed_t, smalls, up_row,
    key_aux_out, query_aux_out, qa, ot, columns,
):
    me = me_ref[0]
    for c, j, i in slots():
        source = (mine, other)[c]
        row = block_row(me, c, j, i, 16)
        weight[pl.ds(row, 16), :] = source[4 * j + i, :, 0:1536]
        columns[pl.ds(row, 16), :] = source[4 * j + i, :, 1536:1664].astype(F32)
    smalls[...] = columns[...].T[0:8, :]
    lane = lax.broadcasted_iota(jnp.int32, (1, 128), 1)
    for a in range(16):
        even = pltpu.roll(columns[32 * a : 32 * a + 8, :], 64, 1)[0:1, :]
        odd = columns[32 * a + 16 : 32 * a + 17, :]
        up_row[:, 128 * a : 128 * a + 128] = jnp.where(lane < 64, even, odd)
    query_side, key_side = aux_rows(chain[...])
    qa[128:256, :] = query_side
    query_aux_out[...] = query_side
    key_aux_out[...] = key_side

    def norm_block(index, carry):
        span = pl.ds(pl.multiple_of(index * 256, 256), 256)
        centred, scale = row_stats(tokens[span, :].astype(F32))
        normed_out[span, :] = (centred * scale * smalls[0:1, :] + smalls[2:3, :]).astype(BF)
        return carry

    lax.fori_loop(0, tokens.shape[0] // 256, norm_block, 0)
    normed = normed_out[...]
    normed_t[0:512, :] = normed.T
    ones_row = lax.broadcasted_iota(jnp.int32, (16, normed.shape[0]), 0) == 0
    normed_t[512:528, :] = ones_row.astype(F32).astype(BF)
    outs = (q_out, k_out, v_out, o_out, ot_out, lse_out)
    for pair in range(4):
        cols = slice(128 * pair, 128 * pair + 128)
        pair_forward(
            normed, weight[:, 384 * pair : 384 * pair + 384], smalls[4:5, cols], smalls[5:6, cols],
            key_side, qa, ot, outs, pair, 512,
        )


def forward(me, tokens, chain, mine, other):
    rows = tokens.shape[0]
    return pl.pallas_call(
        forward_kernel,
        in_specs=[smem()] + [vmem()] * 4,
        out_specs=[vmem()] * 13,
        out_shape=[shape((rows, 512), BF)] * 4
        + [
            shape((512, rows), BF),
            shape((8, rows), F32),
            shape((512, 1536), BF),
            shape((rows, 512), BF),
            shape((528, rows), BF),
            shape((8, 512), F32),
            shape((1, 2048), F32),
            shape((rows, 128), BF),
            shape((128, rows), BF),
        ],
        scratch_shapes=[
            pltpu.VMEM((256, rows), BF),
            pltpu.VMEM((128, rows), F32),
            pltpu.VMEM((512, 128), F32),
        ],
        compiler_params=pltpu.CompilerParams(vmem_limit_bytes=40 * MIB),
        cost_estimate=cost(15),
        name="attend",
    )(me, tokens, chain, mine, other)


def gelu_parts(u):
    half_cdf = 0.5 + 0.5 * lax.erf(u * math.sqrt(0.5))
    density = jnp.exp2(u * u * (-0.5 * math.log2(math.e))) * (1.0 / math.sqrt(2.0 * math.pi))
    return u * half_cdf, half_cdf + u * density


def scatter_blocks(me, source, rows, base_block, blocks, send, keep, span):
    core = me & 1
    for half in range(blocks // 2):
        first = base_block + 2 * half
        row = 2 * half * rows
        r = (me ^ first) >> 1
        place = ((r & 3) << 2) | (r >> 2)
        kept = source[pl.ds(pl.multiple_of(row + core * rows, rows), rows), :]
        sent = source[pl.ds(pl.multiple_of(row + (1 - core) * rows, rows), rows), :]
        keep[place, :, span] = kept
        send[place, :, span] = sent.astype(BF)


def feed_first_kernel(
    me_ref, tokens, o_in, mine_a, other_a, mine_b, other_b, smalls, up_row, cot,
    output, middle, normed_t, grad_pre_out, d_send, d_keep, mix, up, down, normed, total, stage,
):
    me = me_ref[0]
    for c, j, i in slots():
        first, second = ((mine_a, mine_b), (other_a, other_b))[c]
        row = block_row(me, c, j, i, 16)
        mix[pl.ds(row, 16), :] = first[4 * j + i, :, 0:512]
        up[pl.ds(row, 16), :] = first[4 * j + i, :, 512:2560]
        for part in range(4):
            row4 = pl.multiple_of(block_row(me, c, j, i, 64) + 16 * part, 16)
            down[pl.ds(row4, 16), :] = second[4 * i + j, :, 512 * part : 512 * part + 512]
    rows = tokens.shape[0]
    block = 256

    def ahead(index, carry):
        span = pl.ds(pl.multiple_of(index * block, block), block)
        mid = tokens[span, :].astype(F32) + dot(o_in[span, :], mix[...]) + smalls[6:7, :]
        middle[span, :] = mid
        centred, scale = row_stats(mid)
        normed[span, :] = (centred * scale * smalls[1:2, :] + smalls[3:4, :]).astype(BF)
        total[span, :] = mid + smalls[7:8, :]
        return carry

    lax.fori_loop(0, rows // block, ahead, 0)
    normed_t[0:512, :] = normed[...].T
    ones_row = lax.broadcasted_iota(jnp.int32, (16, rows), 0) == 0
    normed_t[512:528, :] = ones_row.astype(F32).astype(BF)
    width = 512
    for chunk in range(2048 // width):
        span = slice(chunk * width, chunk * width + width)
        down_part = down[span, :]
        act, slope = gelu_parts(dot(normed[...], up[:, span]) + up_row[:, span])
        act_low = act.astype(BF)
        grad_pre_out[:, span] = (dot(cot[...], down_part, NT) * slope).astype(BF)
        total[...] += dot(act_low, down_part)
        stage[...] = dot(act_low, cot[...], TN)
        scatter_blocks(me, stage, 64, chunk * width // 64, width // 64, d_send, d_keep, slice(None))
    output[...] = total[...].astype(BF)


def feed_first(me, tokens, o_in, a_pair, b_pair, smalls, up_row, cot):
    rows = tokens.shape[0]
    return pl.pallas_call(
        feed_first_kernel,
        in_specs=[smem()] + [vmem()] * 9,
        out_specs=[vmem()] * 8,
        out_shape=[
            shape((rows, 512), BF),
            shape((rows, 512), F32),
            shape((528, rows), BF),
            shape((rows, 2048), BF),
            shape((16, 64, 512), BF),
            shape((16, 64, 512), F32),
            shape((512, 512), BF),
            shape((512, 2048), BF),
        ],
        scratch_shapes=[
            pltpu.VMEM((2048, 512), BF),
            pltpu.VMEM((rows, 512), BF),
            pltpu.VMEM((rows, 512), F32),
            pltpu.VMEM((512, 512), F32),
        ],
        compiler_params=pltpu.CompilerParams(vmem_limit_bytes=48 * MIB),
        cost_estimate=cost(18),
        name="feed_first",
    )(me, tokens, o_in, *a_pair, *b_pair, smalls, up_row, cot)


def feed_second_kernel(
    me_ref, middle, normed_t, grad_pre, mix, up, smalls, cot, ot_in,
    grad_middle, grad_att, m_send, m_keep, small_grads, up_bias_grad, low_rows, stage,
):
    me = me_ref[0]
    rows = middle.shape[0]
    block = 256
    width = 512
    for chunk in range(2048 // width):
        span = slice(chunk * width, chunk * width + width)
        stage[...] = dot(normed_t[...], grad_pre[:, span])
        up_bias_grad[:, span] = stage[512:513, :]
        scatter_blocks(me, stage, 16, 0, 32, m_send, m_keep, span)

    def behind(index, carry):
        gain_sum, shift_sum, branch_sum, cot_sum = carry
        span = pl.ds(pl.multiple_of(index * block, block), block)
        centred, scale = row_stats(middle[span, :])
        xh = centred * scale
        h = dot(grad_pre[span, :], up[...], NT)
        hg = h * smalls[1:2, :]
        cot_rows = cot[span, :].astype(F32)
        grad = cot_rows + scale * (
            hg
            - jnp.mean(hg, axis=-1, keepdims=True)
            - xh * jnp.mean(hg * xh, axis=-1, keepdims=True)
        )
        grad_middle[span, :] = grad
        low = grad.astype(BF)
        low_rows[span, :] = low
        grad_att[span, :] = dot(low, mix[...], NT).astype(BF)
        return (
            gain_sum + jnp.sum(h * xh, axis=0, keepdims=True),
            shift_sum + jnp.sum(h, axis=0, keepdims=True),
            branch_sum + jnp.sum(low.astype(F32), axis=0, keepdims=True),
            cot_sum + jnp.sum(cot_rows, axis=0, keepdims=True),
        )

    zero = jnp.zeros((1, 512), F32)
    sums = lax.fori_loop(0, rows // block, behind, (zero, zero, zero, zero))
    for index in range(4):
        small_grads[index : index + 1, :] = sums[index]
    small_grads[4:8, :] = jnp.zeros((4, 512), F32)
    stage[0:512, :] = dot(ot_in[...], low_rows[...])
    scatter_blocks(me, stage, 16, 0, 32, m_send, m_keep, slice(2048, 2560))


def feed_second(me, middle, normed_t, grad_pre, mix, up, smalls, cot, ot_in):
    rows = middle.shape[0]
    return pl.pallas_call(
        feed_second_kernel,
        in_specs=[smem()] + [vmem()] * 8,
        out_specs=[vmem()] * 6,
        out_shape=[
            shape((rows, 512), F32),
            shape((rows, 512), BF),
            shape((16, 16, 2560), BF),
            shape((16, 16, 2560), F32),
            shape((8, 512), F32),
            shape((1, 2048), F32),
        ],
        scratch_shapes=[pltpu.VMEM((rows, 512), BF), pltpu.VMEM((528, 512), F32)],
        compiler_params=pltpu.CompilerParams(vmem_limit_bytes=48 * MIB),
        cost_estimate=cost(11),
        name="feed_second",
    )(me, middle, normed_t, grad_pre, mix, up, smalls, cot, ot_in)


def pair_backward(q, k, v, do, ot_in, lse, key_aux, qa, da, dqt, acc_k, acc_v, gm, pair, block):
    k2 = k[...]
    v2 = v[...]
    rows = k2.shape[0]
    kt = k2.T
    lane = lax.broadcasted_iota(jnp.int32, k2.shape, 1)
    zero = jnp.zeros_like(k2)
    keys = []
    vals = []
    for h in range(2):
        own = (lane >= 64) == bool(h)
        keys.append(jnp.concatenate([jnp.where(own, k2, zero), key_aux], axis=1))
        vals.append(jnp.concatenate([jnp.where(own, v2, zero), key_aux], axis=1))
    qt = q[...].T
    dt = do[...].T
    product = dt.astype(F32) * ot_in[...].astype(F32)
    row = lax.broadcasted_iota(jnp.int32, (16, rows), 0)
    for h in range(2):
        qa[h, 0:128, :] = qt
        da[h, 0:128, :] = dt
        delta = jnp.sum(product[64 * h : 64 * h + 64], axis=0, keepdims=True)
        base = qa[h, 128:144, :].astype(F32)
        one, two, three = split_three(-lse[2 * pair + h : 2 * pair + h + 1, :])
        base = jnp.where(row == 14, one, jnp.where(row == 15, two, base))
        qa[h, 128:144, :] = base.astype(BF)
        qa[h, 144:160, :] = jnp.where(row == 0, three, 0.0).astype(BF)
        one, two, three = split_three(-delta)
        base = jnp.where(row == 14, one, jnp.where(row == 15, two, 0.0))
        da[h, 128:144, :] = base.astype(BF)
        da[h, 144:160, :] = jnp.where(row == 0, three, 0.0).astype(BF)
    small_lane = lax.broadcasted_iota(jnp.int32, (block, 128), 1)
    for index in range(rows // block):
        span = slice(block * index, block * index + block)
        do_rows = do[span, :]
        q_rows = q[span, :]
        blank = jnp.zeros_like(do_rows)
        sum_k = None
        sum_v = None
        for h in range(2):
            own = (small_lane >= 64) == bool(h)
            probs = jnp.exp2(dot(keys[h], qa[h, :, span]) * EXP_SCALE)
            grad = (probs * dot(vals[h], da[h, :, span])).astype(BF)
            probs = probs.astype(BF)
            dqt[64 * h : 64 * h + 64, span] = dot(kt[64 * h : 64 * h + 64, :], grad)
            part_k = dot(grad, jnp.where(own, q_rows, blank))
            part_v = dot(probs, jnp.where(own, do_rows, blank))
            sum_k = part_k if sum_k is None else sum_k + part_k
            sum_v = part_v if sum_v is None else sum_v + part_v
        if index == 0:
            acc_k[...] = sum_k
            acc_v[...] = sum_v
        else:
            acc_k[...] += sum_k
            acc_v[...] += sum_v
    gm[:, 0:128] = (dqt[...].T * SCALE).astype(BF)
    gm[:, 128:256] = (acc_k[...] * SCALE).astype(BF)
    gm[:, 256:384] = acc_v[...].astype(BF)


def backward_pair(q, k, v, do, ot_in, lse, key_aux, query_aux, gm, scratch, pair):
    qa, da, dqt, acc_k, acc_v = scratch
    for h in range(2):
        qa[h, 128:256, :] = query_aux[...]
        da[h, 128:256, :] = jnp.zeros((128, da.shape[2]), BF)
    pair_backward(q, k, v, do, ot_in, lse, key_aux[...], qa, da, dqt, acc_k, acc_v, gm, pair, 256)


def weight_terms(me, gm_first, gm, normed_t, weight, smalls, stage, send, keep, sums, vectors):
    stage[:, 0:384] = dot(normed_t[...], gm_first[...])
    stage[:, 384:768] = dot(normed_t[...], gm[...])
    total = stage[512:513, :]
    sums[0:1, :] = total
    scatter_blocks(me, stage, 16, 0, 32, send, keep, slice(0, 768))
    wide = weight[...].astype(F32)
    vectors[:, 0:1] = jnp.sum(stage[0:512, :] * wide, axis=1, keepdims=True)
    vectors[:, 1:2] = jnp.sum(wide * total, axis=1, keepdims=True)


def backward_even_kernel(pair, q, k, v, do, ot_in, lse, key_aux, query_aux, gm, *scratch):
    backward_pair(q, k, v, do, ot_in, lse, key_aux, query_aux, gm, scratch, pair)


def backward_odd_kernel(
    me_ref, q, k, v, do, ot_in, lse, key_aux, query_aux, gm_first, normed_t, weight, smalls,
    gm, send, keep, sums, vectors, *scratch,
):
    backward_pair(q, k, v, do, ot_in, lse, key_aux, query_aux, gm, scratch[:5], 1)
    weight_terms(
        me_ref[0], gm_first, gm, normed_t, weight, smalls, scratch[5], send, keep, sums, vectors
    )


def backward_last_kernel(
    me_ref, q, k, v, do, ot_in, lse, key_aux, query_aux, gm_first, normed_t, weight, smalls,
    small_grads, up_bias_grad, sums_first, vectors_first,
    gm, send, keep, *scratch,
):
    me = me_ref[0]
    stage, sums, vectors, columns = scratch[5:]
    backward_pair(q, k, v, do, ot_in, lse, key_aux, query_aux, gm, scratch[:5], 3)
    weight_terms(me, gm_first, gm, normed_t, weight, smalls, stage, send, keep, sums, vectors)
    columns[...] = jnp.zeros_like(columns)
    columns[1:2, :] = small_grads[0:1, :]
    columns[3:4, :] = small_grads[1:2, :]
    for pair in range(4):
        source = (sums_first, sums)[pair // 2]
        base = (pair % 2) * 384
        span = slice(128 * pair, 128 * pair + 128)
        columns[4:5, span] = source[0:1, base : base + 128]
        columns[5:6, span] = source[0:1, base + 256 : base + 384]
    columns[6:7, :] = small_grads[2:3, :]
    columns[7:8, :] = small_grads[3:4, :]
    columns[8:9, :] = smalls[0:1, :]
    columns[9:10, :] = smalls[2:3, :]
    tile = columns[...].T
    product = vectors[:, 0:1] + vectors_first[:, 0:1]
    plain = vectors[:, 1:2] + vectors_first[:, 1:2]
    gain_sum = (product - tile[:, 9:10] * plain) / tile[:, 8:9]
    lanes = lax.broadcasted_iota(jnp.int32, (512, 128), 1)
    stage[0:512, 0:128] = jnp.where(lanes == 0, gain_sum, jnp.where(lanes == 2, plain, tile))
    lane = lax.broadcasted_iota(jnp.int32, (1, 128), 1)
    for a in range(16):
        piece = up_bias_grad[:, 128 * a : 128 * a + 128]
        rolled = pltpu.roll(jnp.broadcast_to(piece, (8, 128)), 64, 1)[0:1, :]
        for half, values in enumerate((rolled, piece)):
            row = 32 * a + 16 * half
            stage[row : row + 1, 0:128] = jnp.where(lane < 64, stage[row : row + 1, 0:128], values)
    core = me & 1
    for half in range(16):
        r = (me ^ (2 * half)) >> 1
        place = ((r & 3) << 2) | (r >> 2)
        kept = pl.multiple_of(32 * half + core * 16, 16)
        sent = pl.multiple_of(32 * half + (1 - core) * 16, 16)
        keep[place, :, 768:896] = stage[pl.ds(kept, 16), 0:128]
        send[place, :, 768:896] = stage[pl.ds(sent, 16), 0:128].astype(BF)


def backward_scratch(rows):
    return [
        pltpu.VMEM((2, 256, rows), BF),
        pltpu.VMEM((2, 256, rows), BF),
        pltpu.VMEM((128, rows), F32),
        pltpu.VMEM((rows, 128), F32),
        pltpu.VMEM((rows, 128), F32),
    ]


def pair_specs(rows, pair):
    column = pl.BlockSpec((rows, 128), lambda i: (0, pair))
    return [column] * 4 + [
        pl.BlockSpec((128, rows), lambda i: (pair, 0)),
        vmem(), vmem(), vmem(),
    ]


def backward_even(pair, *operands):
    rows = operands[0].shape[0]
    return pl.pallas_call(
        functools.partial(backward_even_kernel, pair),
        grid=(1,),
        in_specs=pair_specs(rows, pair),
        out_specs=vmem(),
        out_shape=shape((rows, 384), BF),
        scratch_shapes=backward_scratch(rows),
        compiler_params=pltpu.CompilerParams(vmem_limit_bytes=32 * MIB),
        cost_estimate=cost(8),
        name=f"attend_back_{pair}",
    )(*operands)


def backward_odd(me, *operands):
    rows = operands[0].shape[0]
    return pl.pallas_call(
        backward_odd_kernel,
        grid=(1,),
        in_specs=[smem()]
        + pair_specs(rows, 1)
        + [vmem(), vmem(), pl.BlockSpec((512, 768), lambda i: (0, 0)), vmem()],
        out_specs=[vmem()] * 5,
        out_shape=[
            shape((rows, 384), BF),
            shape((16, 16, 768), BF),
            shape((16, 16, 768), F32),
            shape((8, 768), F32),
            shape((512, 128), F32),
        ],
        scratch_shapes=backward_scratch(rows) + [pltpu.VMEM((528, 768), F32)],
        compiler_params=pltpu.CompilerParams(vmem_limit_bytes=40 * MIB),
        cost_estimate=cost(9),
        name="attend_back_1",
    )(me, *operands)


def backward_last(me, *operands):
    rows = operands[0].shape[0]
    return pl.pallas_call(
        backward_last_kernel,
        grid=(1,),
        in_specs=[smem()]
        + pair_specs(rows, 3)
        + [vmem(), vmem(), pl.BlockSpec((512, 768), lambda i: (0, 1))]
        + [vmem()] * 5,
        out_specs=[vmem()] * 3,
        out_shape=[
            shape((rows, 384), BF),
            shape((16, 16, 896), BF),
            shape((16, 16, 896), F32),
        ],
        scratch_shapes=backward_scratch(rows)
        + [
            pltpu.VMEM((528, 768), F32),
            pltpu.VMEM((8, 768), F32),
            pltpu.VMEM((512, 128), F32),
            pltpu.VMEM((128, 512), F32),
        ],
        compiler_params=pltpu.CompilerParams(vmem_limit_bytes=40 * MIB),
        cost_estimate=cost(9),
        name="attend_back_3",
    )(me, *operands)


def input_kernel(tokens, gm0, gm1, gm2, gm3, weight, smalls, grad_middle, input_grad):
    block = 256

    def behind(index, carry):
        span = pl.ds(pl.multiple_of(index * block, block), block)
        centred, scale = row_stats(tokens[span, :].astype(F32))
        xh = centred * scale
        gm = jnp.concatenate([ref[span, :] for ref in (gm0, gm1, gm2, gm3)], axis=1)
        hg = dot(gm, weight[...], NT) * smalls[0:1, :]
        input_grad[span, :] = grad_middle[span, :] + scale * (
            hg
            - jnp.mean(hg, axis=-1, keepdims=True)
            - xh * jnp.mean(hg * xh, axis=-1, keepdims=True)
        )
        return carry

    lax.fori_loop(0, tokens.shape[0] // block, behind, 0)


def input_terms(*operands):
    rows = operands[0].shape[0]
    return pl.pallas_call(
        input_kernel,
        in_specs=[vmem()] * 8,
        out_specs=vmem(),
        out_shape=shape((rows, 512), F32),
        compiler_params=pltpu.CompilerParams(vmem_limit_bytes=32 * MIB),
        cost_estimate=cost(5),
        name="input_terms",
    )(*operands)


def swap(value, mask, count):
    return lax.ppermute(value, AXES, [(d, d ^ mask) for d in range(count)])


Z_MASKS = (8, 16, 24)
PLANE_MASKS = (2, 4, 6)


def swaps(value, masks, count):
    return [swap(value, mask, count) for mask in masks]


def after(value, *tokens):
    return lax.optimization_barrier((value, tokens))[0]


def group(own, others):
    joined = jnp.stack([own] + others)
    return joined.reshape((-1,) + joined.shape[-2:])


def merge(own, received):
    for part in received:
        own = own + part.astype(F32)
    return own


def slices(total, rows, width):
    quarters = total.reshape((4, -1, rows, width))
    return quarters[0], [quarters[j].astype(BF) for j in range(1, 4)]


def pack_whole(qkv, mix, up, down, gain, shift, qv, proj, up_bias):
    pieces = []
    for pair in range(4):
        for part in range(3):
            base = 512 * part + 128 * pair
            pieces.append(qkv[:, base : base + 128])
    rows = jnp.concatenate([gain, shift, qv, proj], axis=0)
    tile = jnp.pad(rows.T, ((0, 0), (0, 120))).reshape(32, 16, 128)
    tile = tile.at[:, 0, 64:128].set(up_bias.reshape(32, 64))
    a0 = jnp.concatenate([jnp.concatenate(pieces, 1).reshape(32, 16, 1536), tile], axis=2)
    b0 = jnp.concatenate([mix, up], axis=1).reshape(32, 16, 2560)
    b1 = down.reshape(32, 4, 16, 512).swapaxes(1, 2).reshape(32, 16, 2048)
    return a0, b0, b1


def relative_halves(blocks):
    parts = blocks.reshape((4, 4, 2) + blocks.shape[1:])
    parts = parts.transpose((2, 1, 0) + tuple(range(3, parts.ndim)))
    return parts[0].reshape((16,) + blocks.shape[1:]), parts[1].reshape((16,) + blocks.shape[1:])


def whole_blocks(send, keep):
    parts = jnp.stack([keep, send.astype(F32)]).reshape((2, 4, 4) + keep.shape[1:])
    parts = parts.transpose((2, 1, 0) + tuple(range(3, parts.ndim)))
    return parts.reshape((32,) + keep.shape[1:])


def body(cubic, count, tokens, chain_ids, qkv, mix, up, down, gain, shift, qv, proj, up_bias, cot):
    params = (qkv, mix, up, down, gain, shift, qv, proj, up_bias)
    if cubic:
        index = lax.axis_index("dp") * (count // lax.axis_size("dp")) + lax.axis_index("fsdp")
        me = index.astype(jnp.int32).reshape(1)
        a_own, b_own, c_own = pack(*params)
        a_recv = swaps(a_own, Z_MASKS, count)
        c_recv = swaps(c_own, PLANE_MASKS, count)
        a_col = group(a_own, a_recv)
        a_recv = swaps(a_col, PLANE_MASKS, count)
        b_recv = swaps(after(b_own, a_col), Z_MASKS, count)
        c_plane = group(c_own, [after(part, a_col) for part in c_recv])
        c_recv = swaps(c_plane, Z_MASKS, count)
        a_mine = group(a_col, a_recv)
        a_other = swap(a_mine, 1, count)
        b_col = group(b_own, [after(part, a_mine) for part in b_recv])
        b_recv = swaps(b_col, PLANE_MASKS, count)
        a_mine, a_other = after((a_mine, a_other), b_col)
    else:
        me = jnp.zeros((1,), jnp.int32)
        dims = (0, 0, 0, 0, 1, 1, 1, 1, 0)
        whole = [
            lax.all_gather(value, AXES, axis=dim, tiled=True)
            for value, dim in zip(params, dims, strict=True)
        ]
        a_parts, b_parts, c_parts = pack_whole(*whole)
        a_mine, a_other = relative_halves(a_parts)
        b_pair = relative_halves(b_parts)
        c_pair = [
            half.reshape(4, 4, 16, 2048).swapaxes(0, 1).reshape(16, 16, 2048)
            for half in relative_halves(c_parts)
        ]
    q, k, v, o, ot, lse, weight, normed, normed_t, smalls, up_row, key_aux, query_aux = forward(
        me, tokens, chain_ids, a_mine, a_other
    )
    if cubic:
        b_mine = group(b_col, [after(part, smalls) for part in b_recv])
        c_mine = group(c_plane, [after(part, smalls) for part in c_recv])
        b_pair = (b_mine, swap(b_mine, 1, count))
        c_pair = (c_mine, swap(c_mine, 1, count))
    output, middle, normed_two_t, grad_pre, d_send, d_keep, mix_whole, up_whole = feed_first(
        me, tokens, o, b_pair, c_pair, smalls, up_row, cot
    )
    if cubic:
        d_recv = swap(d_send, 1, count)
    grad_middle, grad_att, m_send, m_keep, small_grads, up_bias_grad = feed_second(
        me, middle, normed_two_t, grad_pre, mix_whole, up_whole, smalls, cot, ot
    )
    if cubic:
        d_total = merge(d_keep, [after(d_recv, small_grads)])
        d_own, d_parts = slices(d_total, 64, 512)
        d_recv = [swap(part, mask, count) for part, mask in zip(d_parts, PLANE_MASKS, strict=True)]
        m_recv = swap(m_send, 1, count)
        lse = after(lse, d_parts)
    gm0 = backward_even(0, q, k, v, grad_att, ot, lse, key_aux, query_aux)
    if cubic:
        m_total = merge(m_keep, [after(m_recv, gm0)])
        m_own, m_parts = slices(m_total, 16, 2560)
        m_recv = [swap(part, mask, count) for part, mask in zip(m_parts, PLANE_MASKS, strict=True)]
        lse = after(lse, m_parts)
    gm1, f_send, f_keep, sums, vectors = backward_odd(
        me, q, k, v, grad_att, ot, lse, key_aux, query_aux, gm0, normed_t, weight, smalls
    )
    if cubic:
        f_recv = swap(f_send, 1, count)
        d_total = merge(d_own, [after(part, sums) for part in d_recv])
        d_own, d_parts = slices(d_total, 64, 512)
        d_recv = [swap(part, mask, count) for part, mask in zip(d_parts, Z_MASKS, strict=True)]
        lse = after(lse, d_parts)
    gm2 = backward_even(2, q, k, v, grad_att, ot, lse, key_aux, query_aux)
    if cubic:
        m_total = merge(m_own, [after(part, gm2) for part in m_recv])
        m_own, m_parts = slices(m_total, 16, 2560)
        m_recv = [swap(part, mask, count) for part, mask in zip(m_parts, Z_MASKS, strict=True)]
        f_total = merge(f_keep, [after(f_recv, gm2)])
        f_own, f_parts = slices(f_total, 16, 768)
        f_recv = [swap(part, mask, count) for part, mask in zip(f_parts, PLANE_MASKS, strict=True)]
        down_grad = merge(d_own, [after(part, gm2) for part in d_recv])
        lse = after(lse, m_parts, f_parts)
    gm3, g_send, g_keep = backward_last(
        me, q, k, v, grad_att, ot, lse, key_aux, query_aux, gm2, normed_t, weight, smalls,
        small_grads, up_bias_grad, sums, vectors,
    )
    if cubic:
        g_total = merge(g_keep, [swap(g_send, 1, count)])
        g_own, g_parts = slices(g_total, 16, 896)
        g_recv = [swap(part, mask, count) for part, mask in zip(g_parts, PLANE_MASKS, strict=True)]
        smalls = after(smalls, g_parts)
    input_grad = input_terms(tokens, gm0, gm1, gm2, gm3, weight, smalls, grad_middle)
    if cubic:
        token = input_grad
        m_grad = merge(m_own, [after(part, g_parts) for part in m_recv])[0]
        f_total = merge(f_own, [after(part, g_parts) for part in f_recv])
        g_total = merge(g_own, [after(part, token) for part in g_recv])
        total = jnp.concatenate([f_total, g_total], axis=-1)
        own, parts = slices(total, 16, 1664)
        recv = [swap(part, mask, count) for part, mask in zip(parts, Z_MASKS, strict=True)]
        final = merge(own, recv)[0]
        m_grad = m_grad.reshape(16, 2560)
        final = final.reshape(16, 1664)
        down_grad = down_grad.reshape(64, 512)
        tile = final[:, 1536:1664]
        return (
            output, input_grad, unpack_columns([final[:, :768], final[:, 768:1536]]),
            m_grad[:, 2048:], m_grad[:, :2048], down_grad,
            tile[:, 0:2].T, tile[:, 2:4].T, tile[:, 4:6].T, tile[:, 6:8].T, tile[0, 64:128],
        )
    pairs = ((d_send, d_keep), (m_send, m_keep), (f_send, f_keep), (g_send, g_keep))
    blocks = [whole_blocks(s, r) for s, r in pairs]
    tiles = blocks[3][:, :, 768:896]
    joined = blocks[1].reshape(512, 2560)
    wholes = (
        blocks[0].reshape(2048, 512),
        joined[:, :2048],
        joined[:, 2048:],
        unpack_columns([blocks[2].reshape(512, 768), blocks[3][:, :, :768].reshape(512, 768)]),
        tiles[:, 0, 64:128].reshape(2048),
    )
    down_grad, up_grad, mix_grad, qkv_grad, bias_grad = [
        lax.psum_scatter(value, AXES, scatter_dimension=0, tiled=True) for value in wholes
    ]
    vectors = lax.psum_scatter(
        tiles[:, :, 0:8].reshape(512, 8).T, AXES, scatter_dimension=1, tiled=True
    )
    return (
        output, input_grad, qkv_grad, mix_grad, up_grad, down_grad,
        vectors[0:2], vectors[2:4], vectors[4:6], vectors[6:8], bias_grad,
    )


def unpack_columns(halves):
    pieces = []
    for part in range(3):
        for pair in range(4):
            base = (pair % 2) * 384 + 128 * part
            pieces.append(halves[pair // 2][:, base : base + 128])
    return jnp.concatenate(pieces, axis=1)


def solution(mesh):
    count = mesh.shape["dp"] * mesh.shape["fsdp"]
    cubic = count == 32

    def entry(*operands):
        return body(cubic, count, *operands)

    rows = P(AXES, None)
    columns = P(None, AXES)
    flat = P(AXES)
    return jax.shard_map(
        entry,
        mesh=mesh,
        in_specs=(rows,) * 6 + (columns,) * 4 + (flat, rows),
        out_specs=(rows,) * 6 + (columns,) * 4 + (flat,),
        check_vma=False,
    )
```

```python
import functools
import math

import jax
import jax.numpy as jnp
from jax import lax
from jax.experimental import pallas as pl
from jax.experimental.pallas import tpu as pltpu
from jax.sharding import PartitionSpec as P

AXES = ("dp", "plane", "core")
HEADS = 8
EPS = 1e-05
SCALE = 0.125
EXP_SCALE = SCALE * math.log2(math.e)
HIDE = -(2.0**60)
MIB = 2**20

BF = jnp.bfloat16
F32 = jnp.float32
NN = (((1,), (0,)), ((), ()))
NT = (((1,), (1,)), ((), ()))
TN = (((0,), (0,)), ((), ()))


def dot(a, b, dims=NN):
    return lax.dot_general(a, b, dims, preferred_element_type=F32)


def vmem():
    return pl.BlockSpec(memory_space=pltpu.VMEM)


def smem():
    return pl.BlockSpec(memory_space=pltpu.SMEM)


def shape(dims, dtype):
    return jax.ShapeDtypeStruct(dims, dtype)


def block_of(index, block):
    return pl.ds(pl.multiple_of(index * block, block), block)


def cost(us):
    return pl.CostEstimate(flops=int(us * 1.1e9), bytes_accessed=0, transcendentals=0)


TALL_ORDER = (0, 2, 1, 3)


def slots():
    return [(c, j, i) for c in range(2) for j in range(4) for i in range(4)]


def block_row(me, c, j, i, rows):
    return pl.multiple_of((me ^ (c | (j << 1) | (i << 3))) * rows, rows)


def row_stats(rows_in):
    mean = jnp.mean(rows_in, axis=-1, keepdims=True)
    centred = rows_in - mean
    spread = jnp.mean(centred * centred, axis=-1, keepdims=True)
    return centred, lax.rsqrt(spread + EPS)


def split_three(row):
    first = row.astype(BF).astype(F32)
    rest = row - first
    second = rest.astype(BF).astype(F32)
    return first, second, rest - second


def pack_kernel(qkv, mix, up, down, gain, shift, qv, proj, up_bias, a0, b0, rows128):
    for pair in range(4):
        for part in range(3):
            base = 384 * pair + 128 * part
            a0[:, base : base + 128] = qkv[:, 512 * part + 128 * pair : 512 * part + 128 * pair + 128]
    rows128[...] = jnp.zeros_like(rows128)
    for index, ref in enumerate((gain, shift, qv, proj)):
        rows128[2 * index : 2 * index + 2, :] = ref[...].astype(F32)
    eye = (
        lax.broadcasted_iota(jnp.int32, (16, 16), 0) == lax.broadcasted_iota(jnp.int32, (16, 16), 1)
    ).astype(F32)
    columns = dot(eye.astype(BF), rows128[...].astype(BF), NT)
    bias = jnp.concatenate([jnp.zeros((1, 64), F32), up_bias[...].astype(F32)], axis=1)
    row = lax.broadcasted_iota(jnp.int32, (16, 128), 0)
    lane = lax.broadcasted_iota(jnp.int32, (16, 128), 1)
    a0[:, 1536:1664] = jnp.where((row == 0) & (lane >= 64), bias, columns).astype(BF)
    a0[:, 1664:2176] = mix[...]
    a0[:, 2176:4224] = up[...]
    for part in range(4):
        b0[:, 512 * part : 512 * part + 512] = down[16 * part : 16 * part + 16, :]


def pack(qkv, mix, up, down, gain, shift, qv, proj, up_bias):
    return pl.pallas_call(
        pack_kernel,
        in_specs=[vmem()] * 9,
        out_specs=[vmem()] * 2,
        out_shape=[shape((16, 4224), BF), shape((16, 2048), BF)],
        scratch_shapes=[pltpu.VMEM((128, 16), F32)],
        cost_estimate=cost(1.5),
        name="pack",
    )(qkv, mix, up, down, gain, shift, qv, proj, up_bias.reshape(1, 64))


def aux_rows(chain):
    row = lax.broadcasted_iota(jnp.int32, (128, chain.shape[1]), 0)
    low_bits = jnp.where(row < 7, (chain >> jnp.minimum(row, 6)) & 1, 0)
    high_bits = jnp.where(
        (row >= 7) & (row < 14), 1 - ((chain >> jnp.minimum(jnp.maximum(row - 7, 0), 6)) & 1), 0
    )
    bits = low_bits + high_bits
    query_side = bits.astype(F32) * HIDE
    key_side = jnp.where(row < 14, 1 - bits, jnp.where(row < 17, 1, 0)).astype(F32)
    return query_side.astype(BF), key_side.T.astype(BF)


def pair_forward(normed, weight, bias_q, bias_v, key_aux, qa, ot, outs, pair, block):
    qkv_out, o_out, ot_out, lse_out = outs
    rows = normed.shape[0]
    cols = block_of(pair, 128)
    q2 = (dot(normed, weight[:, 0:128]) + bias_q).astype(BF)
    k2 = dot(normed, weight[:, 128:256]).astype(BF)
    v2 = (dot(normed, weight[:, 256:384]) + bias_v).astype(BF)
    for index, value in enumerate((q2, k2, v2)):
        qkv_out[pair, index] = value
    qa[0:128, :] = q2.T
    vt = v2.T
    ones = (lax.broadcasted_iota(jnp.int32, (16, rows), 0) == 0).astype(F32).astype(BF)
    lane = lax.broadcasted_iota(jnp.int32, k2.shape, 1)
    zero = jnp.zeros_like(k2)
    keys = [
        jnp.concatenate([jnp.where((lane >= 64) == bool(h), k2, zero), key_aux], axis=1)
        for h in range(2)
    ]
    vts = [jnp.concatenate([vt[64 * h : 64 * h + 64], ones], axis=0) for h in range(2)]
    count = rows // block

    def score(index):
        q_cols = qa[:, block * index : block * index + block]
        return [dot(keys[h], q_cols) for h in range(2)]

    ahead = score(0)
    for index in range(count):
        scores = ahead
        if index + 1 < count:
            ahead = score(index + 1)
        span = slice(block * index, block * index + block)
        for h in range(2):
            peak = jnp.max(scores[h], axis=0, keepdims=True)
            probs = jnp.exp2((scores[h] - peak) * EXP_SCALE).astype(BF)
            mixed = dot(vts[h], probs)
            total = mixed[64:65]
            ot[64 * h : 64 * h + 64, span] = mixed[:64] * (1.0 / total)
            lse_out[pair, h : h + 1, span] = peak + jnp.log(total) * (1.0 / SCALE)
    ot_out[cols, :] = ot[...].astype(BF)
    o_out[:, cols] = ot[...].T.astype(BF)


def forward_kernel(me_ref, tokens, chain, mine, other, *refs):
    qkv_hbm, normed_t_hbm, weight_hbm, o_out, ot_out, lse_out = refs[:6]
    smalls, up_row, key_aux_out, query_aux_out = refs[6:10]
    qa, ot, columns, qkv_out, normed_out, normed_t, weight, sems = refs[10:]
    me = me_ref[1]
    for c, j, i in slots():
        source = (mine, other)[c]
        row = block_row(me, c, j, i, 16)
        weight[pl.ds(row, 16), :] = source[4 * j + i, :, 0:1536]
        columns[pl.ds(row, 16), :] = source[4 * j + i, :, 1536:1664].astype(F32)
    smalls[...] = columns[...].T[0:8, :]
    lane = lax.broadcasted_iota(jnp.int32, (1, 128), 1)
    for a in range(16):
        even = pltpu.roll(columns[32 * a : 32 * a + 8, :], 64, 1)[0:1, :]
        odd = columns[32 * a + 16 : 32 * a + 17, :]
        up_row[:, 128 * a : 128 * a + 128] = jnp.where(lane < 64, even, odd)
    query_side, key_side = aux_rows(chain[...])
    qa[128:256, :] = query_side
    query_aux_out[...] = query_side
    key_aux_out[...] = key_side

    def norm_block(index, carry):
        span = pl.ds(pl.multiple_of(index * 256, 256), 256)
        centred, scale = row_stats(tokens[span, :].astype(F32))
        normed_out[span, :] = (centred * scale * smalls[0:1, :] + smalls[2:3, :]).astype(BF)
        return carry

    lax.fori_loop(0, tokens.shape[0] // 256, norm_block, 0)
    normed = normed_out[...]
    normed_t[0:512, :] = normed.T
    ones_row = lax.broadcasted_iota(jnp.int32, (16, normed.shape[0]), 0) == 0
    normed_t[512:528, :] = ones_row.astype(F32).astype(BF)
    copies = [
        pltpu.make_async_copy(normed_t, normed_t_hbm, sems.at[4]),
        pltpu.make_async_copy(weight, weight_hbm, sems.at[5]),
    ]
    for copy in copies:
        copy.start()
    outs = (qkv_out, o_out, ot_out, lse_out)

    def one_pair(pair, carry):
        cols = block_of(pair, 128)
        pair_forward(
            normed_out[...], weight[:, block_of(pair, 384)], smalls[4:5, cols], smalls[5:6, cols],
            key_aux_out[...], qa, ot, outs, pair, 512,
        )
        pltpu.make_async_copy(qkv_out.at[pair], qkv_hbm.at[pair], sems.at[pair]).start()
        return carry

    lax.fori_loop(0, 4, one_pair, 0)
    for pair in range(4):
        pltpu.make_async_copy(qkv_out.at[pair], qkv_hbm.at[pair], sems.at[pair]).wait()
    for copy in copies:
        copy.wait()


def hbm():
    return pl.BlockSpec(memory_space=pltpu.HBM)


def forward(me, tokens, chain, mine, other):
    rows = tokens.shape[0]
    return pl.pallas_call(
        forward_kernel,
        in_specs=[smem()] + [vmem()] * 4,
        out_specs=[hbm()] * 3 + [vmem()] * 7,
        out_shape=[
            shape((4, 3, rows, 128), BF),
            shape((528, rows), BF),
            shape((512, 1536), BF),
            shape((rows, 512), BF),
            shape((512, rows), BF),
            shape((4, 2, rows), F32),
            shape((8, 512), F32),
            shape((1, 2048), F32),
            shape((rows, 128), BF),
            shape((128, rows), BF),
        ],
        scratch_shapes=[
            pltpu.VMEM((256, rows), BF),
            pltpu.VMEM((128, rows), F32),
            pltpu.VMEM((512, 128), F32),
            pltpu.VMEM((4, 3, rows, 128), BF),
            pltpu.VMEM((rows, 512), BF),
            pltpu.VMEM((528, rows), BF),
            pltpu.VMEM((512, 1536), BF),
            pltpu.SemaphoreType.DMA((6,)),
        ],
        compiler_params=pltpu.CompilerParams(vmem_limit_bytes=24 * MIB),
        cost_estimate=cost(15),
        name="attend",
    )(me, tokens, chain, mine, other)


def gelu_parts(u):
    half_cdf = 0.5 + 0.5 * lax.erf(u * math.sqrt(0.5))
    density = jnp.exp2(u * u * (-0.5 * math.log2(math.e))) * (1.0 / math.sqrt(2.0 * math.pi))
    return u * half_cdf, half_cdf + u * density


def scatter_tall(me, source, base_block, send, keep):
    core = me & 1
    for half in range(4):
        r = (me ^ (base_block + 2 * half)) >> 1
        place = ((r & 3) << 2) | (r >> 2)
        for part in range(4):
            row = 128 * half + 16 * part
            span = slice(512 * part, 512 * part + 512)
            keep[place, :, span] = source[pl.ds(pl.multiple_of(row + core * 64, 16), 16), :]
            sent = source[pl.ds(pl.multiple_of(row + (1 - core) * 64, 16), 16), :]
            send[place, :, span] = sent.astype(BF)


def scatter_blocks(me, source, rows, base_block, blocks, send, keep, span):
    core = me & 1
    for half in range(blocks // 2):
        first = base_block + 2 * half
        row = 2 * half * rows
        r = (me ^ first) >> 1
        place = ((r & 3) << 2) | (r >> 2)
        kept = source[pl.ds(pl.multiple_of(row + core * rows, rows), rows), :]
        sent = source[pl.ds(pl.multiple_of(row + (1 - core) * rows, rows), rows), :]
        keep[place, :, span] = kept
        send[place, :, span] = sent.astype(BF)


def feed_first_kernel(
    me_ref, tokens, o_in, mine, other, mine_tall, other_tall, smalls, up_row, cot,
    output, middle, normed_t, grad_pre_out, d_send, d_keep, mix, up, down, normed, total, stage,
):
    me = me_ref[0]
    for c, j, i in slots():
        source = (mine, other)[c]
        row = block_row(me, c, j, i, 16)
        mix[pl.ds(row, 16), :] = source[4 * j + i, :, 0:512]
        up[pl.ds(row, 16), :] = source[4 * j + i, :, 512:2560]
        source = (mine_tall, other_tall)[c]
        for part in range(4):
            row = pl.multiple_of(block_row(me, c, j, i, 64) + 16 * part, 16)
            span = slice(512 * part, 512 * part + 512)
            down[pl.ds(row, 16), :] = source[4 * TALL_ORDER[i] + j, :, span]
    rows = tokens.shape[0]
    block = 256

    def ahead(index, carry):
        span = pl.ds(pl.multiple_of(index * block, block), block)
        mid = tokens[span, :].astype(F32) + dot(o_in[span, :], mix[...]) + smalls[6:7, :]
        middle[span, :] = mid
        centred, scale = row_stats(mid)
        normed[span, :] = (centred * scale * smalls[1:2, :] + smalls[3:4, :]).astype(BF)
        total[span, :] = mid + smalls[7:8, :]
        return carry

    lax.fori_loop(0, rows // block, ahead, 0)
    normed_t[0:512, :] = normed[...].T
    ones_row = lax.broadcasted_iota(jnp.int32, (16, rows), 0) == 0
    normed_t[512:528, :] = ones_row.astype(F32).astype(BF)
    width = 512

    def one_chunk(chunk, carry):
        span = block_of(chunk, width)
        down_part = down[span, :]
        act, slope = gelu_parts(dot(normed[...], up[:, span]) + up_row[:, span])
        act_low = act.astype(BF)
        grad_pre_out[:, span] = (dot(cot[...], down_part, NT) * slope).astype(BF)
        total[...] += dot(act_low, down_part)
        stage[...] = dot(act_low, cot[...], TN)
        scatter_tall(me, stage, chunk * (width // 64), d_send, d_keep)
        return carry

    lax.fori_loop(0, 2048 // width, one_chunk, 0)
    output[...] = total[...].astype(BF)


def feed_first(me, tokens, o_in, b_pair, c_pair, smalls, up_row, cot):
    rows = tokens.shape[0]
    return pl.pallas_call(
        feed_first_kernel,
        in_specs=[smem()] + [vmem()] * 9,
        out_specs=[vmem()] * 8,
        out_shape=[
            shape((rows, 512), BF),
            shape((rows, 512), F32),
            shape((528, rows), BF),
            shape((rows, 2048), BF),
            shape((16, 16, 2048), BF),
            shape((16, 16, 2048), F32),
            shape((512, 512), BF),
            shape((512, 2048), BF),
        ],
        scratch_shapes=[
            pltpu.VMEM((2048, 512), BF),
            pltpu.VMEM((rows, 512), BF),
            pltpu.VMEM((rows, 512), F32),
            pltpu.VMEM((512, 512), F32),
        ],
        compiler_params=pltpu.CompilerParams(vmem_limit_bytes=24 * MIB),
        cost_estimate=cost(18),
        name="feed_first",
    )(me, tokens, o_in, *b_pair, *c_pair, smalls, up_row, cot)


def feed_second_kernel(me_ref, normed_t, grad_pre, u_send, u_keep, up_bias_grad, stage):
    me = me_ref[0]
    width = 512

    def one_chunk(chunk, carry):
        span = block_of(chunk, width)
        stage[...] = dot(normed_t[...], grad_pre[:, span])
        up_bias_grad[:, span] = stage[512:513, :]
        scatter_blocks(me, stage, 16, 0, 32, u_send, u_keep, span)
        return carry

    lax.fori_loop(0, 2048 // width, one_chunk, 0)


def feed_second(me, normed_t, grad_pre):
    return pl.pallas_call(
        feed_second_kernel,
        in_specs=[smem()] + [vmem()] * 2,
        out_specs=[vmem()] * 3,
        out_shape=[
            shape((16, 16, 2048), BF),
            shape((16, 16, 2048), F32),
            shape((1, 2048), F32),
        ],
        scratch_shapes=[pltpu.VMEM((528, 512), F32)],
        compiler_params=pltpu.CompilerParams(vmem_limit_bytes=20 * MIB),
        cost_estimate=cost(5),
        name="feed_second",
    )(me, normed_t, grad_pre)


def feed_third_kernel(
    middle, grad_pre, mix, up, smalls, cot, ot_in,
    grad_middle, grad_att, mix_grad, small_grads, low_rows,
):
    rows = middle.shape[0]
    block = 256

    def behind(index, carry):
        gain_sum, shift_sum, branch_sum, cot_sum = carry
        span = pl.ds(pl.multiple_of(index * block, block), block)
        centred, scale = row_stats(middle[span, :])
        xh = centred * scale
        h = dot(grad_pre[span, :], up[...], NT)
        hg = h * smalls[1:2, :]
        cot_rows = cot[span, :].astype(F32)
        grad = cot_rows + scale * (
            hg
            - jnp.mean(hg, axis=-1, keepdims=True)
            - xh * jnp.mean(hg * xh, axis=-1, keepdims=True)
        )
        grad_middle[span, :] = grad
        low = grad.astype(BF)
        low_rows[span, :] = low
        grad_att[span, :] = dot(low, mix[...], NT).astype(BF)
        return (
            gain_sum + jnp.sum(h * xh, axis=0, keepdims=True),
            shift_sum + jnp.sum(h, axis=0, keepdims=True),
            branch_sum + jnp.sum(low.astype(F32), axis=0, keepdims=True),
            cot_sum + jnp.sum(cot_rows, axis=0, keepdims=True),
        )

    zero = jnp.zeros((1, 512), F32)
    sums = lax.fori_loop(0, rows // block, behind, (zero, zero, zero, zero))
    for index in range(4):
        small_grads[index : index + 1, :] = sums[index]
    small_grads[4:8, :] = jnp.zeros((4, 512), F32)
    mix_grad[0:256, :] = dot(ot_in[0:256, :], low_rows[...])
    mix_grad[256:512, :] = dot(ot_in[256:512, :], low_rows[...])


def feed_third(middle, grad_pre, mix, up, smalls, cot, ot_in):
    rows = middle.shape[0]
    return pl.pallas_call(
        feed_third_kernel,
        in_specs=[vmem()] * 7,
        out_specs=[vmem()] * 4,
        out_shape=[
            shape((rows, 512), F32),
            shape((rows, 512), BF),
            shape((512, 512), F32),
            shape((8, 512), F32),
        ],
        scratch_shapes=[pltpu.VMEM((rows, 512), BF)],
        compiler_params=pltpu.CompilerParams(vmem_limit_bytes=20 * MIB),
        cost_estimate=cost(8),
        name="feed_third",
    )(middle, grad_pre, mix, up, smalls, cot, ot_in)


def pair_backward(q, k, v, do, ot_in, lse, key_aux, qa, da, dqt, acc_k, acc_v, gm, pair, block):
    k2 = k[0, 0]
    v2 = v[0, 0]
    rows = k2.shape[0]
    kt = k2.T
    lane = lax.broadcasted_iota(jnp.int32, k2.shape, 1)
    zero = jnp.zeros_like(k2)
    keys = []
    vals = []
    for h in range(2):
        own = (lane >= 64) == bool(h)
        keys.append(jnp.concatenate([jnp.where(own, k2, zero), key_aux], axis=1))
        vals.append(jnp.concatenate([jnp.where(own, v2, zero), key_aux], axis=1))
    qt = q[0, 0].T
    dt = do[...].T
    product = dt.astype(F32) * ot_in[...].astype(F32)
    row = lax.broadcasted_iota(jnp.int32, (16, rows), 0)
    for h in range(2):
        qa[h, 0:128, :] = qt
        da[h, 0:128, :] = dt
        delta = jnp.sum(product[64 * h : 64 * h + 64], axis=0, keepdims=True)
        base = qa[h, 128:144, :].astype(F32)
        one, two, three = split_three(-lse[pair, h : h + 1, :])
        base = jnp.where(row == 14, one, jnp.where(row == 15, two, base))
        qa[h, 128:144, :] = base.astype(BF)
        qa[h, 144:160, :] = jnp.where(row == 0, three, 0.0).astype(BF)
        one, two, three = split_three(-delta)
        base = jnp.where(row == 14, one, jnp.where(row == 15, two, 0.0))
        da[h, 128:144, :] = base.astype(BF)
        da[h, 144:160, :] = jnp.where(row == 0, three, 0.0).astype(BF)
    small_lane = lax.broadcasted_iota(jnp.int32, (block, 128), 1)
    for index in range(rows // block):
        span = slice(block * index, block * index + block)
        do_rows = do[span, :]
        q_rows = q[0, 0, span, :]
        blank = jnp.zeros_like(do_rows)
        sum_k = None
        sum_v = None
        for h in range(2):
            own = (small_lane >= 64) == bool(h)
            probs = jnp.exp2(dot(keys[h], qa[h, :, span]) * EXP_SCALE)
            grad = (probs * dot(vals[h], da[h, :, span])).astype(BF)
            probs = probs.astype(BF)
            dqt[64 * h : 64 * h + 64, span] = dot(kt[64 * h : 64 * h + 64, :], grad)
            part_k = dot(grad, jnp.where(own, q_rows, blank))
            part_v = dot(probs, jnp.where(own, do_rows, blank))
            sum_k = part_k if sum_k is None else sum_k + part_k
            sum_v = part_v if sum_v is None else sum_v + part_v
        if index == 0:
            acc_k[...] = sum_k
            acc_v[...] = sum_v
        else:
            acc_k[...] += sum_k
            acc_v[...] += sum_v
    gm[:, 0:128] = (dqt[...].T * SCALE).astype(BF)
    gm[:, 128:256] = (acc_k[...] * SCALE).astype(BF)
    gm[:, 256:384] = acc_v[...].astype(BF)


def backward_pair(q, k, v, do, ot_in, lse, key_aux, query_aux, gm, scratch, pair):
    qa, da, dqt, acc_k, acc_v = scratch
    for h in range(2):
        qa[h, 128:256, :] = query_aux[...]
        da[h, 128:256, :] = jnp.zeros((128, da.shape[2]), BF)
    pair_backward(q, k, v, do, ot_in, lse, key_aux[...], qa, da, dqt, acc_k, acc_v, gm, pair, 256)


def weight_terms(me, gm_first, gm, normed_t, weight, smalls, stage, send, keep, sums, vectors):
    stage[:, 0:384] = dot(normed_t[...], gm_first[...])
    stage[:, 384:768] = dot(normed_t[...], gm[...])
    total = stage[512:513, :]
    sums[0:1, :] = total
    scatter_blocks(me, stage, 16, 0, 32, send, keep, slice(0, 768))
    wide = weight[...].astype(F32)
    vectors[:, 0:1] = jnp.sum(stage[0:512, :] * wide, axis=1, keepdims=True)
    vectors[:, 1:2] = jnp.sum(wide * total, axis=1, keepdims=True)


def backward_even_kernel(pair, q, k, v, do, ot_in, lse, key_aux, query_aux, gm, *scratch):
    backward_pair(q, k, v, do, ot_in, lse, key_aux, query_aux, gm, scratch, pair)


def backward_odd_kernel(
    me_ref, q, k, v, do, ot_in, lse, key_aux, query_aux, gm_first, normed_t, weight, smalls,
    mix_grad, gm, send, keep, sums, vectors, *scratch,
):
    scatter_blocks(me_ref[0], mix_grad, 16, 0, 32, send, keep, slice(768, 1280))
    backward_pair(q, k, v, do, ot_in, lse, key_aux, query_aux, gm, scratch[:5], 1)
    weight_terms(
        me_ref[0], gm_first, gm, normed_t, weight, smalls, scratch[5], send, keep, sums, vectors
    )


def backward_last_kernel(
    me_ref, q, k, v, do, ot_in, lse, key_aux, query_aux, gm_first, normed_t, weight, smalls,
    small_grads, up_bias_grad, sums_first, vectors_first,
    gm, send, keep, *scratch,
):
    me = me_ref[0]
    stage, sums, vectors, columns = scratch[5:]
    backward_pair(q, k, v, do, ot_in, lse, key_aux, query_aux, gm, scratch[:5], 3)
    weight_terms(me, gm_first, gm, normed_t, weight, smalls, stage, send, keep, sums, vectors)
    columns[...] = jnp.zeros_like(columns)
    columns[1:2, :] = small_grads[0:1, :]
    columns[3:4, :] = small_grads[1:2, :]
    for pair in range(4):
        source = (sums_first, sums)[pair // 2]
        base = (pair % 2) * 384
        span = slice(128 * pair, 128 * pair + 128)
        columns[4:5, span] = source[0:1, base : base + 128]
        columns[5:6, span] = source[0:1, base + 256 : base + 384]
    columns[6:7, :] = small_grads[2:3, :]
    columns[7:8, :] = small_grads[3:4, :]
    columns[8:9, :] = smalls[0:1, :]
    columns[9:10, :] = smalls[2:3, :]
    tile = columns[...].T
    product = vectors[:, 0:1] + vectors_first[:, 0:1]
    plain = vectors[:, 1:2] + vectors_first[:, 1:2]
    gain_sum = (product - tile[:, 9:10] * plain) / tile[:, 8:9]
    lanes = lax.broadcasted_iota(jnp.int32, (512, 128), 1)
    stage[0:512, 0:128] = jnp.where(lanes == 0, gain_sum, jnp.where(lanes == 2, plain, tile))
    lane = lax.broadcasted_iota(jnp.int32, (1, 128), 1)
    for a in range(16):
        piece = up_bias_grad[:, 128 * a : 128 * a + 128]
        rolled = pltpu.roll(jnp.broadcast_to(piece, (8, 128)), 64, 1)[0:1, :]
        for half, values in enumerate((rolled, piece)):
            row = 32 * a + 16 * half
            stage[row : row + 1, 0:128] = jnp.where(lane < 64, stage[row : row + 1, 0:128], values)
    core = me & 1
    for half in range(16):
        r = (me ^ (2 * half)) >> 1
        place = ((r & 3) << 2) | (r >> 2)
        kept = pl.multiple_of(32 * half + core * 16, 16)
        sent = pl.multiple_of(32 * half + (1 - core) * 16, 16)
        keep[place, :, 768:896] = stage[pl.ds(kept, 16), 0:128]
        send[place, :, 768:896] = stage[pl.ds(sent, 16), 0:128].astype(BF)


def backward_scratch(rows):
    return [
        pltpu.VMEM((2, 256, rows), BF),
        pltpu.VMEM((2, 256, rows), BF),
        pltpu.VMEM((128, rows), F32),
        pltpu.VMEM((rows, 128), F32),
        pltpu.VMEM((rows, 128), F32),
    ]


def pair_specs(rows, pair):
    parts = [pl.BlockSpec((1, 1, rows, 128), lambda i, part=part: (pair, part, 0, 0)) for part in range(3)]
    return parts + [
        pl.BlockSpec((rows, 128), lambda i: (0, pair)),
        pl.BlockSpec((128, rows), lambda i: (pair, 0)),
        vmem(), vmem(), vmem(),
    ]


def backward_even(pair, *operands):
    rows = operands[3].shape[0]
    return pl.pallas_call(
        functools.partial(backward_even_kernel, pair),
        grid=(1,),
        in_specs=pair_specs(rows, pair),
        out_specs=vmem(),
        out_shape=shape((rows, 384), BF),
        scratch_shapes=backward_scratch(rows),
        compiler_params=pltpu.CompilerParams(vmem_limit_bytes=20 * MIB),
        cost_estimate=cost(8),
        name=f"attend_back_{pair}",
    )(*operands)


def backward_odd(me, *operands):
    rows = operands[3].shape[0]
    return pl.pallas_call(
        backward_odd_kernel,
        grid=(1,),
        in_specs=[smem()]
        + pair_specs(rows, 1)
        + [vmem(), vmem(), pl.BlockSpec((512, 768), lambda i: (0, 0)), vmem(), vmem()],
        out_specs=[vmem()] * 5,
        out_shape=[
            shape((rows, 384), BF),
            shape((16, 16, 1280), BF),
            shape((16, 16, 1280), F32),
            shape((8, 768), F32),
            shape((512, 128), F32),
        ],
        scratch_shapes=backward_scratch(rows) + [pltpu.VMEM((528, 768), F32)],
        compiler_params=pltpu.CompilerParams(vmem_limit_bytes=20 * MIB),
        cost_estimate=cost(9),
        name="attend_back_1",
    )(me, *operands)


def backward_last(me, *operands):
    rows = operands[3].shape[0]
    return pl.pallas_call(
        backward_last_kernel,
        grid=(1,),
        in_specs=[smem()]
        + pair_specs(rows, 3)
        + [vmem(), vmem(), pl.BlockSpec((512, 768), lambda i: (0, 1))]
        + [vmem()] * 5,
        out_specs=[vmem()] * 3,
        out_shape=[
            shape((rows, 384), BF),
            shape((16, 16, 896), BF),
            shape((16, 16, 896), F32),
        ],
        scratch_shapes=backward_scratch(rows)
        + [
            pltpu.VMEM((528, 768), F32),
            pltpu.VMEM((8, 768), F32),
            pltpu.VMEM((512, 128), F32),
            pltpu.VMEM((128, 512), F32),
        ],
        compiler_params=pltpu.CompilerParams(vmem_limit_bytes=20 * MIB),
        cost_estimate=cost(9),
        name="attend_back_3",
    )(me, *operands)


def input_kernel(tokens, gm0, gm1, gm2, gm3, weight, smalls, grad_middle, input_grad):
    block = 256

    def behind(index, carry):
        span = pl.ds(pl.multiple_of(index * block, block), block)
        centred, scale = row_stats(tokens[span, :].astype(F32))
        xh = centred * scale
        gm = jnp.concatenate([ref[span, :] for ref in (gm0, gm1, gm2, gm3)], axis=1)
        hg = dot(gm, weight[...], NT) * smalls[0:1, :]
        input_grad[span, :] = grad_middle[span, :] + scale * (
            hg
            - jnp.mean(hg, axis=-1, keepdims=True)
            - xh * jnp.mean(hg * xh, axis=-1, keepdims=True)
        )
        return carry

    lax.fori_loop(0, tokens.shape[0] // block, behind, 0)


def input_terms(operands):
    rows = operands[0].shape[0]
    return pl.pallas_call(
        input_kernel,
        in_specs=[vmem()] * 8,
        out_specs=vmem(),
        out_shape=shape((rows, 512), F32),
        compiler_params=pltpu.CompilerParams(vmem_limit_bytes=20 * MIB),
        cost_estimate=cost(5),
        name="input_terms",
    )(*operands)


def combine_kernel(counts, pieces, *refs):
    total_in = sum(counts) + len(counts)
    outs = refs[total_in:]
    position = 0
    base = 0
    for count in counts:
        own, incoming = refs[position], refs[position + 1 : position + 1 + count]
        position += 1 + count
        width = own.shape[2]
        rows = own.shape[0] // pieces
        for index in range(pieces):
            span = slice(rows * index, rows * index + rows)
            total = own[span]
            for ref in incoming:
                total = total + ref[span].astype(F32)
            outs[index][:, :, base : base + width] = total.astype(outs[index].dtype)
        base += width


def combine(name, pieces, *sums):
    slot_count = sums[0][0].shape[0] // pieces
    width = sum(own.shape[2] for own, _ in sums)
    operands = [part for own, received in sums for part in (own, *received)]
    dims = (slot_count, 16, width)
    first, *rest = pl.pallas_call(
        functools.partial(combine_kernel, [len(received) for _, received in sums], pieces),
        in_specs=[vmem()] * len(operands),
        out_specs=[vmem()] * pieces,
        out_shape=[shape(dims, F32)] + [shape(dims, BF)] * (pieces - 1),
        compiler_params=pltpu.CompilerParams(vmem_limit_bytes=24 * MIB),
        cost_estimate=cost(1.5),
        name=name,
    )(*operands)
    return first, rest


def finish_kernel(
    own, r0, r1, r2, du_own, du_recv,
    qkv_grad, mix_grad, up_grad, down_grad, gain, shift, qv, proj, bias,
):
    total = own[0]
    for ref in (r0, r1, r2):
        total = total + ref[0].astype(F32)
    mix_grad[...] = total[:, 768:1280]
    for pair in range(4):
        for part in range(3):
            base = (0, 384, 1280, 1664)[pair] + 128 * part
            column = 512 * part + 128 * pair
            qkv_grad[:, column : column + 128] = total[:, base : base + 128]
    tile = total[:, 2048:2176]
    wide = jnp.concatenate([tile, jnp.zeros((112, 128), F32)], axis=0).T
    for index, ref in enumerate((gain, shift, qv, proj)):
        ref[...] = wide[2 * index : 2 * index + 2, 0:16]
    bias[...] = tile[0:1, 64:128]
    total = du_own[0] + du_recv[0].astype(F32)
    for part in range(4):
        down_grad[16 * part : 16 * part + 16, :] = total[:, 512 * part : 512 * part + 512]
    up_grad[...] = total[:, 2048:4096]


def finish(own, received, du_own, du_recv):
    return pl.pallas_call(
        finish_kernel,
        in_specs=[vmem()] * 6,
        out_specs=[vmem()] * 9,
        out_shape=[
            shape((16, 1536), F32),
            shape((16, 512), F32),
            shape((16, 2048), F32),
            shape((64, 512), F32),
        ]
        + [shape((2, 16), F32)] * 4
        + [shape((1, 64), F32)],
        cost_estimate=cost(1.5),
        name="finish",
    )(own, *received, du_own, *du_recv)


def swap(value, mask, count):
    return lax.ppermute(value, AXES, [(d, d ^ mask) for d in range(count)])


Z_MASKS = (8, 16, 24)
PLANE_MASKS = (2, 4, 6)


def swaps(value, masks, count):
    return [swap(value, mask, count) for mask in masks]


def point(values, *tokens):
    return lax.optimization_barrier((values, tokens))[0]


def after(value, *tokens):
    return lax.optimization_barrier((value, tokens))[0]


def exchange(parts, masks, count):
    return [swap(part, mask, count) for part, mask in zip(parts, masks, strict=True)]


def group(own, others):
    joined = jnp.stack([own] + others)
    return joined.reshape((-1,) + joined.shape[-2:])


def pack_whole(qkv, mix, up, down, gain, shift, qv, proj, up_bias):
    pieces = []
    for pair in range(4):
        for part in range(3):
            base = 512 * part + 128 * pair
            pieces.append(qkv[:, base : base + 128])
    rows = jnp.concatenate([gain, shift, qv, proj], axis=0)
    tile = jnp.pad(rows.T, ((0, 0), (0, 120))).reshape(32, 16, 128)
    tile = tile.at[:, 0, 64:128].set(up_bias.reshape(32, 64))
    a0 = jnp.concatenate([jnp.concatenate(pieces, 1).reshape(32, 16, 1536), tile], axis=2)
    b0 = jnp.concatenate([mix, up], axis=1).reshape(32, 16, 2560)
    b1 = down.reshape(32, 4, 16, 512).swapaxes(1, 2).reshape(32, 16, 2048)
    return a0, b0, b1


def relative_halves(blocks):
    parts = blocks.reshape((4, 4, 2) + blocks.shape[1:])
    parts = parts.transpose((2, 1, 0) + tuple(range(3, parts.ndim)))
    return parts[0].reshape((16,) + blocks.shape[1:]), parts[1].reshape((16,) + blocks.shape[1:])


def whole_blocks(send, keep):
    parts = jnp.stack([keep, send.astype(F32)]).reshape((2, 4, 4) + keep.shape[1:])
    parts = parts.transpose((2, 1, 0) + tuple(range(3, parts.ndim)))
    return parts.reshape((32,) + keep.shape[1:])


def body(cubic, count, tokens, chain_ids, qkv, mix, up, down, gain, shift, qv, proj, up_bias, cot):
    params = (qkv, mix, up, down, gain, shift, qv, proj, up_bias)
    if cubic:
        index = lax.axis_index(AXES).astype(jnp.int32)
        me = jnp.stack([index, index & ~6])
        own, c_own = pack(*params)
        recv = swaps(own, Z_MASKS, count)
        c_recv = swaps(c_own, PLANE_MASKS, count)
        recv = point(recv)
        a_col = jnp.stack([part[:, :1664] for part in (own, *recv)])
        c_plane = group(c_own, after(c_recv, a_col))
        c_recv = swap(c_plane, 16, count)
        a_mine = lax.all_gather(after(a_col, c_plane), "plane").reshape(16, 16, -1)
        a_mine, c_recv = point((a_mine, c_recv))
        a_other = swap(a_mine, 1, count)
        own, *recv = after((own, *recv), a_mine)
        b_col = jnp.stack([part[:, 1664:] for part in (own, *recv)])
        b_recv = swaps(b_col, PLANE_MASKS, count)
        c_half = group(c_plane, [c_recv])
        c_recv = swap(c_half, 8, count)
        a_mine, a_other = after((a_mine, a_other), b_col, c_half)
    else:
        me = jnp.zeros((2,), jnp.int32)
        dims = (0, 0, 0, 0, 1, 1, 1, 1, 0)
        whole = [
            lax.all_gather(value, AXES, axis=dim, tiled=True)
            for value, dim in zip(params, dims, strict=True)
        ]
        a_parts, b_parts, c_parts = pack_whole(*whole)
        a_mine, a_other = relative_halves(a_parts)
        b_pair = relative_halves(b_parts)
        c_pair = [
            half.reshape(4, 2, 2, 16, 2048).transpose(2, 1, 0, 3, 4).reshape(16, 16, 2048)
            for half in relative_halves(c_parts)
        ]
    (
        qkv_rows, normed_t, weight, o, ot, lse, smalls, up_row, key_aux, query_aux,
    ) = forward(me, tokens, chain_ids, a_mine, a_other)
    if cubic:
        b_recv, c_recv, lse = point((b_recv, c_recv, lse))
        b_mine = group(b_col, b_recv)
        c_mine = group(c_half, [c_recv])
        b_pair = (b_mine, swap(b_mine, 1, count))
        c_pair = (c_mine, swap(c_mine, 1, count))
    output, middle, normed_two_t, grad_pre, d_send, d_keep, mix_whole, up_whole = feed_first(
        me, tokens, o, b_pair, c_pair, smalls, up_row, cot
    )
    if cubic:
        d_recv = swap(d_send, 1, count)
    u_send, u_keep, up_bias_grad = feed_second(me, normed_two_t, grad_pre)
    if cubic:
        u_recv = swap(u_send, 1, count)
    grad_middle, grad_att, mix_term, small_grads = feed_third(
        middle, grad_pre, mix_whole, up_whole, smalls, cot, ot
    )
    if cubic:
        d_recv, u_recv, small_grads = point((d_recv, u_recv, small_grads))
        du_own, du_parts = combine("feed_sum", 4, (d_keep, [d_recv]), (u_keep, [u_recv]))
        du_recv = exchange(du_parts, PLANE_MASKS, count)
        lse = after(lse, du_own)
    gm0 = backward_even(0, qkv_rows, qkv_rows, qkv_rows, grad_att, ot, lse, key_aux, query_aux)
    gm1, f_send, f_keep, sums, vectors = backward_odd(
        me, qkv_rows, qkv_rows, qkv_rows, grad_att, ot, lse, key_aux, query_aux, gm0, normed_t,
        weight, smalls, mix_term,
    )
    if cubic:
        f_recv = swap(f_send, 1, count)
    gm2 = backward_even(
        2, qkv_rows, qkv_rows, qkv_rows, grad_att, ot, after(lse, gm1), key_aux, query_aux
    )
    if cubic:
        du_recv, f_recv, gm2 = point((du_recv, f_recv, gm2))
        du_own, du_parts = combine("feed_sum_two", 2, (du_own, du_recv))
        du_recv = exchange(du_parts, (16,), count)
        f_own, f_parts = combine("qkv_sum", 4, (f_keep, [f_recv]))
        f_recv = exchange(f_parts, PLANE_MASKS, count)
        lse = after(lse, f_own, du_own)
    gm3, g_send, g_keep = backward_last(
        me, qkv_rows, qkv_rows, qkv_rows, grad_att, ot, lse, key_aux, query_aux, gm2, normed_t, weight, smalls,
        small_grads, up_bias_grad, sums, vectors,
    )
    operands = [tokens, gm0, gm1, gm2, gm3, weight, smalls, grad_middle]
    if cubic:
        f_recv, du_recv, g_send, operands[4] = point((f_recv, du_recv, g_send, gm3))
        g_recv = swap(g_send, 1, count)
        du_own, du_parts = combine("feed_sum_three", 2, (du_own, du_recv))
        du_recv = exchange(du_parts, (8,), count)
        g_own, g_parts = combine("last_sum", 4, (g_keep, [after(g_recv, du_own)]))
        g_recv = exchange(g_parts, PLANE_MASKS, count)
        operands[6] = after(smalls, g_own)
        input_grad = input_terms(operands)
        g_recv = after(g_recv, input_grad)
        own, parts = combine("join_sum", 4, (f_own, f_recv), (g_own, g_recv))
        qkv_grad, mix_grad, up_grad, down_grad, *vectors, bias_grad = finish(
            own, exchange(parts, Z_MASKS, count), du_own, du_recv
        )
        return (
            output, input_grad, qkv_grad, mix_grad, up_grad, down_grad, *vectors,
            bias_grad.reshape(64),
        )
    input_grad = input_terms(operands)
    pairs = ((d_send, d_keep), (u_send, u_keep), (f_send, f_keep), (g_send, g_keep))
    blocks = [whole_blocks(s, r) for s, r in pairs]
    tiles = blocks[3][:, :, 768:896]
    joined = blocks[2].reshape(512, 1280)
    wholes = (
        blocks[0].reshape(32, 16, 4, 512).swapaxes(1, 2).reshape(2048, 512),
        blocks[1].reshape(512, 2048),
        joined[:, 768:],
        unpack_columns([joined[:, :768], blocks[3][:, :, :768].reshape(512, 768)]),
        tiles[:, 0, 64:128].reshape(2048),
    )
    down_grad, up_grad, mix_grad, qkv_grad, bias_grad = [
        lax.psum_scatter(value, AXES, scatter_dimension=0, tiled=True) for value in wholes
    ]
    vectors = lax.psum_scatter(
        tiles[:, :, 0:8].reshape(512, 8).T, AXES, scatter_dimension=1, tiled=True
    )
    return (
        output, input_grad, qkv_grad, mix_grad, up_grad, down_grad,
        vectors[0:2], vectors[2:4], vectors[4:6], vectors[6:8], bias_grad,
    )


def unpack_columns(halves):
    pieces = []
    for part in range(3):
        for pair in range(4):
            base = (pair % 2) * 384 + 128 * part
            pieces.append(halves[pair // 2][:, base : base + 128])
    return jnp.concatenate(pieces, axis=1)


def solution(mesh):
    groups = mesh.shape["dp"]
    count = groups * mesh.shape["fsdp"]
    inner = jax.sharding.Mesh(mesh.devices.reshape(groups, -1, 2), AXES)
    cubic = inner.devices.shape == (4, 4, 2)

    def entry(*operands):
        return body(cubic, count, *operands)

    rows = P(AXES, None)
    columns = P(None, AXES)
    flat = P(AXES)
    return jax.shard_map(
        entry,
        mesh=inner,
        in_specs=(rows,) * 6 + (columns,) * 4 + (flat, rows),
        out_specs=(rows,) * 6 + (columns,) * 4 + (flat,),
        check_vma=False,
    )
```

```python
import functools
import math

import jax
import jax.numpy as jnp
from jax import lax
from jax.experimental import pallas as pl
from jax.experimental.pallas import tpu as pltpu
from jax.sharding import PartitionSpec as P

AXES = ("dp", "plane", "core")
HEADS = 8
EPS = 1e-05
SCALE = 0.125
EXP_SCALE = SCALE * math.log2(math.e)
HIDE = -(2.0**60)
MIB = 2**20

BF = jnp.bfloat16
F32 = jnp.float32
NN = (((1,), (0,)), ((), ()))
NT = (((1,), (1,)), ((), ()))
TN = (((0,), (0,)), ((), ()))


def dot(a, b, dims=NN):
    return lax.dot_general(a, b, dims, preferred_element_type=F32)


def vmem():
    return pl.BlockSpec(memory_space=pltpu.VMEM)


def smem():
    return pl.BlockSpec(memory_space=pltpu.SMEM)


def shape(dims, dtype):
    return jax.ShapeDtypeStruct(dims, dtype)


def block_of(index, block):
    return pl.ds(pl.multiple_of(index * block, block), block)


def cost(us):
    return pl.CostEstimate(flops=int(us * 1.1e9), bytes_accessed=0, transcendentals=0)


TALL_ORDER = (0, 2, 1, 3)


def slots():
    return [(c, j, i) for c in range(2) for j in range(4) for i in range(4)]


def block_row(me, c, j, i, rows):
    return pl.multiple_of((me ^ (c | (j << 1) | (i << 3))) * rows, rows)


def row_stats(rows_in):
    mean = jnp.mean(rows_in, axis=-1, keepdims=True)
    centred = rows_in - mean
    spread = jnp.mean(centred * centred, axis=-1, keepdims=True)
    return centred, lax.rsqrt(spread + EPS)


def split_three(row):
    first = row.astype(BF).astype(F32)
    rest = row - first
    second = rest.astype(BF).astype(F32)
    return first, second, rest - second


def pack_kernel(qkv, mix, up, down, gain, shift, qv, proj, up_bias, a0, c0, rows128):
    for pair in range(4):
        for part in range(3):
            base = 384 * pair + 128 * part
            a0[:, base : base + 128] = qkv[:, 512 * part + 128 * pair : 512 * part + 128 * pair + 128]
    rows128[...] = jnp.zeros_like(rows128)
    for index, ref in enumerate((gain, shift, qv, proj)):
        rows128[2 * index : 2 * index + 2, :] = ref[...].astype(F32)
    eye = (
        lax.broadcasted_iota(jnp.int32, (16, 16), 0) == lax.broadcasted_iota(jnp.int32, (16, 16), 1)
    ).astype(F32)
    columns = dot(eye.astype(BF), rows128[...].astype(BF), NT)
    bias = jnp.concatenate([jnp.zeros((1, 64), F32), up_bias[...].astype(F32)], axis=1)
    row = lax.broadcasted_iota(jnp.int32, (16, 128), 0)
    lane = lax.broadcasted_iota(jnp.int32, (16, 128), 1)
    a0[:, 1536:1664] = jnp.where((row == 0) & (lane >= 64), bias, columns).astype(BF)
    a0[:, 1664:2176] = mix[...]
    a0[:, 2176:4224] = up[...]
    for part in range(4):
        c0[:, 512 * part : 512 * part + 512] = down[16 * part : 16 * part + 16, :]


def pack(qkv, mix, up, down, gain, shift, qv, proj, up_bias):
    return pl.pallas_call(
        pack_kernel,
        in_specs=[vmem()] * 9,
        out_specs=[vmem()] * 2,
        out_shape=[shape((16, 4224), BF), shape((16, 2048), BF)],
        scratch_shapes=[pltpu.VMEM((128, 16), F32)],
        cost_estimate=cost(1.5),
        name="pack",
    )(qkv, mix, up, down, gain, shift, qv, proj, up_bias.reshape(1, 64))


def aux_rows(chain):
    row = lax.broadcasted_iota(jnp.int32, (128, chain.shape[1]), 0)
    low_bits = jnp.where(row < 7, (chain >> jnp.minimum(row, 6)) & 1, 0)
    high_bits = jnp.where(
        (row >= 7) & (row < 14), 1 - ((chain >> jnp.minimum(jnp.maximum(row - 7, 0), 6)) & 1), 0
    )
    bits = low_bits + high_bits
    query_side = bits.astype(F32) * HIDE
    key_side = jnp.where(row < 14, 1 - bits, jnp.where(row < 17, 1, 0)).astype(F32)
    return query_side.astype(BF), key_side.T.astype(BF)


def pair_forward(normed, weight, bias_q, bias_v, key_aux, qa, ot, outs, pair, block):
    qkv_out, o_out, ot_out, lse_out = outs
    rows = normed.shape[0]
    cols = block_of(pair, 128)
    q2 = (dot(normed, weight[:, 0:128]) + bias_q).astype(BF)
    k2 = dot(normed, weight[:, 128:256]).astype(BF)
    v2 = (dot(normed, weight[:, 256:384]) + bias_v).astype(BF)
    for index, value in enumerate((q2, k2, v2)):
        qkv_out[pair, index] = value
    qa[0:128, :] = q2.T
    vt = v2.T
    ones = (lax.broadcasted_iota(jnp.int32, (16, rows), 0) == 0).astype(F32).astype(BF)
    lane = lax.broadcasted_iota(jnp.int32, k2.shape, 1)
    zero = jnp.zeros_like(k2)
    keys = [
        jnp.concatenate([jnp.where((lane >= 64) == bool(h), k2, zero), key_aux], axis=1)
        for h in range(2)
    ]
    vts = [jnp.concatenate([vt[64 * h : 64 * h + 64], ones], axis=0) for h in range(2)]
    count = rows // block

    def score(index):
        q_cols = qa[:, block * index : block * index + block]
        return [dot(keys[h], q_cols) for h in range(2)]

    ahead = score(0)
    for index in range(count):
        scores = ahead
        if index + 1 < count:
            ahead = score(index + 1)
        span = slice(block * index, block * index + block)
        for h in range(2):
            peak = jnp.max(scores[h], axis=0, keepdims=True)
            probs = jnp.exp2((scores[h] - peak) * EXP_SCALE).astype(BF)
            mixed = dot(vts[h], probs)
            total = mixed[64:65]
            ot[64 * h : 64 * h + 64, span] = mixed[:64] * (1.0 / total)
            lse_out[pair, h : h + 1, span] = peak + jnp.log(total) * (1.0 / SCALE)
    ot_out[cols, :] = ot[...].astype(BF)
    o_out[:, cols] = ot[...].T.astype(BF)


def forward_kernel(me_ref, tokens, chain, mine, other, *refs):
    qkv_hbm, normed_t_hbm, weight_hbm, o_out, ot_out, lse_out = refs[:6]
    smalls, up_row, key_aux_out, query_aux_out = refs[6:10]
    qa, ot, columns, qkv_out, normed_out, normed_t, weight, sems = refs[10:]
    me = me_ref[1]
    for c, j, i in slots():
        source = (mine, other)[c]
        row = block_row(me, c, j, i, 16)
        weight[pl.ds(row, 16), :] = source[4 * j + i, :, 0:1536]
        columns[pl.ds(row, 16), :] = source[4 * j + i, :, 1536:1664].astype(F32)
    smalls[...] = columns[...].T[0:8, :]
    lane = lax.broadcasted_iota(jnp.int32, (1, 128), 1)
    for a in range(16):
        even = pltpu.roll(columns[32 * a : 32 * a + 8, :], 64, 1)[0:1, :]
        odd = columns[32 * a + 16 : 32 * a + 17, :]
        up_row[:, 128 * a : 128 * a + 128] = jnp.where(lane < 64, even, odd)
    query_side, key_side = aux_rows(chain[...])
    qa[128:256, :] = query_side
    query_aux_out[...] = query_side
    key_aux_out[...] = key_side

    def norm_block(index, carry):
        span = pl.ds(pl.multiple_of(index * 256, 256), 256)
        centred, scale = row_stats(tokens[span, :].astype(F32))
        normed_out[span, :] = (centred * scale * smalls[0:1, :] + smalls[2:3, :]).astype(BF)
        return carry

    lax.fori_loop(0, tokens.shape[0] // 256, norm_block, 0)
    normed = normed_out[...]
    normed_t[0:512, :] = normed.T
    ones_row = lax.broadcasted_iota(jnp.int32, (16, normed.shape[0]), 0) == 0
    normed_t[512:528, :] = ones_row.astype(F32).astype(BF)
    copies = [
        pltpu.make_async_copy(normed_t, normed_t_hbm, sems.at[4]),
        pltpu.make_async_copy(weight, weight_hbm, sems.at[5]),
    ]
    for copy in copies:
        copy.start()
    outs = (qkv_out, o_out, ot_out, lse_out)

    def one_pair(pair, carry):
        cols = block_of(pair, 128)
        pair_forward(
            normed_out[...], weight[:, block_of(pair, 384)], smalls[4:5, cols], smalls[5:6, cols],
            key_aux_out[...], qa, ot, outs, pair, 512,
        )
        pltpu.make_async_copy(qkv_out.at[pair], qkv_hbm.at[pair], sems.at[pair]).start()
        return carry

    lax.fori_loop(0, 4, one_pair, 0)
    for pair in range(4):
        pltpu.make_async_copy(qkv_out.at[pair], qkv_hbm.at[pair], sems.at[pair]).wait()
    for copy in copies:
        copy.wait()


def hbm():
    return pl.BlockSpec(memory_space=pltpu.HBM)


def forward(me, tokens, chain, mine, other):
    rows = tokens.shape[0]
    return pl.pallas_call(
        forward_kernel,
        in_specs=[smem()] + [vmem()] * 4,
        out_specs=[hbm()] * 3 + [vmem()] * 7,
        out_shape=[
            shape((4, 3, rows, 128), BF),
            shape((528, rows), BF),
            shape((512, 1536), BF),
            shape((rows, 512), BF),
            shape((512, rows), BF),
            shape((4, 2, rows), F32),
            shape((8, 512), F32),
            shape((1, 2048), F32),
            shape((rows, 128), BF),
            shape((128, rows), BF),
        ],
        scratch_shapes=[
            pltpu.VMEM((256, rows), BF),
            pltpu.VMEM((128, rows), F32),
            pltpu.VMEM((512, 128), F32),
            pltpu.VMEM((4, 3, rows, 128), BF),
            pltpu.VMEM((rows, 512), BF),
            pltpu.VMEM((528, rows), BF),
            pltpu.VMEM((512, 1536), BF),
            pltpu.SemaphoreType.DMA((6,)),
        ],
        compiler_params=pltpu.CompilerParams(vmem_limit_bytes=20 * MIB),
        cost_estimate=cost(15),
        name="attend",
    )(me, tokens, chain, mine, other)


def gelu_parts(u):
    half_cdf = 0.5 + 0.5 * lax.erf(u * math.sqrt(0.5))
    density = jnp.exp2(u * u * (-0.5 * math.log2(math.e))) * (1.0 / math.sqrt(2.0 * math.pi))
    return u * half_cdf, half_cdf + u * density


def scatter_tall(me, source, base_block, send, keep):
    core = me & 1
    for half in range(4):
        r = (me ^ (base_block + 2 * half)) >> 1
        place = ((r & 3) << 2) | (r >> 2)
        for part in range(4):
            row = 128 * half + 16 * part
            span = slice(512 * part, 512 * part + 512)
            keep[place, :, span] = source[pl.ds(pl.multiple_of(row + core * 64, 16), 16), :]
            sent = source[pl.ds(pl.multiple_of(row + (1 - core) * 64, 16), 16), :]
            send[place, :, span] = sent.astype(BF)


def scatter_blocks(me, source, rows, base_block, blocks, send, keep, span):
    core = me & 1
    for half in range(blocks // 2):
        first = base_block + 2 * half
        row = 2 * half * rows
        r = (me ^ first) >> 1
        place = ((r & 3) << 2) | (r >> 2)
        kept = source[pl.ds(pl.multiple_of(row + core * rows, rows), rows), :]
        sent = source[pl.ds(pl.multiple_of(row + (1 - core) * rows, rows), rows), :]
        keep[place, :, span] = kept
        send[place, :, span] = sent.astype(BF)


def feed_first_kernel(
    me_ref, tokens, o_in, mine, other, mine_tall, other_tall, smalls, up_row, cot,
    middle, normed_t, grad_pre_out, d_send, d_keep, mix, up, act_rows, down,
    normed, stage,
):
    me = me_ref[0]
    for c, j, i in slots():
        source = (mine, other)[c]
        row = block_row(me, c, j, i, 16)
        mix[pl.ds(row, 16), :] = source[4 * j + i, :, 0:512]
        up[pl.ds(row, 16), :] = source[4 * j + i, :, 512:2560]
        source = (mine_tall, other_tall)[c]
        for part in range(4):
            row = pl.multiple_of(block_row(me, c, j, i, 64) + 16 * part, 16)
            span = slice(512 * part, 512 * part + 512)
            down[pl.ds(row, 16), :] = source[4 * TALL_ORDER[i] + j, :, span]
    rows = tokens.shape[0]
    block = 256

    def ahead(index, carry):
        span = pl.ds(pl.multiple_of(index * block, block), block)
        mid = tokens[span, :].astype(F32) + dot(o_in[span, :], mix[...]) + smalls[6:7, :]
        middle[span, :] = mid
        centred, scale = row_stats(mid)
        normed[span, :] = (centred * scale * smalls[1:2, :] + smalls[3:4, :]).astype(BF)
        return carry

    lax.fori_loop(0, rows // block, ahead, 0)
    normed_t[0:512, :] = normed[...].T
    ones_row = lax.broadcasted_iota(jnp.int32, (16, rows), 0) == 0
    normed_t[512:528, :] = ones_row.astype(F32).astype(BF)
    width = 512

    def one_chunk(chunk, carry):
        span = block_of(chunk, width)
        down_part = down[span, :]
        act, slope = gelu_parts(dot(normed[...], up[:, span]) + up_row[:, span])
        act_low = act.astype(BF)
        grad_pre_out[:, span] = (dot(cot[...], down_part, NT) * slope).astype(BF)
        act_rows[:, span] = act_low
        stage[...] = dot(act_low, cot[...], TN)
        scatter_tall(me, stage, chunk * (width // 64), d_send, d_keep)
        return carry

    lax.fori_loop(0, 2048 // width, one_chunk, 0)


def feed_first(me, tokens, o_in, b_pair, c_pair, smalls, up_row, cot):
    rows = tokens.shape[0]
    return pl.pallas_call(
        feed_first_kernel,
        in_specs=[smem()] + [vmem()] * 9,
        out_specs=[vmem()] * 9,
        out_shape=[
            shape((rows, 512), F32),
            shape((528, rows), BF),
            shape((rows, 2048), BF),
            shape((16, 16, 2048), BF),
            shape((16, 16, 2048), F32),
            shape((512, 512), BF),
            shape((512, 2048), BF),
            shape((rows, 2048), BF),
            shape((2048, 512), BF),
        ],
        scratch_shapes=[
            pltpu.VMEM((rows, 512), BF),
            pltpu.VMEM((512, 512), F32),
        ],
        compiler_params=pltpu.CompilerParams(vmem_limit_bytes=14 * MIB),
        cost_estimate=cost(18),
        name="feed_first",
    )(me, tokens, o_in, *b_pair, *c_pair, smalls, up_row, cot)


def feed_second_kernel(me_ref, normed_t, grad_pre, u_send, u_keep, up_bias_grad, stage):
    me = me_ref[0]
    width = 512

    def one_chunk(chunk, carry):
        span = block_of(chunk, width)
        stage[...] = dot(normed_t[...], grad_pre[:, span])
        up_bias_grad[:, span] = stage[512:513, :]
        scatter_blocks(me, stage, 16, 0, 32, u_send, u_keep, span)
        return carry

    lax.fori_loop(0, 2048 // width, one_chunk, 0)


def feed_second(me, normed_t, grad_pre):
    return pl.pallas_call(
        feed_second_kernel,
        in_specs=[smem()] + [vmem()] * 2,
        out_specs=[vmem()] * 3,
        out_shape=[
            shape((16, 16, 2048), BF),
            shape((16, 16, 2048), F32),
            shape((1, 2048), F32),
        ],
        scratch_shapes=[pltpu.VMEM((528, 512), F32)],
        compiler_params=pltpu.CompilerParams(vmem_limit_bytes=10 * MIB),
        cost_estimate=cost(5),
        name="feed_second",
    )(me, normed_t, grad_pre)


def feed_third_kernel(
    middle, grad_pre, mix, up, smalls, cot, ot_in,
    grad_middle, grad_att, mix_grad, small_grads, low_rows,
):
    rows = middle.shape[0]
    block = 256

    def behind(index, carry):
        gain_sum, shift_sum, branch_sum, cot_sum = carry
        span = pl.ds(pl.multiple_of(index * block, block), block)
        centred, scale = row_stats(middle[span, :])
        xh = centred * scale
        h = dot(grad_pre[span, :], up[...], NT)
        hg = h * smalls[1:2, :]
        cot_rows = cot[span, :].astype(F32)
        grad = cot_rows + scale * (
            hg
            - jnp.mean(hg, axis=-1, keepdims=True)
            - xh * jnp.mean(hg * xh, axis=-1, keepdims=True)
        )
        grad_middle[span, :] = grad
        low = grad.astype(BF)
        low_rows[span, :] = low
        grad_att[span, :] = dot(low, mix[...], NT).astype(BF)
        return (
            gain_sum + jnp.sum(h * xh, axis=0, keepdims=True),
            shift_sum + jnp.sum(h, axis=0, keepdims=True),
            branch_sum + jnp.sum(low.astype(F32), axis=0, keepdims=True),
            cot_sum + jnp.sum(cot_rows, axis=0, keepdims=True),
        )

    zero = jnp.zeros((1, 512), F32)
    sums = lax.fori_loop(0, rows // block, behind, (zero, zero, zero, zero))
    for index in range(4):
        small_grads[index : index + 1, :] = sums[index]
    small_grads[4:8, :] = jnp.zeros((4, 512), F32)
    mix_grad[0:256, :] = dot(ot_in[0:256, :], low_rows[...])
    mix_grad[256:512, :] = dot(ot_in[256:512, :], low_rows[...])


def feed_third(middle, grad_pre, mix, up, smalls, cot, ot_in):
    rows = middle.shape[0]
    return pl.pallas_call(
        feed_third_kernel,
        in_specs=[vmem()] * 7,
        out_specs=[vmem()] * 4,
        out_shape=[
            shape((rows, 512), F32),
            shape((rows, 512), BF),
            shape((512, 512), F32),
            shape((8, 512), F32),
        ],
        scratch_shapes=[pltpu.VMEM((rows, 512), BF)],
        compiler_params=pltpu.CompilerParams(vmem_limit_bytes=12 * MIB),
        cost_estimate=cost(8),
        name="feed_third",
    )(middle, grad_pre, mix, up, smalls, cot, ot_in)


def pair_backward(q, k, v, do, ot_in, lse, key_aux, qa, da, dqt, acc_k, acc_v, gm, block):
    k2 = k[0, 0]
    v2 = v[0, 0]
    rows = k2.shape[0]
    kt = k2.T
    lane = lax.broadcasted_iota(jnp.int32, k2.shape, 1)
    zero = jnp.zeros_like(k2)
    keys = []
    vals = []
    for h in range(2):
        own = (lane >= 64) == bool(h)
        keys.append(jnp.concatenate([jnp.where(own, k2, zero), key_aux], axis=1))
        vals.append(jnp.concatenate([jnp.where(own, v2, zero), key_aux], axis=1))
    qt = q[0, 0].T
    dt = do[...].T
    product = dt.astype(F32) * ot_in[...].astype(F32)
    row = lax.broadcasted_iota(jnp.int32, (16, rows), 0)
    for h in range(2):
        qa[h, 0:128, :] = qt
        da[h, 0:128, :] = dt
        delta = jnp.sum(product[64 * h : 64 * h + 64], axis=0, keepdims=True)
        base = qa[h, 128:144, :].astype(F32)
        one, two, three = split_three(-lse[0, h : h + 1, :])
        base = jnp.where(row == 14, one, jnp.where(row == 15, two, base))
        qa[h, 128:144, :] = base.astype(BF)
        qa[h, 144:160, :] = jnp.where(row == 0, three, 0.0).astype(BF)
        one, two, three = split_three(-delta)
        base = jnp.where(row == 14, one, jnp.where(row == 15, two, 0.0))
        da[h, 128:144, :] = base.astype(BF)
        da[h, 144:160, :] = jnp.where(row == 0, three, 0.0).astype(BF)
    small_lane = lax.broadcasted_iota(jnp.int32, (block, 128), 1)
    for index in range(rows // block):
        span = slice(block * index, block * index + block)
        do_rows = do[span, :]
        q_rows = q[0, 0, span, :]
        blank = jnp.zeros_like(do_rows)
        sum_k = None
        sum_v = None
        for h in range(2):
            own = (small_lane >= 64) == bool(h)
            probs = jnp.exp2(dot(keys[h], qa[h, :, span]) * EXP_SCALE)
            grad = (probs * dot(vals[h], da[h, :, span])).astype(BF)
            probs = probs.astype(BF)
            dqt[64 * h : 64 * h + 64, span] = dot(kt[64 * h : 64 * h + 64, :], grad)
            part_k = dot(grad, jnp.where(own, q_rows, blank))
            part_v = dot(probs, jnp.where(own, do_rows, blank))
            sum_k = part_k if sum_k is None else sum_k + part_k
            sum_v = part_v if sum_v is None else sum_v + part_v
        if index == 0:
            acc_k[...] = sum_k
            acc_v[...] = sum_v
        else:
            acc_k[...] += sum_k
            acc_v[...] += sum_v
    gm[:, 0:128] = (dqt[...].T * SCALE).astype(BF)
    gm[:, 128:256] = (acc_k[...] * SCALE).astype(BF)
    gm[:, 256:384] = acc_v[...].astype(BF)


def backward_kernel(
    me_ref, q, k, v, do, ot_in, lse, weight, key_aux, query_aux, normed_t, smalls, small_grads,
    up_bias_grad, mix_term, gm, send, keep,
    qa, da, dqt, acc_k, acc_v, gm_pair, stage, sums, vectors, columns,
):
    me = me_ref[0]
    pair = pl.program_id(0)

    @pl.when(pair == 0)
    def _():
        for h in range(2):
            qa[h, 128:256, :] = query_aux[...]
            da[h, 128:256, :] = jnp.zeros((128, da.shape[2]), BF)
        vectors[...] = jnp.zeros_like(vectors)
        scatter_blocks(me, mix_term, 16, 0, 32, send, keep, slice(1536, 2048))

    pair_backward(q, k, v, do, ot_in, lse, key_aux[...], qa, da, dqt, acc_k, acc_v, gm_pair, 512)
    span = block_of(pair, 384)
    gm[:, span] = gm_pair[...]
    stage[...] = dot(normed_t[...], gm_pair[...])
    total = stage[512:513, :]
    sums[:, span] = jnp.broadcast_to(total, (8, 384))
    scatter_blocks(me, stage, 16, 0, 32, send, keep, span)
    wide = weight[...].astype(F32)
    vectors[:, 0:1] += jnp.sum(stage[0:512, :] * wide, axis=1, keepdims=True)
    vectors[:, 1:2] += jnp.sum(wide * total, axis=1, keepdims=True)

    @pl.when(pair == 3)
    def _():
        columns[...] = jnp.zeros_like(columns)
        columns[1:2, :] = small_grads[0:1, :]
        columns[3:4, :] = small_grads[1:2, :]
        for index in range(4):
            cols = slice(128 * index, 128 * index + 128)
            columns[4:5, cols] = sums[0:1, 384 * index : 384 * index + 128]
            columns[5:6, cols] = sums[0:1, 384 * index + 256 : 384 * index + 384]
        columns[6:7, :] = small_grads[2:3, :]
        columns[7:8, :] = small_grads[3:4, :]
        columns[8:9, :] = smalls[0:1, :]
        columns[9:10, :] = smalls[2:3, :]
        tile = columns[...].T
        plain = vectors[:, 1:2]
        gain_sum = (vectors[:, 0:1] - tile[:, 9:10] * plain) / tile[:, 8:9]
        lanes = lax.broadcasted_iota(jnp.int32, (512, 128), 1)
        stage[0:512, 0:128] = jnp.where(lanes == 0, gain_sum, jnp.where(lanes == 2, plain, tile))
        lane = lax.broadcasted_iota(jnp.int32, (1, 128), 1)
        for a in range(16):
            piece = up_bias_grad[:, 128 * a : 128 * a + 128]
            rolled = pltpu.roll(jnp.broadcast_to(piece, (8, 128)), 64, 1)[0:1, :]
            for half, values in enumerate((rolled, piece)):
                row = 32 * a + 16 * half
                old = stage[row : row + 1, 0:128]
                stage[row : row + 1, 0:128] = jnp.where(lane < 64, old, values)
        core = me & 1
        for half in range(16):
            r = (me ^ (2 * half)) >> 1
            place = ((r & 3) << 2) | (r >> 2)
            kept = pl.multiple_of(32 * half + core * 16, 16)
            sent = pl.multiple_of(32 * half + (1 - core) * 16, 16)
            keep[place, :, 2048:2176] = stage[pl.ds(kept, 16), 0:128]
            send[place, :, 2048:2176] = stage[pl.ds(sent, 16), 0:128].astype(BF)


def backward(me, qkv_rows, do, ot, lse, weight, *rest):
    rows = do.shape[0]
    parts = [pl.BlockSpec((1, 1, rows, 128), lambda i, part=part: (i, part, 0, 0)) for part in range(3)]
    return pl.pallas_call(
        backward_kernel,
        grid=(4,),
        in_specs=[smem()]
        + parts
        + [
            pl.BlockSpec((rows, 128), lambda i: (0, i)),
            pl.BlockSpec((128, rows), lambda i: (i, 0)),
            pl.BlockSpec((1, 2, rows), lambda i: (i, 0, 0)),
            pl.BlockSpec((512, 384), lambda i: (0, i)),
        ]
        + [vmem()] * 7,
        out_specs=[vmem()] * 3,
        out_shape=[
            shape((rows, 1536), BF),
            shape((16, 16, 2176), BF),
            shape((16, 16, 2176), F32),
        ],
        scratch_shapes=[
            pltpu.VMEM((2, 256, rows), BF),
            pltpu.VMEM((2, 256, rows), BF),
            pltpu.VMEM((128, rows), F32),
            pltpu.VMEM((rows, 128), F32),
            pltpu.VMEM((rows, 128), F32),
            pltpu.VMEM((rows, 384), BF),
            pltpu.VMEM((528, 384), F32),
            pltpu.VMEM((8, 1536), F32),
            pltpu.VMEM((512, 128), F32),
            pltpu.VMEM((128, 512), F32),
        ],
        compiler_params=pltpu.CompilerParams(vmem_limit_bytes=20 * MIB),
        cost_estimate=cost(25),
        name="attend_back",
    )(me, qkv_rows, qkv_rows, qkv_rows, do, ot, lse, weight, *rest)


def input_kernel(
    tokens, gm, weight, smalls, grad_middle, act, down, middle, input_grad, output
):
    block = 256

    def behind(index, carry):
        span = pl.ds(pl.multiple_of(index * block, block), block)
        centred, scale = row_stats(tokens[span, :].astype(F32))
        xh = centred * scale
        total = middle[span, :] + dot(act[span, :], down[...]) + smalls[7:8, :]
        output[span, :] = total.astype(BF)
        hg = dot(gm[span, :], weight[...], NT) * smalls[0:1, :]
        input_grad[span, :] = grad_middle[span, :] + scale * (
            hg
            - jnp.mean(hg, axis=-1, keepdims=True)
            - xh * jnp.mean(hg * xh, axis=-1, keepdims=True)
        )
        return carry

    lax.fori_loop(0, tokens.shape[0] // block, behind, 0)


def input_terms(operands):
    rows = operands[0].shape[0]
    return pl.pallas_call(
        input_kernel,
        in_specs=[vmem()] * 8,
        out_specs=[vmem()] * 2,
        out_shape=[shape((rows, 512), F32), shape((rows, 512), BF)],
        compiler_params=pltpu.CompilerParams(vmem_limit_bytes=12 * MIB),
        cost_estimate=cost(8),
        name="input_terms",
    )(*operands)


def combine_kernel(counts, pieces, *refs):
    total_in = sum(counts) + len(counts)
    outs = refs[total_in:]
    position = 0
    base = 0
    for count in counts:
        own, incoming = refs[position], refs[position + 1 : position + 1 + count]
        position += 1 + count
        width = own.shape[2]
        rows = own.shape[0] // pieces
        for index in range(pieces):
            span = slice(rows * index, rows * index + rows)
            total = own[span]
            for ref in incoming:
                total = total + ref[span].astype(F32)
            outs[index][:, :, base : base + width] = total.astype(outs[index].dtype)
        base += width


def combine(name, pieces, *sums):
    slot_count = sums[0][0].shape[0] // pieces
    width = sum(own.shape[2] for own, _ in sums)
    operands = [part for own, received in sums for part in (own, *received)]
    dims = (slot_count, 16, width)
    first, *rest = pl.pallas_call(
        functools.partial(combine_kernel, [len(received) for _, received in sums], pieces),
        in_specs=[vmem()] * len(operands),
        out_specs=[vmem()] * pieces,
        out_shape=[shape(dims, F32)] + [shape(dims, BF)] * (pieces - 1),
        compiler_params=pltpu.CompilerParams(vmem_limit_bytes=8 * MIB),
        cost_estimate=cost(1.5),
        name=name,
    )(*operands)
    return first, rest


def finish_kernel(
    own, r0, r1, r2, du_own, du_recv,
    qkv_grad, mix_grad, up_grad, down_grad, gain, shift, qv, proj, bias,
):
    total = own[0]
    for ref in (r0, r1, r2):
        total = total + ref[0].astype(F32)
    mix_grad[...] = total[:, 1536:2048]
    for pair in range(4):
        for part in range(3):
            base = 384 * pair + 128 * part
            column = 512 * part + 128 * pair
            qkv_grad[:, column : column + 128] = total[:, base : base + 128]
    tile = total[:, 2048:2176]
    wide = jnp.concatenate([tile, jnp.zeros((112, 128), F32)], axis=0).T
    for index, ref in enumerate((gain, shift, qv, proj)):
        ref[...] = wide[2 * index : 2 * index + 2, 0:16]
    bias[...] = tile[0:1, 64:128]
    total = du_own[0] + du_recv[0].astype(F32)
    for part in range(4):
        down_grad[16 * part : 16 * part + 16, :] = total[:, 512 * part : 512 * part + 512]
    up_grad[...] = total[:, 2048:4096]


def finish(own, received, du_own, du_recv):
    return pl.pallas_call(
        finish_kernel,
        in_specs=[vmem()] * 6,
        out_specs=[vmem()] * 9,
        out_shape=[
            shape((16, 1536), F32),
            shape((16, 512), F32),
            shape((16, 2048), F32),
            shape((64, 512), F32),
        ]
        + [shape((2, 16), F32)] * 4
        + [shape((1, 64), F32)],
        cost_estimate=cost(1.5),
        name="finish",
    )(own, *received, du_own, *du_recv)


def swap(value, mask, count):
    return lax.ppermute(value, AXES, [(d, d ^ mask) for d in range(count)])


Z_MASKS = (8, 16, 24)
PLANE_MASKS = (2, 4, 6)


def swaps(value, masks, count):
    return [swap(value, mask, count) for mask in masks]


def point(values, *tokens):
    return lax.optimization_barrier((values, tokens))[0]


def after(value, *tokens):
    return lax.optimization_barrier((value, tokens))[0]


def exchange(parts, masks, count):
    return [swap(part, mask, count) for part, mask in zip(parts, masks, strict=True)]


def group(own, others):
    joined = jnp.stack([own] + others)
    return joined.reshape((-1,) + joined.shape[-2:])


def pack_whole(qkv, mix, up, down, gain, shift, qv, proj, up_bias):
    pieces = []
    for pair in range(4):
        for part in range(3):
            base = 512 * part + 128 * pair
            pieces.append(qkv[:, base : base + 128])
    rows = jnp.concatenate([gain, shift, qv, proj], axis=0)
    tile = jnp.pad(rows.T, ((0, 0), (0, 120))).reshape(32, 16, 128)
    tile = tile.at[:, 0, 64:128].set(up_bias.reshape(32, 64))
    a0 = jnp.concatenate([jnp.concatenate(pieces, 1).reshape(32, 16, 1536), tile], axis=2)
    b0 = jnp.concatenate([mix, up], axis=1).reshape(32, 16, 2560)
    b1 = down.reshape(32, 4, 16, 512).swapaxes(1, 2).reshape(32, 16, 2048)
    return a0, b0, b1


def relative_halves(blocks):
    parts = blocks.reshape((4, 4, 2) + blocks.shape[1:])
    parts = parts.transpose((2, 1, 0) + tuple(range(3, parts.ndim)))
    return parts[0].reshape((16,) + blocks.shape[1:]), parts[1].reshape((16,) + blocks.shape[1:])


def whole_blocks(send, keep):
    parts = jnp.stack([keep, send.astype(F32)]).reshape((2, 4, 4) + keep.shape[1:])
    parts = parts.transpose((2, 1, 0) + tuple(range(3, parts.ndim)))
    return parts.reshape((32,) + keep.shape[1:])


def body(cubic, count, tokens, chain_ids, qkv, mix, up, down, gain, shift, qv, proj, up_bias, cot):
    params = (qkv, mix, up, down, gain, shift, qv, proj, up_bias)
    if cubic:
        index = lax.axis_index(AXES).astype(jnp.int32)
        me = jnp.stack([index, index & ~6])
        own, c_own = pack(*params)
        recv = swaps(own, Z_MASKS, count)
        c_recv = swaps(c_own, PLANE_MASKS, count)
        recv = point(recv)
        a_col = jnp.stack([part[:, :1664] for part in (own, *recv)])
        c_plane = group(c_own, after(c_recv, a_col))
        c_recv = swap(c_plane, 16, count)
        a_mine = lax.all_gather(after(a_col, c_plane), "plane").reshape(16, 16, -1)
        a_mine, c_recv = point((a_mine, c_recv))
        a_other = swap(a_mine, 1, count)
        own, *recv = after((own, *recv), a_mine)
        b_col = jnp.stack([part[:, 1664:] for part in (own, *recv)])
        b_recv = swaps(b_col, PLANE_MASKS, count)
        c_half = group(c_plane, [c_recv])
        c_recv = swap(c_half, 8, count)
        a_mine, a_other = after((a_mine, a_other), b_col, c_half)
    else:
        me = jnp.zeros((2,), jnp.int32)
        dims = (0, 0, 0, 0, 1, 1, 1, 1, 0)
        whole = [
            lax.all_gather(value, AXES, axis=dim, tiled=True)
            for value, dim in zip(params, dims, strict=True)
        ]
        a_parts, b_parts, c_parts = pack_whole(*whole)
        a_mine, a_other = relative_halves(a_parts)
        b_pair = relative_halves(b_parts)
        c_pair = [
            half.reshape(4, 2, 2, 16, 2048).transpose(2, 1, 0, 3, 4).reshape(16, 16, 2048)
            for half in relative_halves(c_parts)
        ]
    (
        qkv_rows, normed_t, weight, o, ot, lse, smalls, up_row, key_aux, query_aux,
    ) = forward(me, tokens, chain_ids, a_mine, a_other)
    if cubic:
        b_recv, c_recv, lse = point((b_recv, c_recv, lse))
        b_mine = group(b_col, b_recv)
        c_mine = group(c_half, [c_recv])
        b_pair = (b_mine, swap(b_mine, 1, count))
        c_pair = (c_mine, swap(c_mine, 1, count))
    (
        middle, normed_two_t, grad_pre, d_send, d_keep, mix_whole, up_whole, act_rows, down_whole,
    ) = feed_first(me, tokens, o, b_pair, c_pair, smalls, up_row, cot)
    if cubic:
        d_recv = swap(d_send, 1, count)
    u_send, u_keep, up_bias_grad = feed_second(me, normed_two_t, grad_pre)
    if cubic:
        u_recv = swap(u_send, 1, count)
    grad_middle, grad_att, mix_term, small_grads = feed_third(
        middle, grad_pre, mix_whole, up_whole, smalls, cot, ot
    )
    if cubic:
        d_recv, u_recv, small_grads = point((d_recv, u_recv, small_grads))
        du_own, du_parts = combine("feed_sum", 4, (d_keep, [d_recv]), (u_keep, [u_recv]))
        du_recv = exchange(du_parts, PLANE_MASKS, count)
        lse = after(lse, du_own)
    gm, g_send, g_keep = backward(
        me, qkv_rows, grad_att, ot, lse, weight, key_aux, query_aux, normed_t, smalls, small_grads,
        up_bias_grad, mix_term,
    )
    if cubic:
        du_recv, g_send, gm = point((du_recv, g_send, gm))
        g_recv = swap(g_send, 1, count)
        du_own, du_parts = combine("feed_sum_two", 2, (du_own, du_recv))
        du_recv = exchange(du_parts, (16,), count)
        g_own, g_parts = combine("last_sum", 4, (g_keep, [after(g_recv, du_own)]))
        g_recv = exchange(g_parts, PLANE_MASKS, count)
        smalls = after(smalls, g_own)
    input_grad, output = input_terms(
        [tokens, gm, weight, smalls, grad_middle, act_rows, down_whole, middle]
    )
    if cubic:
        g_recv, du_recv, input_grad = point((g_recv, du_recv, input_grad))
        own, parts = combine("last_sum_two", 4, (g_own, g_recv))
        g_recv = exchange(parts, Z_MASKS, count)
        du_own, du_parts = combine("feed_sum_three", 2, (du_own, du_recv))
        du_recv = exchange(du_parts, (8,), count)
        qkv_grad, mix_grad, up_grad, down_grad, *vectors, bias_grad = finish(
            own, g_recv, du_own, du_recv
        )
        return (
            output, input_grad, qkv_grad, mix_grad, up_grad, down_grad, *vectors,
            bias_grad.reshape(64),
        )
    pairs = ((d_send, d_keep), (u_send, u_keep), (g_send, g_keep))
    blocks = [whole_blocks(s, r) for s, r in pairs]
    tiles = blocks[2][:, :, 2048:2176]
    joined = blocks[2].reshape(512, 2176)
    wholes = (
        blocks[0].reshape(32, 16, 4, 512).swapaxes(1, 2).reshape(2048, 512),
        blocks[1].reshape(512, 2048),
        joined[:, 1536:2048],
        joined[:, :1536].reshape(512, 4, 3, 128).swapaxes(1, 2).reshape(512, 1536),
        tiles[:, 0, 64:128].reshape(2048),
    )
    down_grad, up_grad, mix_grad, qkv_grad, bias_grad = [
        lax.psum_scatter(value, AXES, scatter_dimension=0, tiled=True) for value in wholes
    ]
    vectors = lax.psum_scatter(
        tiles[:, :, 0:8].reshape(512, 8).T, AXES, scatter_dimension=1, tiled=True
    )
    return (
        output, input_grad, qkv_grad, mix_grad, up_grad, down_grad,
        vectors[0:2], vectors[2:4], vectors[4:6], vectors[6:8], bias_grad,
    )


def solution(mesh):
    groups = mesh.shape["dp"]
    count = groups * mesh.shape["fsdp"]
    inner = jax.sharding.Mesh(mesh.devices.reshape(groups, -1, 2), AXES)
    cubic = inner.devices.shape == (4, 4, 2)

    def entry(*operands):
        return body(cubic, count, *operands)

    rows = P(AXES, None)
    columns = P(None, AXES)
    flat = P(AXES)
    return jax.shard_map(
        entry,
        mesh=inner,
        in_specs=(rows,) * 6 + (columns,) * 4 + (flat, rows),
        out_specs=(rows,) * 6 + (columns,) * 4 + (flat,),
        check_vma=False,
    )
```

```python
import functools
import math

import jax
import jax.numpy as jnp
from jax import lax
from jax.experimental import pallas as pl
from jax.experimental.pallas import tpu as pltpu
from jax.sharding import PartitionSpec as P

AXES = ("dp", "plane", "core")
HEADS = 8
EPS = 1e-05
SCALE = 0.125
EXP_SCALE = SCALE * math.log2(math.e)
HIDE = -(2.0**60)
MIB = 2**20

BF = jnp.bfloat16
F32 = jnp.float32
NN = (((1,), (0,)), ((), ()))
NT = (((1,), (1,)), ((), ()))
TN = (((0,), (0,)), ((), ()))


def dot(a, b, dims=NN):
    return lax.dot_general(a, b, dims, preferred_element_type=F32)


def vmem():
    return pl.BlockSpec(memory_space=pltpu.VMEM)


def smem():
    return pl.BlockSpec(memory_space=pltpu.SMEM)


def shape(dims, dtype):
    return jax.ShapeDtypeStruct(dims, dtype)


def block_of(index, block):
    return pl.ds(pl.multiple_of(index * block, block), block)


def cost(us):
    return pl.CostEstimate(flops=int(us * 1.1e9), bytes_accessed=0, transcendentals=0)


TALL_ORDER = (0, 2, 1, 3)


def slots():
    return [(c, j, i) for c in range(2) for j in range(4) for i in range(4)]


def block_row(me, c, j, i, rows):
    return pl.multiple_of((me ^ (c | (j << 1) | (i << 3))) * rows, rows)


def row_stats(rows_in):
    mean = jnp.mean(rows_in, axis=-1, keepdims=True)
    centred = rows_in - mean
    spread = jnp.mean(centred * centred, axis=-1, keepdims=True)
    return centred, lax.rsqrt(spread + EPS)


def split_three(row):
    first = row.astype(BF).astype(F32)
    rest = row - first
    second = rest.astype(BF).astype(F32)
    return first, second, rest - second


def pack_kernel(qkv, mix, up, down, gain, shift, qv, proj, up_bias, a0, c0, rows128):
    for pair in range(4):
        for part in range(3):
            base = 384 * pair + 128 * part
            a0[:, base : base + 128] = qkv[:, 512 * part + 128 * pair : 512 * part + 128 * pair + 128]
    rows128[...] = jnp.zeros_like(rows128)
    for index, ref in enumerate((gain, shift, qv, proj)):
        rows128[2 * index : 2 * index + 2, :] = ref[...].astype(F32)
    eye = (
        lax.broadcasted_iota(jnp.int32, (16, 16), 0) == lax.broadcasted_iota(jnp.int32, (16, 16), 1)
    ).astype(F32)
    columns = dot(eye.astype(BF), rows128[...].astype(BF), NT)
    bias = jnp.concatenate([jnp.zeros((1, 64), F32), up_bias[...].astype(F32)], axis=1)
    row = lax.broadcasted_iota(jnp.int32, (16, 128), 0)
    lane = lax.broadcasted_iota(jnp.int32, (16, 128), 1)
    a0[:, 1536:1664] = jnp.where((row == 0) & (lane >= 64), bias, columns).astype(BF)
    a0[:, 1664:2176] = mix[...]
    a0[:, 2176:4224] = up[...]
    for part in range(4):
        c0[:, 512 * part : 512 * part + 512] = down[16 * part : 16 * part + 16, :]


def pack(qkv, mix, up, down, gain, shift, qv, proj, up_bias):
    return pl.pallas_call(
        pack_kernel,
        in_specs=[vmem()] * 9,
        out_specs=[vmem()] * 2,
        out_shape=[shape((16, 4224), BF), shape((16, 2048), BF)],
        scratch_shapes=[pltpu.VMEM((128, 16), F32)],
        cost_estimate=cost(1.5),
        name="pack",
    )(qkv, mix, up, down, gain, shift, qv, proj, up_bias.reshape(1, 64))


def aux_rows(chain):
    row = lax.broadcasted_iota(jnp.int32, (128, chain.shape[1]), 0)
    low_bits = jnp.where(row < 7, (chain >> jnp.minimum(row, 6)) & 1, 0)
    high_bits = jnp.where(
        (row >= 7) & (row < 14), 1 - ((chain >> jnp.minimum(jnp.maximum(row - 7, 0), 6)) & 1), 0
    )
    bits = low_bits + high_bits
    query_side = bits.astype(F32) * HIDE
    key_side = jnp.where(row < 14, 1 - bits, jnp.where(row < 17, 1, 0)).astype(F32)
    return query_side.astype(BF), key_side.T.astype(BF)


def pair_forward(normed, weight, bias_q, bias_v, key_aux, qa, ot, outs, pair, block):
    qkv_out, o_out, ot_out, lse_out = outs
    rows = normed.shape[0]
    cols = block_of(pair, 128)
    q2 = (dot(normed, weight[:, 0:128]) + bias_q).astype(BF)
    k2 = dot(normed, weight[:, 128:256]).astype(BF)
    v2 = (dot(normed, weight[:, 256:384]) + bias_v).astype(BF)
    for index, value in enumerate((q2, k2, v2)):
        qkv_out[pair, index] = value
    qa[0:128, :] = q2.T
    vt = v2.T
    ones = (lax.broadcasted_iota(jnp.int32, (16, rows), 0) == 0).astype(F32).astype(BF)
    lane = lax.broadcasted_iota(jnp.int32, k2.shape, 1)
    zero = jnp.zeros_like(k2)
    keys = [
        jnp.concatenate([jnp.where((lane >= 64) == bool(h), k2, zero), key_aux], axis=1)
        for h in range(2)
    ]
    vts = [jnp.concatenate([vt[64 * h : 64 * h + 64], ones], axis=0) for h in range(2)]
    count = rows // block

    def score(index):
        q_cols = qa[:, block * index : block * index + block]
        return [dot(keys[h], q_cols) for h in range(2)]

    ahead = score(0)
    for index in range(count):
        scores = ahead
        if index + 1 < count:
            ahead = score(index + 1)
        span = slice(block * index, block * index + block)
        for h in range(2):
            peak = jnp.max(scores[h], axis=0, keepdims=True)
            probs = jnp.exp2((scores[h] - peak) * EXP_SCALE).astype(BF)
            mixed = dot(vts[h], probs)
            total = mixed[64:65]
            ot[64 * h : 64 * h + 64, span] = mixed[:64] * (1.0 / total)
            lse_out[pair, h : h + 1, span] = peak + jnp.log(total) * (1.0 / SCALE)
    ot_out[cols, :] = ot[...].astype(BF)
    o_out[:, cols] = ot[...].T.astype(BF)


def forward_kernel(me_ref, tokens, chain, mine, other, *refs):
    qkv_hbm, normed_t_hbm, weight_hbm, o_out, ot_out, lse_out = refs[:6]
    smalls, up_row, key_aux_out, query_aux_out = refs[6:10]
    qa, ot, columns, qkv_out, normed_out, normed_t, weight, sems = refs[10:]
    me = me_ref[1]
    for c, j, i in slots():
        source = (mine, other)[c]
        row = block_row(me, c, j, i, 16)
        weight[pl.ds(row, 16), :] = source[4 * j + i, :, 0:1536]
        columns[pl.ds(row, 16), :] = source[4 * j + i, :, 1536:1664].astype(F32)
    smalls[...] = columns[...].T[0:8, :]
    lane = lax.broadcasted_iota(jnp.int32, (1, 128), 1)
    for a in range(16):
        even = pltpu.roll(columns[32 * a : 32 * a + 8, :], 64, 1)[0:1, :]
        odd = columns[32 * a + 16 : 32 * a + 17, :]
        up_row[:, 128 * a : 128 * a + 128] = jnp.where(lane < 64, even, odd)
    query_side, key_side = aux_rows(chain[...])
    qa[128:256, :] = query_side
    query_aux_out[...] = query_side
    key_aux_out[...] = key_side

    def norm_block(index, carry):
        span = pl.ds(pl.multiple_of(index * 256, 256), 256)
        centred, scale = row_stats(tokens[span, :].astype(F32))
        normed_out[span, :] = (centred * scale * smalls[0:1, :] + smalls[2:3, :]).astype(BF)
        return carry

    lax.fori_loop(0, tokens.shape[0] // 256, norm_block, 0)
    normed = normed_out[...]
    normed_t[0:512, :] = normed.T
    ones_row = lax.broadcasted_iota(jnp.int32, (16, normed.shape[0]), 0) == 0
    normed_t[512:528, :] = ones_row.astype(F32).astype(BF)
    copies = [
        pltpu.make_async_copy(normed_t, normed_t_hbm, sems.at[4]),
        pltpu.make_async_copy(weight, weight_hbm, sems.at[5]),
    ]
    for copy in copies:
        copy.start()
    outs = (qkv_out, o_out, ot_out, lse_out)

    def one_pair(pair, carry):
        cols = block_of(pair, 128)
        pair_forward(
            normed_out[...], weight[:, block_of(pair, 384)], smalls[4:5, cols], smalls[5:6, cols],
            key_aux_out[...], qa, ot, outs, pair, 512,
        )
        pltpu.make_async_copy(qkv_out.at[pair], qkv_hbm.at[pair], sems.at[pair]).start()
        return carry

    lax.fori_loop(0, 4, one_pair, 0)
    for pair in range(4):
        pltpu.make_async_copy(qkv_out.at[pair], qkv_hbm.at[pair], sems.at[pair]).wait()
    for copy in copies:
        copy.wait()


def hbm():
    return pl.BlockSpec(memory_space=pltpu.HBM)


def forward(me, tokens, chain, mine, other):
    rows = tokens.shape[0]
    return pl.pallas_call(
        forward_kernel,
        in_specs=[smem()] + [vmem()] * 4,
        out_specs=[hbm()] * 3 + [vmem()] * 7,
        out_shape=[
            shape((4, 3, rows, 128), BF),
            shape((528, rows), BF),
            shape((512, 1536), BF),
            shape((rows, 512), BF),
            shape((512, rows), BF),
            shape((4, 2, rows), F32),
            shape((8, 512), F32),
            shape((1, 2048), F32),
            shape((rows, 128), BF),
            shape((128, rows), BF),
        ],
        scratch_shapes=[
            pltpu.VMEM((256, rows), BF),
            pltpu.VMEM((128, rows), F32),
            pltpu.VMEM((512, 128), F32),
            pltpu.VMEM((4, 3, rows, 128), BF),
            pltpu.VMEM((rows, 512), BF),
            pltpu.VMEM((528, rows), BF),
            pltpu.VMEM((512, 1536), BF),
            pltpu.SemaphoreType.DMA((6,)),
        ],
        compiler_params=pltpu.CompilerParams(vmem_limit_bytes=20 * MIB),
        cost_estimate=cost(15),
        name="attend",
    )(me, tokens, chain, mine, other)


def gelu_parts(u):
    half_cdf = 0.5 + 0.5 * lax.erf(u * math.sqrt(0.5))
    density = jnp.exp2(u * u * (-0.5 * math.log2(math.e))) * (1.0 / math.sqrt(2.0 * math.pi))
    return u * half_cdf, half_cdf + u * density


def scatter_tall(me, source, base_block, send, keep):
    core = me & 1
    for half in range(4):
        r = (me ^ (base_block + 2 * half)) >> 1
        place = ((r & 3) << 2) | (r >> 2)
        for part in range(4):
            row = 128 * half + 16 * part
            span = slice(512 * part, 512 * part + 512)
            keep[place, :, span] = source[pl.ds(pl.multiple_of(row + core * 64, 16), 16), :]
            sent = source[pl.ds(pl.multiple_of(row + (1 - core) * 64, 16), 16), :]
            send[place, :, span] = sent.astype(BF)


def scatter_blocks(me, source, rows, base_block, blocks, send, keep, span):
    core = me & 1
    for half in range(blocks // 2):
        first = base_block + 2 * half
        row = 2 * half * rows
        r = (me ^ first) >> 1
        place = ((r & 3) << 2) | (r >> 2)
        kept = source[pl.ds(pl.multiple_of(row + core * rows, rows), rows), :]
        sent = source[pl.ds(pl.multiple_of(row + (1 - core) * rows, rows), rows), :]
        keep[place, :, span] = kept
        send[place, :, span] = sent.astype(BF)


def feed_first_kernel(
    me_ref, tokens, o_in, mine, other, mine_tall, other_tall, smalls, up_row, cot,
    middle, normed_t, grad_pre_out, d_send, d_keep, mix, up, act_rows, down,
    normed, stage,
):
    me = me_ref[0]
    for c, j, i in slots():
        source = (mine, other)[c]
        row = block_row(me, c, j, i, 16)
        mix[pl.ds(row, 16), :] = source[4 * j + i, :, 0:512]
        up[pl.ds(row, 16), :] = source[4 * j + i, :, 512:2560]
        source = (mine_tall, other_tall)[c]
        for part in range(4):
            row = pl.multiple_of(block_row(me, c, j, i, 64) + 16 * part, 16)
            span = slice(512 * part, 512 * part + 512)
            down[pl.ds(row, 16), :] = source[4 * TALL_ORDER[i] + j, :, span]
    rows = tokens.shape[0]
    block = 256

    def ahead(index, carry):
        span = pl.ds(pl.multiple_of(index * block, block), block)
        mid = tokens[span, :].astype(F32) + dot(o_in[span, :], mix[...]) + smalls[6:7, :]
        middle[span, :] = mid
        centred, scale = row_stats(mid)
        normed[span, :] = (centred * scale * smalls[1:2, :] + smalls[3:4, :]).astype(BF)
        return carry

    lax.fori_loop(0, rows // block, ahead, 0)
    normed_t[0:512, :] = normed[...].T
    ones_row = lax.broadcasted_iota(jnp.int32, (16, rows), 0) == 0
    normed_t[512:528, :] = ones_row.astype(F32).astype(BF)
    width = 512

    def one_chunk(chunk, carry):
        span = block_of(chunk, width)
        down_part = down[span, :]
        act, slope = gelu_parts(dot(normed[...], up[:, span]) + up_row[:, span])
        act_low = act.astype(BF)
        grad_pre_out[:, span] = (dot(cot[...], down_part, NT) * slope).astype(BF)
        act_rows[:, span] = act_low
        stage[...] = dot(act_low, cot[...], TN)
        scatter_tall(me, stage, chunk * (width // 64), d_send, d_keep)
        return carry

    lax.fori_loop(0, 2048 // width, one_chunk, 0)


def feed_first(me, tokens, o_in, b_pair, c_pair, smalls, up_row, cot):
    rows = tokens.shape[0]
    return pl.pallas_call(
        feed_first_kernel,
        in_specs=[smem()] + [vmem()] * 9,
        out_specs=[vmem()] * 9,
        out_shape=[
            shape((rows, 512), F32),
            shape((528, rows), BF),
            shape((rows, 2048), BF),
            shape((16, 16, 2048), BF),
            shape((16, 16, 2048), F32),
            shape((512, 512), BF),
            shape((512, 2048), BF),
            shape((rows, 2048), BF),
            shape((2048, 512), BF),
        ],
        scratch_shapes=[
            pltpu.VMEM((rows, 512), BF),
            pltpu.VMEM((512, 512), F32),
        ],
        compiler_params=pltpu.CompilerParams(vmem_limit_bytes=14 * MIB),
        cost_estimate=cost(18),
        name="feed_first",
    )(me, tokens, o_in, *b_pair, *c_pair, smalls, up_row, cot)


def feed_second_kernel(me_ref, normed_t, grad_pre, u_send, u_keep, up_bias_grad, stage):
    me = me_ref[0]
    width = 512

    def one_chunk(chunk, carry):
        span = block_of(chunk, width)
        stage[...] = dot(normed_t[...], grad_pre[:, span])
        up_bias_grad[:, span] = stage[512:513, :]
        scatter_blocks(me, stage, 16, 0, 32, u_send, u_keep, span)
        return carry

    lax.fori_loop(0, 2048 // width, one_chunk, 0)


def feed_second(me, normed_t, grad_pre):
    return pl.pallas_call(
        feed_second_kernel,
        in_specs=[smem()] + [vmem()] * 2,
        out_specs=[vmem()] * 3,
        out_shape=[
            shape((16, 16, 2048), BF),
            shape((16, 16, 2048), F32),
            shape((1, 2048), F32),
        ],
        scratch_shapes=[pltpu.VMEM((528, 512), F32)],
        compiler_params=pltpu.CompilerParams(vmem_limit_bytes=10 * MIB),
        cost_estimate=cost(5),
        name="feed_second",
    )(me, normed_t, grad_pre)


def feed_third_kernel(
    middle, grad_pre, mix, up, smalls, cot, ot_in,
    grad_middle, grad_att, mix_grad, small_grads, low_rows,
):
    rows = middle.shape[0]
    block = 256

    def behind(index, carry):
        gain_sum, shift_sum, branch_sum, cot_sum = carry
        span = pl.ds(pl.multiple_of(index * block, block), block)
        centred, scale = row_stats(middle[span, :])
        xh = centred * scale
        h = dot(grad_pre[span, :], up[...], NT)
        hg = h * smalls[1:2, :]
        cot_rows = cot[span, :].astype(F32)
        grad = cot_rows + scale * (
            hg
            - jnp.mean(hg, axis=-1, keepdims=True)
            - xh * jnp.mean(hg * xh, axis=-1, keepdims=True)
        )
        grad_middle[span, :] = grad
        low = grad.astype(BF)
        low_rows[span, :] = low
        grad_att[span, :] = dot(low, mix[...], NT).astype(BF)
        return (
            gain_sum + jnp.sum(h * xh, axis=0, keepdims=True),
            shift_sum + jnp.sum(h, axis=0, keepdims=True),
            branch_sum + jnp.sum(low.astype(F32), axis=0, keepdims=True),
            cot_sum + jnp.sum(cot_rows, axis=0, keepdims=True),
        )

    zero = jnp.zeros((1, 512), F32)
    sums = lax.fori_loop(0, rows // block, behind, (zero, zero, zero, zero))
    for index in range(4):
        small_grads[index : index + 1, :] = sums[index]
    small_grads[4:8, :] = jnp.zeros((4, 512), F32)
    mix_grad[0:256, :] = dot(ot_in[0:256, :], low_rows[...])
    mix_grad[256:512, :] = dot(ot_in[256:512, :], low_rows[...])


def feed_third(middle, grad_pre, mix, up, smalls, cot, ot_in):
    rows = middle.shape[0]
    return pl.pallas_call(
        feed_third_kernel,
        in_specs=[vmem()] * 7,
        out_specs=[vmem()] * 4,
        out_shape=[
            shape((rows, 512), F32),
            shape((rows, 512), BF),
            shape((512, 512), F32),
            shape((8, 512), F32),
        ],
        scratch_shapes=[pltpu.VMEM((rows, 512), BF)],
        compiler_params=pltpu.CompilerParams(vmem_limit_bytes=12 * MIB),
        cost_estimate=cost(8),
        name="feed_third",
    )(middle, grad_pre, mix, up, smalls, cot, ot_in)


def pair_backward(q, k, v, do, ot_in, lse, key_aux, qa, da, dqt, acc_k, acc_v, gm, block):
    k2 = k[0, 0]
    v2 = v[0, 0]
    rows = k2.shape[0]
    kt = k2.T
    lane = lax.broadcasted_iota(jnp.int32, k2.shape, 1)
    zero = jnp.zeros_like(k2)
    keys = []
    vals = []
    for h in range(2):
        own = (lane >= 64) == bool(h)
        keys.append(jnp.concatenate([jnp.where(own, k2, zero), key_aux], axis=1))
        vals.append(jnp.concatenate([jnp.where(own, v2, zero), key_aux], axis=1))
    qt = q[0, 0].T
    dt = do[...].T
    product = dt.astype(F32) * ot_in[...].astype(F32)
    row = lax.broadcasted_iota(jnp.int32, (16, rows), 0)
    for h in range(2):
        qa[h, 0:128, :] = qt
        da[h, 0:128, :] = dt
        delta = jnp.sum(product[64 * h : 64 * h + 64], axis=0, keepdims=True)
        base = qa[h, 128:144, :].astype(F32)
        one, two, three = split_three(-lse[0, h : h + 1, :])
        base = jnp.where(row == 14, one, jnp.where(row == 15, two, base))
        qa[h, 128:144, :] = base.astype(BF)
        qa[h, 144:160, :] = jnp.where(row == 0, three, 0.0).astype(BF)
        one, two, three = split_three(-delta)
        base = jnp.where(row == 14, one, jnp.where(row == 15, two, 0.0))
        da[h, 128:144, :] = base.astype(BF)
        da[h, 144:160, :] = jnp.where(row == 0, three, 0.0).astype(BF)
    small_lane = lax.broadcasted_iota(jnp.int32, (block, 128), 1)
    for index in range(rows // block):
        span = slice(block * index, block * index + block)
        do_rows = do[span, :]
        q_rows = q[0, 0, span, :]
        blank = jnp.zeros_like(do_rows)
        sum_k = None
        sum_v = None
        for h in range(2):
            own = (small_lane >= 64) == bool(h)
            probs = jnp.exp2(dot(keys[h], qa[h, :, span]) * EXP_SCALE)
            grad = (probs * dot(vals[h], da[h, :, span])).astype(BF)
            probs = probs.astype(BF)
            dqt[64 * h : 64 * h + 64, span] = dot(kt[64 * h : 64 * h + 64, :], grad)
            part_k = dot(grad, jnp.where(own, q_rows, blank))
            part_v = dot(probs, jnp.where(own, do_rows, blank))
            sum_k = part_k if sum_k is None else sum_k + part_k
            sum_v = part_v if sum_v is None else sum_v + part_v
        if index == 0:
            acc_k[...] = sum_k
            acc_v[...] = sum_v
        else:
            acc_k[...] += sum_k
            acc_v[...] += sum_v
    gm[:, 0:128] = (dqt[...].T * SCALE).astype(BF)
    gm[:, 128:256] = (acc_k[...] * SCALE).astype(BF)
    gm[:, 256:384] = acc_v[...].astype(BF)


def backward_kernel(
    me_ref, q, k, v, do, ot_in, lse, weight, key_aux, query_aux, normed_t, smalls, small_grads,
    up_bias_grad, mix_term, gm, send, keep,
    qa, da, dqt, acc_k, acc_v, gm_pair, stage, sums, vectors, columns,
):
    me = me_ref[0]
    pair = pl.program_id(0)

    @pl.when(pair == 0)
    def _():
        for h in range(2):
            qa[h, 128:256, :] = query_aux[...]
            da[h, 128:256, :] = jnp.zeros((128, da.shape[2]), BF)
        vectors[...] = jnp.zeros_like(vectors)
        scatter_blocks(me, mix_term, 16, 0, 32, send, keep, slice(1536, 2048))

    pair_backward(q, k, v, do, ot_in, lse, key_aux[...], qa, da, dqt, acc_k, acc_v, gm_pair, 512)
    span = block_of(pair, 384)
    gm[:, span] = gm_pair[...]
    stage[...] = dot(normed_t[...], gm_pair[...])
    total = stage[512:513, :]
    sums[:, span] = jnp.broadcast_to(total, (8, 384))
    scatter_blocks(me, stage, 16, 0, 32, send, keep, span)
    wide = weight[...].astype(F32)
    vectors[:, 0:1] += jnp.sum(stage[0:512, :] * wide, axis=1, keepdims=True)
    vectors[:, 1:2] += jnp.sum(wide * total, axis=1, keepdims=True)

    @pl.when(pair == 3)
    def _():
        columns[...] = jnp.zeros_like(columns)
        columns[1:2, :] = small_grads[0:1, :]
        columns[3:4, :] = small_grads[1:2, :]
        for index in range(4):
            cols = slice(128 * index, 128 * index + 128)
            columns[4:5, cols] = sums[0:1, 384 * index : 384 * index + 128]
            columns[5:6, cols] = sums[0:1, 384 * index + 256 : 384 * index + 384]
        columns[6:7, :] = small_grads[2:3, :]
        columns[7:8, :] = small_grads[3:4, :]
        columns[8:9, :] = smalls[0:1, :]
        columns[9:10, :] = smalls[2:3, :]
        tile = columns[...].T
        plain = vectors[:, 1:2]
        gain_sum = (vectors[:, 0:1] - tile[:, 9:10] * plain) / tile[:, 8:9]
        lanes = lax.broadcasted_iota(jnp.int32, (512, 128), 1)
        stage[0:512, 0:128] = jnp.where(lanes == 0, gain_sum, jnp.where(lanes == 2, plain, tile))
        lane = lax.broadcasted_iota(jnp.int32, (1, 128), 1)
        for a in range(16):
            piece = up_bias_grad[:, 128 * a : 128 * a + 128]
            rolled = pltpu.roll(jnp.broadcast_to(piece, (8, 128)), 64, 1)[0:1, :]
            for half, values in enumerate((rolled, piece)):
                row = 32 * a + 16 * half
                old = stage[row : row + 1, 0:128]
                stage[row : row + 1, 0:128] = jnp.where(lane < 64, old, values)
        core = me & 1
        for half in range(16):
            r = (me ^ (2 * half)) >> 1
            place = ((r & 3) << 2) | (r >> 2)
            kept = pl.multiple_of(32 * half + core * 16, 16)
            sent = pl.multiple_of(32 * half + (1 - core) * 16, 16)
            keep[place, :, 2048:2176] = stage[pl.ds(kept, 16), 0:128]
            send[place, :, 2048:2176] = stage[pl.ds(sent, 16), 0:128].astype(BF)


def backward(me, qkv_rows, do, ot, lse, weight, *rest):
    rows = do.shape[0]
    parts = [pl.BlockSpec((1, 1, rows, 128), lambda i, part=part: (i, part, 0, 0)) for part in range(3)]
    return pl.pallas_call(
        backward_kernel,
        grid=(4,),
        in_specs=[smem()]
        + parts
        + [
            pl.BlockSpec((rows, 128), lambda i: (0, i)),
            pl.BlockSpec((128, rows), lambda i: (i, 0)),
            pl.BlockSpec((1, 2, rows), lambda i: (i, 0, 0)),
            pl.BlockSpec((512, 384), lambda i: (0, i)),
        ]
        + [vmem()] * 7,
        out_specs=[vmem()] * 3,
        out_shape=[
            shape((rows, 1536), BF),
            shape((16, 16, 2176), BF),
            shape((16, 16, 2176), F32),
        ],
        scratch_shapes=[
            pltpu.VMEM((2, 256, rows), BF),
            pltpu.VMEM((2, 256, rows), BF),
            pltpu.VMEM((128, rows), F32),
            pltpu.VMEM((rows, 128), F32),
            pltpu.VMEM((rows, 128), F32),
            pltpu.VMEM((rows, 384), BF),
            pltpu.VMEM((528, 384), F32),
            pltpu.VMEM((8, 1536), F32),
            pltpu.VMEM((512, 128), F32),
            pltpu.VMEM((128, 512), F32),
        ],
        compiler_params=pltpu.CompilerParams(vmem_limit_bytes=20 * MIB),
        cost_estimate=cost(25),
        name="attend_back",
    )(me, qkv_rows, qkv_rows, qkv_rows, do, ot, lse, weight, *rest)


def input_kernel(
    tokens, gm, weight, smalls, grad_middle, act, down, middle, input_grad, output
):
    block = 256

    def behind(index, carry):
        span = pl.ds(pl.multiple_of(index * block, block), block)
        centred, scale = row_stats(tokens[span, :].astype(F32))
        xh = centred * scale
        total = middle[span, :] + dot(act[span, :], down[...]) + smalls[7:8, :]
        output[span, :] = total.astype(BF)
        hg = dot(gm[span, :], weight[...], NT) * smalls[0:1, :]
        input_grad[span, :] = grad_middle[span, :] + scale * (
            hg
            - jnp.mean(hg, axis=-1, keepdims=True)
            - xh * jnp.mean(hg * xh, axis=-1, keepdims=True)
        )
        return carry

    lax.fori_loop(0, tokens.shape[0] // block, behind, 0)


def input_terms(operands):
    rows = operands[0].shape[0]
    return pl.pallas_call(
        input_kernel,
        in_specs=[vmem()] * 8,
        out_specs=[vmem()] * 2,
        out_shape=[shape((rows, 512), F32), shape((rows, 512), BF)],
        compiler_params=pltpu.CompilerParams(vmem_limit_bytes=12 * MIB),
        cost_estimate=cost(8),
        name="input_terms",
    )(*operands)


def combine_kernel(counts, pieces, *refs):
    total_in = sum(counts) + len(counts)
    outs = refs[total_in:]
    position = 0
    base = 0
    for count in counts:
        own, incoming = refs[position], refs[position + 1 : position + 1 + count]
        position += 1 + count
        width = own.shape[2]
        rows = own.shape[0] // pieces
        for index in range(pieces):
            span = slice(rows * index, rows * index + rows)
            total = own[span]
            for ref in incoming:
                total = total + ref[span].astype(F32)
            outs[index][:, :, base : base + width] = total.astype(outs[index].dtype)
        base += width


def combine(name, pieces, *sums):
    slot_count = sums[0][0].shape[0] // pieces
    width = sum(own.shape[2] for own, _ in sums)
    operands = [part for own, received in sums for part in (own, *received)]
    dims = (slot_count, 16, width)
    first, *rest = pl.pallas_call(
        functools.partial(combine_kernel, [len(received) for _, received in sums], pieces),
        in_specs=[vmem()] * len(operands),
        out_specs=[vmem()] * pieces,
        out_shape=[shape(dims, F32)] + [shape(dims, BF)] * (pieces - 1),
        compiler_params=pltpu.CompilerParams(vmem_limit_bytes=8 * MIB),
        cost_estimate=cost(1.5),
        name=name,
    )(*operands)
    return first, rest


def last_kernel(g_own, g0, g1, g2, du_own, du_recv, own, du_first, p0, p1, p2):
    width = g_own.shape[2]
    for index in range(4):
        total = g_own[index]
        for ref in (g0, g1, g2):
            total = total + ref[index].astype(F32)
        if index == 0:
            own[0] = total
        else:
            (p0, p1, p2)[index - 1][0, :, 0:width] = total.astype(BF)
    du_first[0] = du_own[0] + du_recv[0].astype(F32)
    p0[0, :, width:] = (du_own[1] + du_recv[1].astype(F32)).astype(BF)


def last_sums(g_own, g_recv, du_own, du_recv):
    width, wide = g_own.shape[2], du_own.shape[2]
    own, du_first, *parts = pl.pallas_call(
        last_kernel,
        in_specs=[vmem()] * 6,
        out_specs=[vmem()] * 5,
        out_shape=[shape((1, 16, width), F32), shape((1, 16, wide), F32)]
        + [shape((1, 16, width + wide), BF)]
        + [shape((1, 16, width), BF)] * 2,
        compiler_params=pltpu.CompilerParams(vmem_limit_bytes=8 * MIB),
        cost_estimate=cost(1.5),
        name="last_sums",
    )(g_own, *g_recv, du_own, du_recv)
    return own, du_first, parts


def finish_kernel(
    own, r0, r1, r2, du_own,
    qkv_grad, mix_grad, up_grad, down_grad, gain, shift, qv, proj, bias,
):
    total = own[0] + r0[0, :, 0:2176].astype(F32)
    for ref in (r1, r2):
        total = total + ref[0].astype(F32)
    mix_grad[...] = total[:, 1536:2048]
    for pair in range(4):
        for part in range(3):
            base = 384 * pair + 128 * part
            column = 512 * part + 128 * pair
            qkv_grad[:, column : column + 128] = total[:, base : base + 128]
    tile = total[:, 2048:2176]
    wide = jnp.concatenate([tile, jnp.zeros((112, 128), F32)], axis=0).T
    for index, ref in enumerate((gain, shift, qv, proj)):
        ref[...] = wide[2 * index : 2 * index + 2, 0:16]
    bias[...] = tile[0:1, 64:128]
    total = du_own[0] + r0[0, :, 2176:].astype(F32)
    for part in range(4):
        down_grad[16 * part : 16 * part + 16, :] = total[:, 512 * part : 512 * part + 512]
    up_grad[...] = total[:, 2048:4096]


def finish(own, received, du_own):
    return pl.pallas_call(
        finish_kernel,
        in_specs=[vmem()] * 5,
        out_specs=[vmem()] * 9,
        out_shape=[
            shape((16, 1536), F32),
            shape((16, 512), F32),
            shape((16, 2048), F32),
            shape((64, 512), F32),
        ]
        + [shape((2, 16), F32)] * 4
        + [shape((1, 64), F32)],
        compiler_params=pltpu.CompilerParams(vmem_limit_bytes=6 * MIB),
        cost_estimate=cost(1.5),
        name="finish",
    )(own, *received, du_own)


def swap(value, mask, count):
    return lax.ppermute(value, AXES, [(d, d ^ mask) for d in range(count)])


Z_MASKS = (8, 16, 24)
PLANE_MASKS = (2, 4, 6)


def swaps(value, masks, count):
    return [swap(value, mask, count) for mask in masks]


def point(values, *tokens):
    return lax.optimization_barrier((values, tokens))[0]


def after(value, *tokens):
    return lax.optimization_barrier((value, tokens))[0]


def exchange(parts, masks, count):
    return [swap(part, mask, count) for part, mask in zip(parts, masks, strict=True)]


def group(own, others):
    joined = jnp.stack([own] + others)
    return joined.reshape((-1,) + joined.shape[-2:])


def pack_whole(qkv, mix, up, down, gain, shift, qv, proj, up_bias):
    pieces = []
    for pair in range(4):
        for part in range(3):
            base = 512 * part + 128 * pair
            pieces.append(qkv[:, base : base + 128])
    rows = jnp.concatenate([gain, shift, qv, proj], axis=0)
    tile = jnp.pad(rows.T, ((0, 0), (0, 120))).reshape(32, 16, 128)
    tile = tile.at[:, 0, 64:128].set(up_bias.reshape(32, 64))
    a0 = jnp.concatenate([jnp.concatenate(pieces, 1).reshape(32, 16, 1536), tile], axis=2)
    b0 = jnp.concatenate([mix, up], axis=1).reshape(32, 16, 2560)
    b1 = down.reshape(32, 4, 16, 512).swapaxes(1, 2).reshape(32, 16, 2048)
    return a0, b0, b1


def relative_halves(blocks):
    parts = blocks.reshape((4, 4, 2) + blocks.shape[1:])
    parts = parts.transpose((2, 1, 0) + tuple(range(3, parts.ndim)))
    return parts[0].reshape((16,) + blocks.shape[1:]), parts[1].reshape((16,) + blocks.shape[1:])


def whole_blocks(send, keep):
    parts = jnp.stack([keep, send.astype(F32)]).reshape((2, 4, 4) + keep.shape[1:])
    parts = parts.transpose((2, 1, 0) + tuple(range(3, parts.ndim)))
    return parts.reshape((32,) + keep.shape[1:])


def body(cubic, count, tokens, chain_ids, qkv, mix, up, down, gain, shift, qv, proj, up_bias, cot):
    params = (qkv, mix, up, down, gain, shift, qv, proj, up_bias)
    if cubic:
        index = lax.axis_index(AXES).astype(jnp.int32)
        me = jnp.stack([index, index & ~6])
        own, c_own = pack(*params)
        recv = swaps(own, Z_MASKS, count)
        c_recv = swaps(c_own, PLANE_MASKS, count)
        recv = point(recv)
        a_col = jnp.stack([part[:, :1664] for part in (own, *recv)])
        c_plane = group(c_own, after(c_recv, a_col))
        c_recv = swap(c_plane, 16, count)
        a_mine = lax.all_gather(after(a_col, c_plane), "plane").reshape(16, 16, -1)
        a_mine, c_recv = point((a_mine, c_recv))
        a_other = swap(a_mine, 1, count)
        own, *recv = after((own, *recv), a_mine)
        b_col = jnp.stack([part[:, 1664:] for part in (own, *recv)])
        b_recv = swaps(b_col, PLANE_MASKS, count)
        c_half = group(c_plane, [c_recv])
        c_recv = swap(c_half, 8, count)
        a_mine, a_other = after((a_mine, a_other), b_col, c_half)
    else:
        me = jnp.zeros((2,), jnp.int32)
        dims = (0, 0, 0, 0, 1, 1, 1, 1, 0)
        whole = [
            lax.all_gather(value, AXES, axis=dim, tiled=True)
            for value, dim in zip(params, dims, strict=True)
        ]
        a_parts, b_parts, c_parts = pack_whole(*whole)
        a_mine, a_other = relative_halves(a_parts)
        b_pair = relative_halves(b_parts)
        c_pair = [
            half.reshape(4, 2, 2, 16, 2048).transpose(2, 1, 0, 3, 4).reshape(16, 16, 2048)
            for half in relative_halves(c_parts)
        ]
    (
        qkv_rows, normed_t, weight, o, ot, lse, smalls, up_row, key_aux, query_aux,
    ) = forward(me, tokens, chain_ids, a_mine, a_other)
    if cubic:
        b_recv, c_recv, lse = point((b_recv, c_recv, lse))
        b_mine = group(b_col, b_recv)
        c_mine = group(c_half, [c_recv])
        b_pair = (b_mine, swap(b_mine, 1, count))
        c_pair = (c_mine, swap(c_mine, 1, count))
    (
        middle, normed_two_t, grad_pre, d_send, d_keep, mix_whole, up_whole, act_rows, down_whole,
    ) = feed_first(me, tokens, o, b_pair, c_pair, smalls, up_row, cot)
    if cubic:
        d_recv = swap(d_send, 1, count)
    u_send, u_keep, up_bias_grad = feed_second(me, normed_two_t, grad_pre)
    if cubic:
        u_recv = swap(u_send, 1, count)
    grad_middle, grad_att, mix_term, small_grads = feed_third(
        middle, grad_pre, mix_whole, up_whole, smalls, cot, ot
    )
    if cubic:
        d_recv, u_recv, small_grads = point((d_recv, u_recv, small_grads))
        du_own, du_parts = combine("feed_sum", 4, (d_keep, [d_recv]), (u_keep, [u_recv]))
        du_recv = exchange(du_parts, PLANE_MASKS, count)
        lse = after(lse, du_own)
    gm, g_send, g_keep = backward(
        me, qkv_rows, grad_att, ot, lse, weight, key_aux, query_aux, normed_t, smalls, small_grads,
        up_bias_grad, mix_term,
    )
    if cubic:
        du_recv, g_send, gm = point((du_recv, g_send, gm))
        g_recv = swap(g_send, 1, count)
        du_own, du_parts = combine("feed_sum_two", 2, (du_own, du_recv))
        du_recv = exchange(du_parts, (16,), count)
        g_own, g_parts = combine("last_sum", 4, (g_keep, [after(g_recv, du_own)]))
        g_recv = exchange(g_parts, PLANE_MASKS, count)
        smalls = after(smalls, g_own)
    input_grad, output = input_terms(
        [tokens, gm, weight, smalls, grad_middle, act_rows, down_whole, middle]
    )
    if cubic:
        g_recv, du_recv, input_grad = point((g_recv, du_recv, input_grad))
        own, du_own, parts = last_sums(g_own, g_recv, du_own, *du_recv)
        g_recv = exchange(parts, Z_MASKS, count)
        qkv_grad, mix_grad, up_grad, down_grad, *vectors, bias_grad = finish(own, g_recv, du_own)
        return (
            output, input_grad, qkv_grad, mix_grad, up_grad, down_grad, *vectors,
            bias_grad.reshape(64),
        )
    pairs = ((d_send, d_keep), (u_send, u_keep), (g_send, g_keep))
    blocks = [whole_blocks(s, r) for s, r in pairs]
    tiles = blocks[2][:, :, 2048:2176]
    joined = blocks[2].reshape(512, 2176)
    wholes = (
        blocks[0].reshape(32, 16, 4, 512).swapaxes(1, 2).reshape(2048, 512),
        blocks[1].reshape(512, 2048),
        joined[:, 1536:2048],
        joined[:, :1536].reshape(512, 4, 3, 128).swapaxes(1, 2).reshape(512, 1536),
        tiles[:, 0, 64:128].reshape(2048),
    )
    down_grad, up_grad, mix_grad, qkv_grad, bias_grad = [
        lax.psum_scatter(value, AXES, scatter_dimension=0, tiled=True) for value in wholes
    ]
    vectors = lax.psum_scatter(
        tiles[:, :, 0:8].reshape(512, 8).T, AXES, scatter_dimension=1, tiled=True
    )
    return (
        output, input_grad, qkv_grad, mix_grad, up_grad, down_grad,
        vectors[0:2], vectors[2:4], vectors[4:6], vectors[6:8], bias_grad,
    )


def solution(mesh):
    groups = mesh.shape["dp"]
    count = groups * mesh.shape["fsdp"]
    inner = jax.sharding.Mesh(mesh.devices.reshape(groups, -1, 2), AXES)
    cubic = inner.devices.shape == (4, 4, 2)

    def entry(*operands):
        return body(cubic, count, *operands)

    rows = P(AXES, None)
    columns = P(None, AXES)
    flat = P(AXES)
    return jax.shard_map(
        entry,
        mesh=inner,
        in_specs=(rows,) * 6 + (columns,) * 4 + (flat, rows),
        out_specs=(rows,) * 6 + (columns,) * 4 + (flat,),
        check_vma=False,
    )
```

```python
import functools
import math

import jax
import jax.numpy as jnp
from jax import lax
from jax.experimental import pallas as pl
from jax.experimental.pallas import tpu as pltpu
from jax.sharding import PartitionSpec as P

AXES = ("dp", "plane", "core")
HEADS = 8
EPS = 1e-05
SCALE = 0.125
EXP_SCALE = SCALE * math.log2(math.e)
HIDE = -(2.0**60)
MIB = 2**20

BF = jnp.bfloat16
F32 = jnp.float32
NN = (((1,), (0,)), ((), ()))
NT = (((1,), (1,)), ((), ()))
TN = (((0,), (0,)), ((), ()))


def dot(a, b, dims=NN):
    return lax.dot_general(a, b, dims, preferred_element_type=F32)


def vmem():
    return pl.BlockSpec(memory_space=pltpu.VMEM)


def smem():
    return pl.BlockSpec(memory_space=pltpu.SMEM)


def shape(dims, dtype):
    return jax.ShapeDtypeStruct(dims, dtype)


def block_of(index, block):
    return pl.ds(pl.multiple_of(index * block, block), block)


def cost(us):
    return pl.CostEstimate(flops=int(us * 1.1e9), bytes_accessed=0, transcendentals=0)


TALL_ORDER = (0, 2, 1, 3)


def slots():
    return [(c, j, i) for c in range(2) for j in range(4) for i in range(4)]


def block_row(me, c, j, i, rows):
    return pl.multiple_of((me ^ (c | (j << 1) | (i << 3))) * rows, rows)


def row_stats(rows_in):
    mean = jnp.mean(rows_in, axis=-1, keepdims=True)
    centred = rows_in - mean
    spread = jnp.mean(centred * centred, axis=-1, keepdims=True)
    return centred, lax.rsqrt(spread + EPS)


def split_three(row):
    first = row.astype(BF).astype(F32)
    rest = row - first
    second = rest.astype(BF).astype(F32)
    return first, second, rest - second


def pack_kernel(qkv, mix, up, down, gain, shift, qv, proj, up_bias, a0, c0, rows128):
    for pair in range(4):
        for part in range(3):
            base = 384 * pair + 128 * part
            a0[:, base : base + 128] = qkv[:, 512 * part + 128 * pair : 512 * part + 128 * pair + 128]
    rows128[...] = jnp.zeros_like(rows128)
    for index, ref in enumerate((gain, shift, qv, proj)):
        rows128[2 * index : 2 * index + 2, :] = ref[...].astype(F32)
    eye = (
        lax.broadcasted_iota(jnp.int32, (16, 16), 0) == lax.broadcasted_iota(jnp.int32, (16, 16), 1)
    ).astype(F32)
    columns = dot(eye.astype(BF), rows128[...].astype(BF), NT)
    bias = jnp.concatenate([jnp.zeros((1, 64), F32), up_bias[...].astype(F32)], axis=1)
    row = lax.broadcasted_iota(jnp.int32, (16, 128), 0)
    lane = lax.broadcasted_iota(jnp.int32, (16, 128), 1)
    a0[:, 1536:1664] = jnp.where((row == 0) & (lane >= 64), bias, columns).astype(BF)
    a0[:, 1664:2176] = mix[...]
    a0[:, 2176:4224] = up[...]
    for part in range(4):
        c0[:, 512 * part : 512 * part + 512] = down[16 * part : 16 * part + 16, :]


def pack(qkv, mix, up, down, gain, shift, qv, proj, up_bias):
    return pl.pallas_call(
        pack_kernel,
        in_specs=[vmem()] * 9,
        out_specs=[vmem()] * 2,
        out_shape=[shape((16, 4224), BF), shape((16, 2048), BF)],
        scratch_shapes=[pltpu.VMEM((128, 16), F32)],
        cost_estimate=cost(1.5),
        name="pack",
    )(qkv, mix, up, down, gain, shift, qv, proj, up_bias.reshape(1, 64))


def aux_rows(chain):
    row = lax.broadcasted_iota(jnp.int32, (128, chain.shape[1]), 0)
    low_bits = jnp.where(row < 7, (chain >> jnp.minimum(row, 6)) & 1, 0)
    high_bits = jnp.where(
        (row >= 7) & (row < 14), 1 - ((chain >> jnp.minimum(jnp.maximum(row - 7, 0), 6)) & 1), 0
    )
    bits = low_bits + high_bits
    query_side = bits.astype(F32) * HIDE
    key_side = jnp.where(row < 14, 1 - bits, jnp.where(row < 17, 1, 0)).astype(F32)
    return query_side.astype(BF), key_side.T.astype(BF)


def longest_pair(q2_t, k2):
    wide_q = q2_t.astype(F32)
    wide_k = k2.astype(F32)
    longest_q = jnp.max(jnp.sum(wide_q * wide_q, axis=0, keepdims=True))
    longest_k = jnp.max(jnp.sum(wide_k * wide_k, axis=1, keepdims=True))
    return longest_q * longest_k


def pair_forward(normed, weight, bias_q, bias_v, key_aux, qa, ot, outs, pair, block):
    qkv_out, o_out, ot_out, lse_out = outs
    rows = normed.shape[0]
    cols = block_of(pair, 128)
    q2 = (dot(normed, weight[:, 0:128]) + bias_q).astype(BF)
    k2 = dot(normed, weight[:, 128:256]).astype(BF)
    v2 = (dot(normed, weight[:, 256:384]) + bias_v).astype(BF)
    for index, value in enumerate((q2, k2, v2)):
        qkv_out[pair, index] = value
    qa[0:128, :] = q2.T
    vt = v2.T
    ones = (lax.broadcasted_iota(jnp.int32, (16, rows), 0) == 0).astype(F32).astype(BF)
    lane = lax.broadcasted_iota(jnp.int32, k2.shape, 1)
    zero = jnp.zeros_like(k2)
    keys = [
        jnp.concatenate([jnp.where((lane >= 64) == bool(h), k2, zero), key_aux], axis=1)
        for h in range(2)
    ]
    vts = [jnp.concatenate([vt[64 * h : 64 * h + 64], ones], axis=0) for h in range(2)]
    count = rows // block

    def score(index):
        q_cols = qa[:, block * index : block * index + block]
        return [dot(keys[h], q_cols) for h in range(2)]

    def attend(shifted):
        ahead = score(0)
        for index in range(count):
            scores = ahead
            if index + 1 < count:
                ahead = score(index + 1)
            span = slice(block * index, block * index + block)
            for h in range(2):
                if shifted:
                    peak = jnp.max(scores[h], axis=0, keepdims=True)
                    probs = jnp.exp2((scores[h] - peak) * EXP_SCALE).astype(BF)
                else:
                    peak = 0.0
                    probs = jnp.exp2(scores[h] * EXP_SCALE).astype(BF)
                mixed = dot(vts[h], probs)
                total = mixed[64:65]
                ot[64 * h : 64 * h + 64, span] = mixed[:64] * (1.0 / total)
                lse_out[pair, h : h + 1, span] = peak + jnp.log(total) * (1.0 / SCALE)

    bound = longest_pair(qa[0:128, :], k2) * (EXP_SCALE * EXP_SCALE)
    small = bound < 90.0 * 90.0

    @pl.when(small)
    def _():
        attend(False)

    @pl.when(jnp.logical_not(small))
    def _():
        attend(True)

    ot_out[cols, :] = ot[...].astype(BF)
    o_out[:, cols] = ot[...].T.astype(BF)


def forward_kernel(me_ref, tokens, chain, mine, other, *refs):
    qkv_hbm, normed_t_hbm, weight_hbm, o_out, ot_out, lse_out = refs[:6]
    smalls, up_row, key_aux_out, query_aux_out = refs[6:10]
    qa, ot, columns, qkv_out, normed_out, normed_t, weight, sems = refs[10:]
    me = me_ref[1]
    for c, j, i in slots():
        source = (mine, other)[c]
        row = block_row(me, c, j, i, 16)
        weight[pl.ds(row, 16), :] = source[4 * j + i, :, 0:1536]
        columns[pl.ds(row, 16), :] = source[4 * j + i, :, 1536:1664].astype(F32)
    smalls[...] = columns[...].T[0:8, :]
    lane = lax.broadcasted_iota(jnp.int32, (1, 128), 1)
    for a in range(16):
        even = pltpu.roll(columns[32 * a : 32 * a + 8, :], 64, 1)[0:1, :]
        odd = columns[32 * a + 16 : 32 * a + 17, :]
        up_row[:, 128 * a : 128 * a + 128] = jnp.where(lane < 64, even, odd)
    query_side, key_side = aux_rows(chain[...])
    qa[128:256, :] = query_side
    query_aux_out[...] = query_side
    key_aux_out[...] = key_side

    def norm_block(index, carry):
        span = pl.ds(pl.multiple_of(index * 256, 256), 256)
        centred, scale = row_stats(tokens[span, :].astype(F32))
        normed_out[span, :] = (centred * scale * smalls[0:1, :] + smalls[2:3, :]).astype(BF)
        return carry

    lax.fori_loop(0, tokens.shape[0] // 256, norm_block, 0)
    normed = normed_out[...]
    normed_t[0:512, :] = normed.T
    ones_row = lax.broadcasted_iota(jnp.int32, (16, normed.shape[0]), 0) == 0
    normed_t[512:528, :] = ones_row.astype(F32).astype(BF)
    copies = [
        pltpu.make_async_copy(normed_t, normed_t_hbm, sems.at[4]),
        pltpu.make_async_copy(weight, weight_hbm, sems.at[5]),
    ]
    for copy in copies:
        copy.start()
    outs = (qkv_out, o_out, ot_out, lse_out)

    def one_pair(pair, carry):
        cols = block_of(pair, 128)
        pair_forward(
            normed_out[...], weight[:, block_of(pair, 384)], smalls[4:5, cols], smalls[5:6, cols],
            key_aux_out[...], qa, ot, outs, pair, 512,
        )
        pltpu.make_async_copy(qkv_out.at[pair], qkv_hbm.at[pair], sems.at[pair]).start()
        return carry

    lax.fori_loop(0, 4, one_pair, 0)
    for pair in range(4):
        pltpu.make_async_copy(qkv_out.at[pair], qkv_hbm.at[pair], sems.at[pair]).wait()
    for copy in copies:
        copy.wait()


def hbm():
    return pl.BlockSpec(memory_space=pltpu.HBM)


def forward(me, tokens, chain, mine, other):
    rows = tokens.shape[0]
    return pl.pallas_call(
        forward_kernel,
        in_specs=[smem()] + [vmem()] * 4,
        out_specs=[hbm()] * 3 + [vmem()] * 7,
        out_shape=[
            shape((4, 3, rows, 128), BF),
            shape((528, rows), BF),
            shape((512, 1536), BF),
            shape((rows, 512), BF),
            shape((512, rows), BF),
            shape((4, 2, rows), F32),
            shape((8, 512), F32),
            shape((1, 2048), F32),
            shape((rows, 128), BF),
            shape((128, rows), BF),
        ],
        scratch_shapes=[
            pltpu.VMEM((256, rows), BF),
            pltpu.VMEM((128, rows), F32),
            pltpu.VMEM((512, 128), F32),
            pltpu.VMEM((4, 3, rows, 128), BF),
            pltpu.VMEM((rows, 512), BF),
            pltpu.VMEM((528, rows), BF),
            pltpu.VMEM((512, 1536), BF),
            pltpu.SemaphoreType.DMA((6,)),
        ],
        compiler_params=pltpu.CompilerParams(vmem_limit_bytes=20 * MIB),
        cost_estimate=cost(15),
        name="attend",
    )(me, tokens, chain, mine, other)


def gelu_parts(u):
    half_cdf = 0.5 + 0.5 * lax.erf(u * math.sqrt(0.5))
    density = jnp.exp2(u * u * (-0.5 * math.log2(math.e))) * (1.0 / math.sqrt(2.0 * math.pi))
    return u * half_cdf, half_cdf + u * density


def scatter_tall(me, source, base_block, send, keep):
    core = me & 1
    for half in range(4):
        r = (me ^ (base_block + 2 * half)) >> 1
        place = ((r & 3) << 2) | (r >> 2)
        for part in range(4):
            row = 128 * half + 16 * part
            span = slice(512 * part, 512 * part + 512)
            keep[place, :, span] = source[pl.ds(pl.multiple_of(row + core * 64, 16), 16), :]
            sent = source[pl.ds(pl.multiple_of(row + (1 - core) * 64, 16), 16), :]
            send[place, :, span] = sent.astype(BF)


def scatter_blocks(me, source, rows, base_block, blocks, send, keep, span):
    core = me & 1
    for half in range(blocks // 2):
        first = base_block + 2 * half
        row = 2 * half * rows
        r = (me ^ first) >> 1
        place = ((r & 3) << 2) | (r >> 2)
        kept = source[pl.ds(pl.multiple_of(row + core * rows, rows), rows), :]
        sent = source[pl.ds(pl.multiple_of(row + (1 - core) * rows, rows), rows), :]
        keep[place, :, span] = kept
        send[place, :, span] = sent.astype(BF)


def feed_first_kernel(
    me_ref, tokens, o_in, mine, other, mine_tall, other_tall, smalls, up_row, cot,
    middle, normed_t, grad_pre_out, d_send, d_keep, mix, up, act_rows, down,
    normed, stage,
):
    me = me_ref[0]
    for c, j, i in slots():
        source = (mine, other)[c]
        row = block_row(me, c, j, i, 16)
        mix[pl.ds(row, 16), :] = source[4 * j + i, :, 0:512]
        up[pl.ds(row, 16), :] = source[4 * j + i, :, 512:2560]
        source = (mine_tall, other_tall)[c]
        for part in range(4):
            row = pl.multiple_of(block_row(me, c, j, i, 64) + 16 * part, 16)
            span = slice(512 * part, 512 * part + 512)
            down[pl.ds(row, 16), :] = source[4 * TALL_ORDER[i] + j, :, span]
    rows = tokens.shape[0]
    block = 256

    def ahead(index, carry):
        span = pl.ds(pl.multiple_of(index * block, block), block)
        mid = tokens[span, :].astype(F32) + dot(o_in[span, :], mix[...]) + smalls[6:7, :]
        middle[span, :] = mid
        centred, scale = row_stats(mid)
        normed[span, :] = (centred * scale * smalls[1:2, :] + smalls[3:4, :]).astype(BF)
        return carry

    lax.fori_loop(0, rows // block, ahead, 0)
    normed_t[0:512, :] = normed[...].T
    ones_row = lax.broadcasted_iota(jnp.int32, (16, rows), 0) == 0
    normed_t[512:528, :] = ones_row.astype(F32).astype(BF)
    width = 512

    def one_chunk(chunk, carry):
        span = block_of(chunk, width)
        down_part = down[span, :]
        act, slope = gelu_parts(dot(normed[...], up[:, span]) + up_row[:, span])
        act_low = act.astype(BF)
        grad_pre_out[:, span] = (dot(cot[...], down_part, NT) * slope).astype(BF)
        act_rows[:, span] = act_low
        stage[...] = dot(act_low, cot[...], TN)
        scatter_tall(me, stage, chunk * (width // 64), d_send, d_keep)
        return carry

    lax.fori_loop(0, 2048 // width, one_chunk, 0)


def feed_first(me, tokens, o_in, b_pair, c_pair, smalls, up_row, cot):
    rows = tokens.shape[0]
    return pl.pallas_call(
        feed_first_kernel,
        in_specs=[smem()] + [vmem()] * 9,
        out_specs=[vmem()] * 9,
        out_shape=[
            shape((rows, 512), F32),
            shape((528, rows), BF),
            shape((rows, 2048), BF),
            shape((16, 16, 2048), BF),
            shape((16, 16, 2048), F32),
            shape((512, 512), BF),
            shape((512, 2048), BF),
            shape((rows, 2048), BF),
            shape((2048, 512), BF),
        ],
        scratch_shapes=[
            pltpu.VMEM((rows, 512), BF),
            pltpu.VMEM((512, 512), F32),
        ],
        compiler_params=pltpu.CompilerParams(vmem_limit_bytes=14 * MIB),
        cost_estimate=cost(18),
        name="feed_first",
    )(me, tokens, o_in, *b_pair, *c_pair, smalls, up_row, cot)


def feed_second_kernel(me_ref, normed_t, grad_pre, u_send, u_keep, up_bias_grad, stage):
    me = me_ref[0]
    width = 512

    def one_chunk(chunk, carry):
        span = block_of(chunk, width)
        stage[...] = dot(normed_t[...], grad_pre[:, span])
        up_bias_grad[:, span] = stage[512:513, :]
        scatter_blocks(me, stage, 16, 0, 32, u_send, u_keep, span)
        return carry

    lax.fori_loop(0, 2048 // width, one_chunk, 0)


def feed_second(me, normed_t, grad_pre):
    return pl.pallas_call(
        feed_second_kernel,
        in_specs=[smem()] + [vmem()] * 2,
        out_specs=[vmem()] * 3,
        out_shape=[
            shape((16, 16, 2048), BF),
            shape((16, 16, 2048), F32),
            shape((1, 2048), F32),
        ],
        scratch_shapes=[pltpu.VMEM((528, 512), F32)],
        compiler_params=pltpu.CompilerParams(vmem_limit_bytes=10 * MIB),
        cost_estimate=cost(5),
        name="feed_second",
    )(me, normed_t, grad_pre)


def feed_third_kernel(
    middle, grad_pre, mix, up, smalls, cot, ot_in,
    grad_middle, grad_att, mix_grad, small_grads, low_rows,
):
    rows = middle.shape[0]
    block = 256

    def behind(index, carry):
        gain_sum, shift_sum, branch_sum, cot_sum = carry
        span = pl.ds(pl.multiple_of(index * block, block), block)
        centred, scale = row_stats(middle[span, :])
        xh = centred * scale
        h = dot(grad_pre[span, :], up[...], NT)
        hg = h * smalls[1:2, :]
        cot_rows = cot[span, :].astype(F32)
        grad = cot_rows + scale * (
            hg
            - jnp.mean(hg, axis=-1, keepdims=True)
            - xh * jnp.mean(hg * xh, axis=-1, keepdims=True)
        )
        grad_middle[span, :] = grad
        low = grad.astype(BF)
        low_rows[span, :] = low
        grad_att[span, :] = dot(low, mix[...], NT).astype(BF)
        return (
            gain_sum + jnp.sum(h * xh, axis=0, keepdims=True),
            shift_sum + jnp.sum(h, axis=0, keepdims=True),
            branch_sum + jnp.sum(low.astype(F32), axis=0, keepdims=True),
            cot_sum + jnp.sum(cot_rows, axis=0, keepdims=True),
        )

    zero = jnp.zeros((1, 512), F32)
    sums = lax.fori_loop(0, rows // block, behind, (zero, zero, zero, zero))
    for index in range(4):
        small_grads[index : index + 1, :] = sums[index]
    small_grads[4:8, :] = jnp.zeros((4, 512), F32)
    mix_grad[0:256, :] = dot(ot_in[0:256, :], low_rows[...])
    mix_grad[256:512, :] = dot(ot_in[256:512, :], low_rows[...])


def feed_third(middle, grad_pre, mix, up, smalls, cot, ot_in):
    rows = middle.shape[0]
    return pl.pallas_call(
        feed_third_kernel,
        in_specs=[vmem()] * 7,
        out_specs=[vmem()] * 4,
        out_shape=[
            shape((rows, 512), F32),
            shape((rows, 512), BF),
            shape((512, 512), F32),
            shape((8, 512), F32),
        ],
        scratch_shapes=[pltpu.VMEM((rows, 512), BF)],
        compiler_params=pltpu.CompilerParams(vmem_limit_bytes=12 * MIB),
        cost_estimate=cost(8),
        name="feed_third",
    )(middle, grad_pre, mix, up, smalls, cot, ot_in)


def pair_backward(q, k, v, do, ot_in, lse, key_aux, qa, da, dqt, acc_k, acc_v, gm, block):
    k2 = k[0, 0]
    v2 = v[0, 0]
    rows = k2.shape[0]
    kt = k2.T
    lane = lax.broadcasted_iota(jnp.int32, k2.shape, 1)
    zero = jnp.zeros_like(k2)
    keys = []
    vals = []
    for h in range(2):
        own = (lane >= 64) == bool(h)
        keys.append(jnp.concatenate([jnp.where(own, k2, zero), key_aux], axis=1))
        vals.append(jnp.concatenate([jnp.where(own, v2, zero), key_aux], axis=1))
    qt = q[0, 0].T
    dt = do[...].T
    product = dt.astype(F32) * ot_in[...].astype(F32)
    row = lax.broadcasted_iota(jnp.int32, (16, rows), 0)
    for h in range(2):
        qa[h, 0:128, :] = qt
        da[h, 0:128, :] = dt
        delta = jnp.sum(product[64 * h : 64 * h + 64], axis=0, keepdims=True)
        base = qa[h, 128:144, :].astype(F32)
        one, two, three = split_three(-lse[0, h : h + 1, :])
        base = jnp.where(row == 14, one, jnp.where(row == 15, two, base))
        qa[h, 128:144, :] = base.astype(BF)
        qa[h, 144:160, :] = jnp.where(row == 0, three, 0.0).astype(BF)
        one, two, three = split_three(-delta)
        base = jnp.where(row == 14, one, jnp.where(row == 15, two, 0.0))
        da[h, 128:144, :] = base.astype(BF)
        da[h, 144:160, :] = jnp.where(row == 0, three, 0.0).astype(BF)
    small_lane = lax.broadcasted_iota(jnp.int32, (block, 128), 1)
    for index in range(rows // block):
        span = slice(block * index, block * index + block)
        do_rows = do[span, :]
        q_rows = q[0, 0, span, :]
        blank = jnp.zeros_like(do_rows)
        sum_k = None
        sum_v = None
        for h in range(2):
            own = (small_lane >= 64) == bool(h)
            probs = jnp.exp2(dot(keys[h], qa[h, :, span]) * EXP_SCALE)
            grad = (probs * dot(vals[h], da[h, :, span])).astype(BF)
            probs = probs.astype(BF)
            dqt[64 * h : 64 * h + 64, span] = dot(kt[64 * h : 64 * h + 64, :], grad)
            part_k = dot(grad, jnp.where(own, q_rows, blank))
            part_v = dot(probs, jnp.where(own, do_rows, blank))
            sum_k = part_k if sum_k is None else sum_k + part_k
            sum_v = part_v if sum_v is None else sum_v + part_v
        if index == 0:
            acc_k[...] = sum_k
            acc_v[...] = sum_v
        else:
            acc_k[...] += sum_k
            acc_v[...] += sum_v
    gm[:, 0:128] = (dqt[...].T * SCALE).astype(BF)
    gm[:, 128:256] = (acc_k[...] * SCALE).astype(BF)
    gm[:, 256:384] = acc_v[...].astype(BF)


def backward_kernel(
    me_ref, q, k, v, do, ot_in, lse, weight, key_aux, query_aux, normed_t, smalls, small_grads,
    up_bias_grad, mix_term, gm, send, keep,
    qa, da, dqt, acc_k, acc_v, gm_pair, stage, sums, vectors, columns,
):
    me = me_ref[0]
    pair = pl.program_id(0)

    @pl.when(pair == 0)
    def _():
        for h in range(2):
            qa[h, 128:256, :] = query_aux[...]
            da[h, 128:256, :] = jnp.zeros((128, da.shape[2]), BF)
        vectors[...] = jnp.zeros_like(vectors)
        scatter_blocks(me, mix_term, 16, 0, 32, send, keep, slice(1536, 2048))

    pair_backward(q, k, v, do, ot_in, lse, key_aux[...], qa, da, dqt, acc_k, acc_v, gm_pair, 512)
    span = block_of(pair, 384)
    gm[:, span] = gm_pair[...]
    stage[...] = dot(normed_t[...], gm_pair[...])
    total = stage[512:513, :]
    sums[:, span] = jnp.broadcast_to(total, (8, 384))
    scatter_blocks(me, stage, 16, 0, 32, send, keep, span)
    wide = weight[...].astype(F32)
    for index, product in enumerate((stage[0:512, :] * wide, wide * total)):
        vectors[index] += product[:, 0:128] + product[:, 128:256] + product[:, 256:384]

    @pl.when(pair == 3)
    def _():
        columns[...] = jnp.zeros_like(columns)
        columns[1:2, :] = small_grads[0:1, :]
        columns[3:4, :] = small_grads[1:2, :]
        for index in range(4):
            cols = slice(128 * index, 128 * index + 128)
            columns[4:5, cols] = sums[0:1, 384 * index : 384 * index + 128]
            columns[5:6, cols] = sums[0:1, 384 * index + 256 : 384 * index + 384]
        columns[6:7, :] = small_grads[2:3, :]
        columns[7:8, :] = small_grads[3:4, :]
        columns[8:9, :] = smalls[0:1, :]
        columns[9:10, :] = smalls[2:3, :]
        tile = columns[...].T
        plain = jnp.sum(vectors[1], axis=1, keepdims=True)
        weighted = jnp.sum(vectors[0], axis=1, keepdims=True)
        gain_sum = (weighted - tile[:, 9:10] * plain) / tile[:, 8:9]
        lanes = lax.broadcasted_iota(jnp.int32, (512, 128), 1)
        stage[0:512, 0:128] = jnp.where(lanes == 0, gain_sum, jnp.where(lanes == 2, plain, tile))
        lane = lax.broadcasted_iota(jnp.int32, (1, 128), 1)
        for a in range(16):
            piece = up_bias_grad[:, 128 * a : 128 * a + 128]
            rolled = pltpu.roll(jnp.broadcast_to(piece, (8, 128)), 64, 1)[0:1, :]
            for half, values in enumerate((rolled, piece)):
                row = 32 * a + 16 * half
                old = stage[row : row + 1, 0:128]
                stage[row : row + 1, 0:128] = jnp.where(lane < 64, old, values)
        core = me & 1
        for half in range(16):
            r = (me ^ (2 * half)) >> 1
            place = ((r & 3) << 2) | (r >> 2)
            kept = pl.multiple_of(32 * half + core * 16, 16)
            sent = pl.multiple_of(32 * half + (1 - core) * 16, 16)
            keep[place, :, 2048:2176] = stage[pl.ds(kept, 16), 0:128]
            send[place, :, 2048:2176] = stage[pl.ds(sent, 16), 0:128].astype(BF)


def backward(me, qkv_rows, do, ot, lse, weight, *rest):
    rows = do.shape[0]
    parts = [pl.BlockSpec((1, 1, rows, 128), lambda i, part=part: (i, part, 0, 0)) for part in range(3)]
    return pl.pallas_call(
        backward_kernel,
        grid=(4,),
        in_specs=[smem()]
        + parts
        + [
            pl.BlockSpec((rows, 128), lambda i: (0, i)),
            pl.BlockSpec((128, rows), lambda i: (i, 0)),
            pl.BlockSpec((1, 2, rows), lambda i: (i, 0, 0)),
            pl.BlockSpec((512, 384), lambda i: (0, i)),
        ]
        + [vmem()] * 7,
        out_specs=[vmem()] * 3,
        out_shape=[
            shape((rows, 1536), BF),
            shape((16, 16, 2176), BF),
            shape((16, 16, 2176), F32),
        ],
        scratch_shapes=[
            pltpu.VMEM((2, 256, rows), BF),
            pltpu.VMEM((2, 256, rows), BF),
            pltpu.VMEM((128, rows), F32),
            pltpu.VMEM((rows, 128), F32),
            pltpu.VMEM((rows, 128), F32),
            pltpu.VMEM((rows, 384), BF),
            pltpu.VMEM((528, 384), F32),
            pltpu.VMEM((8, 1536), F32),
            pltpu.VMEM((2, 512, 128), F32),
            pltpu.VMEM((128, 512), F32),
        ],
        compiler_params=pltpu.CompilerParams(vmem_limit_bytes=20 * MIB),
        cost_estimate=cost(25),
        name="attend_back",
    )(me, qkv_rows, qkv_rows, qkv_rows, do, ot, lse, weight, *rest)


def input_kernel(
    tokens, gm, weight, smalls, grad_middle, act, down, middle, input_grad, output
):
    block = 256

    def behind(index, carry):
        span = pl.ds(pl.multiple_of(index * block, block), block)
        centred, scale = row_stats(tokens[span, :].astype(F32))
        xh = centred * scale
        total = middle[span, :] + dot(act[span, :], down[...]) + smalls[7:8, :]
        output[span, :] = total.astype(BF)
        hg = dot(gm[span, :], weight[...], NT) * smalls[0:1, :]
        input_grad[span, :] = grad_middle[span, :] + scale * (
            hg
            - jnp.mean(hg, axis=-1, keepdims=True)
            - xh * jnp.mean(hg * xh, axis=-1, keepdims=True)
        )
        return carry

    lax.fori_loop(0, tokens.shape[0] // block, behind, 0)


def input_terms(operands):
    rows = operands[0].shape[0]
    return pl.pallas_call(
        input_kernel,
        in_specs=[vmem()] * 8,
        out_specs=[vmem()] * 2,
        out_shape=[shape((rows, 512), F32), shape((rows, 512), BF)],
        compiler_params=pltpu.CompilerParams(vmem_limit_bytes=12 * MIB),
        cost_estimate=cost(8),
        name="input_terms",
    )(*operands)


def combine_kernel(counts, pieces, *refs):
    total_in = sum(counts) + len(counts)
    outs = refs[total_in:]
    position = 0
    base = 0
    for count in counts:
        own, incoming = refs[position], refs[position + 1 : position + 1 + count]
        position += 1 + count
        width = own.shape[2]
        rows = own.shape[0] // pieces
        for index in range(pieces):
            span = slice(rows * index, rows * index + rows)
            total = own[span]
            for ref in incoming:
                total = total + ref[span].astype(F32)
            outs[index][:, :, base : base + width] = total.astype(outs[index].dtype)
        base += width


def combine(name, pieces, *sums):
    slot_count = sums[0][0].shape[0] // pieces
    width = sum(own.shape[2] for own, _ in sums)
    operands = [part for own, received in sums for part in (own, *received)]
    dims = (slot_count, 16, width)
    first, *rest = pl.pallas_call(
        functools.partial(combine_kernel, [len(received) for _, received in sums], pieces),
        in_specs=[vmem()] * len(operands),
        out_specs=[vmem()] * pieces,
        out_shape=[shape(dims, F32)] + [shape(dims, BF)] * (pieces - 1),
        compiler_params=pltpu.CompilerParams(vmem_limit_bytes=8 * MIB),
        cost_estimate=cost(1.5),
        name=name,
    )(*operands)
    return first, rest


def last_kernel(g_own, g0, g1, g2, du_own, du_recv, own, du_first, p0, p1, p2):
    width = g_own.shape[2]
    for index in range(4):
        total = g_own[index]
        for ref in (g0, g1, g2):
            total = total + ref[index].astype(F32)
        if index == 0:
            own[0] = total
        else:
            (p0, p1, p2)[index - 1][0, :, 0:width] = total.astype(BF)
    du_first[0] = du_own[0] + du_recv[0].astype(F32)
    p0[0, :, width:] = (du_own[1] + du_recv[1].astype(F32)).astype(BF)


def last_sums(g_own, g_recv, du_own, du_recv):
    width, wide = g_own.shape[2], du_own.shape[2]
    own, du_first, *parts = pl.pallas_call(
        last_kernel,
        in_specs=[vmem()] * 6,
        out_specs=[vmem()] * 5,
        out_shape=[shape((1, 16, width), F32), shape((1, 16, wide), F32)]
        + [shape((1, 16, width + wide), BF)]
        + [shape((1, 16, width), BF)] * 2,
        compiler_params=pltpu.CompilerParams(vmem_limit_bytes=8 * MIB),
        cost_estimate=cost(1.5),
        name="last_sums",
    )(g_own, *g_recv, du_own, du_recv)
    return own, du_first, parts


def finish_kernel(
    own, r0, r1, r2, du_own,
    qkv_grad, mix_grad, up_grad, down_grad, gain, shift, qv, proj, bias,
):
    total = own[0] + r0[0, :, 0:2176].astype(F32)
    for ref in (r1, r2):
        total = total + ref[0].astype(F32)
    mix_grad[...] = total[:, 1536:2048]
    for pair in range(4):
        for part in range(3):
            base = 384 * pair + 128 * part
            column = 512 * part + 128 * pair
            qkv_grad[:, column : column + 128] = total[:, base : base + 128]
    tile = total[:, 2048:2176]
    wide = jnp.concatenate([tile, jnp.zeros((112, 128), F32)], axis=0).T
    for index, ref in enumerate((gain, shift, qv, proj)):
        ref[...] = wide[2 * index : 2 * index + 2, 0:16]
    bias[...] = tile[0:1, 64:128]
    total = du_own[0] + r0[0, :, 2176:].astype(F32)
    for part in range(4):
        down_grad[16 * part : 16 * part + 16, :] = total[:, 512 * part : 512 * part + 512]
    up_grad[...] = total[:, 2048:4096]


def finish(own, received, du_own):
    return pl.pallas_call(
        finish_kernel,
        in_specs=[vmem()] * 5,
        out_specs=[vmem()] * 9,
        out_shape=[
            shape((16, 1536), F32),
            shape((16, 512), F32),
            shape((16, 2048), F32),
            shape((64, 512), F32),
        ]
        + [shape((2, 16), F32)] * 4
        + [shape((1, 64), F32)],
        compiler_params=pltpu.CompilerParams(vmem_limit_bytes=6 * MIB),
        cost_estimate=cost(1.5),
        name="finish",
    )(own, *received, du_own)


def swap(value, mask, count):
    return lax.ppermute(value, AXES, [(d, d ^ mask) for d in range(count)])


Z_MASKS = (8, 16, 24)
PLANE_MASKS = (2, 4, 6)


def swaps(value, masks, count):
    return [swap(value, mask, count) for mask in masks]


def point(values, *tokens):
    return lax.optimization_barrier((values, tokens))[0]


def after(value, *tokens):
    return lax.optimization_barrier((value, tokens))[0]


def exchange(parts, masks, count):
    return [swap(part, mask, count) for part, mask in zip(parts, masks, strict=True)]


def group(own, others):
    joined = jnp.stack([own] + others)
    return joined.reshape((-1,) + joined.shape[-2:])


def pack_whole(qkv, mix, up, down, gain, shift, qv, proj, up_bias):
    pieces = []
    for pair in range(4):
        for part in range(3):
            base = 512 * part + 128 * pair
            pieces.append(qkv[:, base : base + 128])
    rows = jnp.concatenate([gain, shift, qv, proj], axis=0)
    tile = jnp.pad(rows.T, ((0, 0), (0, 120))).reshape(32, 16, 128)
    tile = tile.at[:, 0, 64:128].set(up_bias.reshape(32, 64))
    a0 = jnp.concatenate([jnp.concatenate(pieces, 1).reshape(32, 16, 1536), tile], axis=2)
    b0 = jnp.concatenate([mix, up], axis=1).reshape(32, 16, 2560)
    b1 = down.reshape(32, 4, 16, 512).swapaxes(1, 2).reshape(32, 16, 2048)
    return a0, b0, b1


def relative_halves(blocks):
    parts = blocks.reshape((4, 4, 2) + blocks.shape[1:])
    parts = parts.transpose((2, 1, 0) + tuple(range(3, parts.ndim)))
    return parts[0].reshape((16,) + blocks.shape[1:]), parts[1].reshape((16,) + blocks.shape[1:])


def whole_blocks(send, keep):
    parts = jnp.stack([keep, send.astype(F32)]).reshape((2, 4, 4) + keep.shape[1:])
    parts = parts.transpose((2, 1, 0) + tuple(range(3, parts.ndim)))
    return parts.reshape((32,) + keep.shape[1:])


def body(cubic, count, tokens, chain_ids, qkv, mix, up, down, gain, shift, qv, proj, up_bias, cot):
    params = (qkv, mix, up, down, gain, shift, qv, proj, up_bias)
    if cubic:
        index = lax.axis_index(AXES).astype(jnp.int32)
        me = jnp.stack([index, index & ~6])
        own, c_own = pack(*params)
        recv = swaps(own, Z_MASKS, count)
        c_recv = swaps(c_own, PLANE_MASKS, count)
        recv = point(recv)
        a_col = jnp.stack([part[:, :1664] for part in (own, *recv)])
        c_plane = group(c_own, after(c_recv, a_col))
        c_recv = swap(c_plane, 16, count)
        a_mine = lax.all_gather(after(a_col, c_plane), "plane").reshape(16, 16, -1)
        a_mine, c_recv = point((a_mine, c_recv))
        a_other = swap(a_mine, 1, count)
        own, *recv = after((own, *recv), a_mine)
        b_col = jnp.stack([part[:, 1664:] for part in (own, *recv)])
        b_recv = swaps(b_col, PLANE_MASKS, count)
        c_half = group(c_plane, [c_recv])
        c_recv = swap(c_half, 8, count)
        a_mine, a_other = after((a_mine, a_other), b_col, c_half)
    else:
        me = jnp.zeros((2,), jnp.int32)
        dims = (0, 0, 0, 0, 1, 1, 1, 1, 0)
        whole = [
            lax.all_gather(value, AXES, axis=dim, tiled=True)
            for value, dim in zip(params, dims, strict=True)
        ]
        a_parts, b_parts, c_parts = pack_whole(*whole)
        a_mine, a_other = relative_halves(a_parts)
        b_pair = relative_halves(b_parts)
        c_pair = [
            half.reshape(4, 2, 2, 16, 2048).transpose(2, 1, 0, 3, 4).reshape(16, 16, 2048)
            for half in relative_halves(c_parts)
        ]
    (
        qkv_rows, normed_t, weight, o, ot, lse, smalls, up_row, key_aux, query_aux,
    ) = forward(me, tokens, chain_ids, a_mine, a_other)
    if cubic:
        b_recv, c_recv, lse = point((b_recv, c_recv, lse))
        b_mine = group(b_col, b_recv)
        c_mine = group(c_half, [c_recv])
        b_pair = (b_mine, swap(b_mine, 1, count))
        c_pair = (c_mine, swap(c_mine, 1, count))
    (
        middle, normed_two_t, grad_pre, d_send, d_keep, mix_whole, up_whole, act_rows, down_whole,
    ) = feed_first(me, tokens, o, b_pair, c_pair, smalls, up_row, cot)
    if cubic:
        d_recv = swap(d_send, 1, count)
    u_send, u_keep, up_bias_grad = feed_second(me, normed_two_t, grad_pre)
    if cubic:
        u_recv = swap(u_send, 1, count)
    grad_middle, grad_att, mix_term, small_grads = feed_third(
        middle, grad_pre, mix_whole, up_whole, smalls, cot, ot
    )
    if cubic:
        d_recv, u_recv, small_grads = point((d_recv, u_recv, small_grads))
        du_own, du_parts = combine("feed_sum", 4, (d_keep, [d_recv]), (u_keep, [u_recv]))
        du_recv = exchange(du_parts, PLANE_MASKS, count)
        lse = after(lse, du_own)
    gm, g_send, g_keep = backward(
        me, qkv_rows, grad_att, ot, lse, weight, key_aux, query_aux, normed_t, smalls, small_grads,
        up_bias_grad, mix_term,
    )
    if cubic:
        du_recv, g_send, gm = point((du_recv, g_send, gm))
        g_recv = swap(g_send, 1, count)
        du_own, du_parts = combine("feed_sum_two", 2, (du_own, du_recv))
        du_recv = exchange(du_parts, (16,), count)
        g_own, g_parts = combine("last_sum", 4, (g_keep, [after(g_recv, du_own)]))
        g_recv = exchange(g_parts, PLANE_MASKS, count)
        smalls = after(smalls, g_own)
    input_grad, output = input_terms(
        [tokens, gm, weight, smalls, grad_middle, act_rows, down_whole, middle]
    )
    if cubic:
        g_recv, du_recv, input_grad = point((g_recv, du_recv, input_grad))
        own, du_own, parts = last_sums(g_own, g_recv, du_own, *du_recv)
        g_recv = exchange(parts, Z_MASKS, count)
        qkv_grad, mix_grad, up_grad, down_grad, *vectors, bias_grad = finish(own, g_recv, du_own)
        return (
            output, input_grad, qkv_grad, mix_grad, up_grad, down_grad, *vectors,
            bias_grad.reshape(64),
        )
    pairs = ((d_send, d_keep), (u_send, u_keep), (g_send, g_keep))
    blocks = [whole_blocks(s, r) for s, r in pairs]
    tiles = blocks[2][:, :, 2048:2176]
    joined = blocks[2].reshape(512, 2176)
    wholes = (
        blocks[0].reshape(32, 16, 4, 512).swapaxes(1, 2).reshape(2048, 512),
        blocks[1].reshape(512, 2048),
        joined[:, 1536:2048],
        joined[:, :1536].reshape(512, 4, 3, 128).swapaxes(1, 2).reshape(512, 1536),
        tiles[:, 0, 64:128].reshape(2048),
    )
    down_grad, up_grad, mix_grad, qkv_grad, bias_grad = [
        lax.psum_scatter(value, AXES, scatter_dimension=0, tiled=True) for value in wholes
    ]
    vectors = lax.psum_scatter(
        tiles[:, :, 0:8].reshape(512, 8).T, AXES, scatter_dimension=1, tiled=True
    )
    return (
        output, input_grad, qkv_grad, mix_grad, up_grad, down_grad,
        vectors[0:2], vectors[2:4], vectors[4:6], vectors[6:8], bias_grad,
    )


def solution(mesh):
    groups = mesh.shape["dp"]
    count = groups * mesh.shape["fsdp"]
    inner = jax.sharding.Mesh(mesh.devices.reshape(groups, -1, 2), AXES)
    cubic = inner.devices.shape == (4, 4, 2)

    def entry(*operands):
        return body(cubic, count, *operands)

    rows = P(AXES, None)
    columns = P(None, AXES)
    flat = P(AXES)
    return jax.shard_map(
        entry,
        mesh=inner,
        in_specs=(rows,) * 6 + (columns,) * 4 + (flat, rows),
        out_specs=(rows,) * 6 + (columns,) * 4 + (flat,),
        check_vma=False,
    )
```

```python
import functools
import math

import jax
import jax.numpy as jnp
from jax import lax
from jax.experimental import pallas as pl
from jax.experimental.pallas import tpu as pltpu
from jax.sharding import PartitionSpec as P

AXES = ("dp", "plane", "core")
HEADS = 8
EPS = 1e-05
SCALE = 0.125
EXP_SCALE = SCALE * math.log2(math.e)
HIDE = -(2.0**60)
MIB = 2**20

BF = jnp.bfloat16
F32 = jnp.float32
NN = (((1,), (0,)), ((), ()))
NT = (((1,), (1,)), ((), ()))
TN = (((0,), (0,)), ((), ()))


def dot(a, b, dims=NN):
    return lax.dot_general(a, b, dims, preferred_element_type=F32)


def vmem():
    return pl.BlockSpec(memory_space=pltpu.VMEM)


def smem():
    return pl.BlockSpec(memory_space=pltpu.SMEM)


def shape(dims, dtype):
    return jax.ShapeDtypeStruct(dims, dtype)


def block_of(index, block):
    return pl.ds(pl.multiple_of(index * block, block), block)


def cost(us):
    return pl.CostEstimate(flops=int(us * 1.1e9), bytes_accessed=0, transcendentals=0)


TALL_ORDER = (0, 2, 1, 3)


def slots():
    return [(c, j, i) for c in range(2) for j in range(4) for i in range(4)]


def block_row(me, c, j, i, rows):
    return pl.multiple_of((me ^ (c | (j << 1) | (i << 3))) * rows, rows)


def row_stats(rows_in):
    mean = jnp.mean(rows_in, axis=-1, keepdims=True)
    centred = rows_in - mean
    spread = jnp.mean(centred * centred, axis=-1, keepdims=True)
    return centred, lax.rsqrt(spread + EPS)


def split_three(row):
    first = row.astype(BF).astype(F32)
    rest = row - first
    second = rest.astype(BF).astype(F32)
    return first, second, rest - second


def pack_kernel(qkv, mix, up, down, gain, shift, qv, proj, up_bias, a0, c0, rows128):
    for pair in range(4):
        for part in range(3):
            base = 384 * pair + 128 * part
            a0[:, base : base + 128] = qkv[:, 512 * part + 128 * pair : 512 * part + 128 * pair + 128]
    rows128[...] = jnp.zeros_like(rows128)
    for index, ref in enumerate((gain, shift, qv, proj)):
        rows128[2 * index : 2 * index + 2, :] = ref[...].astype(F32)
    eye = (
        lax.broadcasted_iota(jnp.int32, (16, 16), 0) == lax.broadcasted_iota(jnp.int32, (16, 16), 1)
    ).astype(F32)
    columns = dot(eye.astype(BF), rows128[...].astype(BF), NT)
    bias = jnp.concatenate([jnp.zeros((1, 64), F32), up_bias[...].astype(F32)], axis=1)
    row = lax.broadcasted_iota(jnp.int32, (16, 128), 0)
    lane = lax.broadcasted_iota(jnp.int32, (16, 128), 1)
    a0[:, 1536:1664] = jnp.where((row == 0) & (lane >= 64), bias, columns).astype(BF)
    a0[:, 1664:2176] = mix[...]
    a0[:, 2176:4224] = up[...]
    for part in range(4):
        c0[:, 512 * part : 512 * part + 512] = down[16 * part : 16 * part + 16, :]


def pack(qkv, mix, up, down, gain, shift, qv, proj, up_bias):
    return pl.pallas_call(
        pack_kernel,
        in_specs=[vmem()] * 9,
        out_specs=[vmem()] * 2,
        out_shape=[shape((16, 4224), BF), shape((16, 2048), BF)],
        scratch_shapes=[pltpu.VMEM((128, 16), F32)],
        cost_estimate=cost(1.5),
        name="pack",
    )(qkv, mix, up, down, gain, shift, qv, proj, up_bias.reshape(1, 64))


def aux_rows(chain):
    row = lax.broadcasted_iota(jnp.int32, (128, chain.shape[1]), 0)
    low_bits = jnp.where(row < 7, (chain >> jnp.minimum(row, 6)) & 1, 0)
    high_bits = jnp.where(
        (row >= 7) & (row < 14), 1 - ((chain >> jnp.minimum(jnp.maximum(row - 7, 0), 6)) & 1), 0
    )
    bits = low_bits + high_bits
    query_side = bits.astype(F32) * HIDE
    key_side = jnp.where(row < 14, 1 - bits, jnp.where(row < 17, 1, 0)).astype(F32)
    return query_side.astype(BF), key_side.T.astype(BF)


def longest_pair(q2_t, k2):
    wide_q = q2_t.astype(F32)
    wide_k = k2.astype(F32)
    longest_q = jnp.max(jnp.sum(wide_q * wide_q, axis=0, keepdims=True))
    longest_k = jnp.max(jnp.sum(wide_k * wide_k, axis=1, keepdims=True))
    return longest_q * longest_k


def pair_forward(normed, weight, bias_q, bias_v, key_aux, qa, ot, outs, pair, block):
    qkv_out, o_out, ot_out, lse_out = outs
    rows = normed.shape[0]
    cols = block_of(pair, 128)
    q2 = (dot(normed, weight[:, 0:128]) + bias_q).astype(BF)
    k2 = dot(normed, weight[:, 128:256]).astype(BF)
    v2 = (dot(normed, weight[:, 256:384]) + bias_v).astype(BF)
    for index, value in enumerate((q2, k2, v2)):
        qkv_out[pair, index] = value
    qa[0:128, :] = q2.T
    vt = v2.T
    ones = (lax.broadcasted_iota(jnp.int32, (16, rows), 0) == 0).astype(F32).astype(BF)
    lane = lax.broadcasted_iota(jnp.int32, k2.shape, 1)
    zero = jnp.zeros_like(k2)
    keys = [
        jnp.concatenate([jnp.where((lane >= 64) == bool(h), k2, zero), key_aux], axis=1)
        for h in range(2)
    ]
    vts = [jnp.concatenate([vt[64 * h : 64 * h + 64], ones], axis=0) for h in range(2)]
    count = rows // block

    def score(index):
        q_cols = qa[:, block * index : block * index + block]
        return [dot(keys[h], q_cols) for h in range(2)]

    def attend(shifted):
        ahead = score(0)
        for index in range(count):
            scores = ahead
            if index + 1 < count:
                ahead = score(index + 1)
            span = slice(block * index, block * index + block)
            for h in range(2):
                if shifted:
                    peak = jnp.max(scores[h], axis=0, keepdims=True)
                    probs = jnp.exp2((scores[h] - peak) * EXP_SCALE).astype(BF)
                else:
                    peak = 0.0
                    probs = jnp.exp2(scores[h] * EXP_SCALE).astype(BF)
                mixed = dot(vts[h], probs)
                total = mixed[64:65]
                ot[64 * h : 64 * h + 64, span] = mixed[:64] * (1.0 / total)
                lse_out[pair, h : h + 1, span] = peak + jnp.log(total) * (1.0 / SCALE)

    bound = longest_pair(qa[0:128, :], k2) * (EXP_SCALE * EXP_SCALE)
    small = bound < 90.0 * 90.0

    @pl.when(small)
    def _():
        attend(False)

    @pl.when(jnp.logical_not(small))
    def _():
        attend(True)

    ot_out[cols, :] = ot[...].astype(BF)
    o_out[:, cols] = ot[...].T.astype(BF)


def forward_kernel(me_ref, tokens, chain, mine, other, *refs):
    qkv_hbm, normed_t_hbm, weight_hbm, o_out, ot_out, lse_out = refs[:6]
    smalls, up_row, key_aux_out, query_aux_out = refs[6:10]
    qa, ot, columns, qkv_out, normed_out, normed_t, weight, sems = refs[10:]
    me = me_ref[1]
    for c, j, i in slots():
        source = (mine, other)[c]
        row = block_row(me, c, j, i, 16)
        weight[pl.ds(row, 16), :] = source[4 * j + i, :, 0:1536]
        columns[pl.ds(row, 16), :] = source[4 * j + i, :, 1536:1664].astype(F32)
    smalls[...] = columns[...].T[0:8, :]
    lane = lax.broadcasted_iota(jnp.int32, (1, 128), 1)
    for a in range(16):
        even = pltpu.roll(columns[32 * a : 32 * a + 8, :], 64, 1)[0:1, :]
        odd = columns[32 * a + 16 : 32 * a + 17, :]
        up_row[:, 128 * a : 128 * a + 128] = jnp.where(lane < 64, even, odd)
    query_side, key_side = aux_rows(chain[...])
    qa[128:256, :] = query_side
    query_aux_out[...] = query_side
    key_aux_out[...] = key_side

    def norm_block(index, carry):
        span = pl.ds(pl.multiple_of(index * 256, 256), 256)
        centred, scale = row_stats(tokens[span, :].astype(F32))
        normed_out[span, :] = (centred * scale * smalls[0:1, :] + smalls[2:3, :]).astype(BF)
        return carry

    lax.fori_loop(0, tokens.shape[0] // 256, norm_block, 0)
    normed = normed_out[...]
    normed_t[0:512, :] = normed.T
    ones_row = lax.broadcasted_iota(jnp.int32, (16, normed.shape[0]), 0) == 0
    normed_t[512:528, :] = ones_row.astype(F32).astype(BF)
    copies = [
        pltpu.make_async_copy(normed_t, normed_t_hbm, sems.at[4]),
        pltpu.make_async_copy(weight, weight_hbm, sems.at[5]),
    ]
    for copy in copies:
        copy.start()
    outs = (qkv_out, o_out, ot_out, lse_out)

    def one_pair(pair, carry):
        cols = block_of(pair, 128)
        pair_forward(
            normed_out[...], weight[:, block_of(pair, 384)], smalls[4:5, cols], smalls[5:6, cols],
            key_aux_out[...], qa, ot, outs, pair, 512,
        )
        pltpu.make_async_copy(qkv_out.at[pair], qkv_hbm.at[pair], sems.at[pair]).start()
        return carry

    lax.fori_loop(0, 4, one_pair, 0)
    for pair in range(4):
        pltpu.make_async_copy(qkv_out.at[pair], qkv_hbm.at[pair], sems.at[pair]).wait()
    for copy in copies:
        copy.wait()


def hbm():
    return pl.BlockSpec(memory_space=pltpu.HBM)


def forward(me, tokens, chain, mine, other):
    rows = tokens.shape[0]
    return pl.pallas_call(
        forward_kernel,
        in_specs=[smem()] + [vmem()] * 4,
        out_specs=[hbm()] * 3 + [vmem()] * 7,
        out_shape=[
            shape((4, 3, rows, 128), BF),
            shape((528, rows), BF),
            shape((512, 1536), BF),
            shape((rows, 512), BF),
            shape((512, rows), BF),
            shape((4, 2, rows), F32),
            shape((8, 512), F32),
            shape((1, 2048), F32),
            shape((rows, 128), BF),
            shape((128, rows), BF),
        ],
        scratch_shapes=[
            pltpu.VMEM((256, rows), BF),
            pltpu.VMEM((128, rows), F32),
            pltpu.VMEM((512, 128), F32),
            pltpu.VMEM((4, 3, rows, 128), BF),
            pltpu.VMEM((rows, 512), BF),
            pltpu.VMEM((528, rows), BF),
            pltpu.VMEM((512, 1536), BF),
            pltpu.SemaphoreType.DMA((6,)),
        ],
        compiler_params=pltpu.CompilerParams(vmem_limit_bytes=20 * MIB),
        cost_estimate=cost(15),
        name="attend",
    )(me, tokens, chain, mine, other)


def gelu_parts(u):
    half_cdf = 0.5 + 0.5 * lax.erf(u * math.sqrt(0.5))
    density = jnp.exp2(u * u * (-0.5 * math.log2(math.e))) * (1.0 / math.sqrt(2.0 * math.pi))
    return u * half_cdf, half_cdf + u * density


def scatter_tall(me, source, base_block, send, keep):
    core = me & 1
    for half in range(4):
        r = (me ^ (base_block + 2 * half)) >> 1
        place = ((r & 3) << 2) | (r >> 2)
        for part in range(4):
            row = 128 * half + 16 * part
            span = slice(512 * part, 512 * part + 512)
            keep[place, :, span] = source[pl.ds(pl.multiple_of(row + core * 64, 16), 16), :]
            sent = source[pl.ds(pl.multiple_of(row + (1 - core) * 64, 16), 16), :]
            send[place, :, span] = sent.astype(BF)


def scatter_blocks(me, source, rows, base_block, blocks, send, keep, span):
    core = me & 1
    for half in range(blocks // 2):
        first = base_block + 2 * half
        row = 2 * half * rows
        r = (me ^ first) >> 1
        place = ((r & 3) << 2) | (r >> 2)
        kept = source[pl.ds(pl.multiple_of(row + core * rows, rows), rows), :]
        sent = source[pl.ds(pl.multiple_of(row + (1 - core) * rows, rows), rows), :]
        keep[place, :, span] = kept
        send[place, :, span] = sent.astype(BF)


def feed_first_kernel(
    me_ref, tokens, o_in, mine, other, mine_tall, other_tall, smalls, up_row, cot,
    middle, normed_t, grad_pre_out, d_send, d_keep, mix, up, act_rows, down,
    normed, stage,
):
    me = me_ref[0]
    for c, j, i in slots():
        source = (mine, other)[c]
        row = block_row(me, c, j, i, 16)
        mix[pl.ds(row, 16), :] = source[4 * j + i, :, 0:512]
        up[pl.ds(row, 16), :] = source[4 * j + i, :, 512:2560]
        source = (mine_tall, other_tall)[c]
        for part in range(4):
            row = pl.multiple_of(block_row(me, c, j, i, 64) + 16 * part, 16)
            span = slice(512 * part, 512 * part + 512)
            down[pl.ds(row, 16), :] = source[4 * TALL_ORDER[i] + j, :, span]
    rows = tokens.shape[0]
    block = 256

    def ahead(index, carry):
        span = pl.ds(pl.multiple_of(index * block, block), block)
        mid = tokens[span, :].astype(F32) + dot(o_in[span, :], mix[...]) + smalls[6:7, :]
        middle[span, :] = mid
        centred, scale = row_stats(mid)
        normed[span, :] = (centred * scale * smalls[1:2, :] + smalls[3:4, :]).astype(BF)
        return carry

    lax.fori_loop(0, rows // block, ahead, 0)
    normed_t[0:512, :] = normed[...].T
    ones_row = lax.broadcasted_iota(jnp.int32, (16, rows), 0) == 0
    normed_t[512:528, :] = ones_row.astype(F32).astype(BF)
    width = 512

    def one_chunk(chunk, carry):
        span = block_of(chunk, width)
        down_part = down[span, :]
        act, slope = gelu_parts(dot(normed[...], up[:, span]) + up_row[:, span])
        act_low = act.astype(BF)
        grad_pre_out[:, span] = (dot(cot[...], down_part, NT) * slope).astype(BF)
        act_rows[:, span] = act_low
        stage[...] = dot(act_low, cot[...], TN)
        scatter_tall(me, stage, chunk * (width // 64), d_send, d_keep)
        return carry

    lax.fori_loop(0, 2048 // width, one_chunk, 0)


def feed_first(me, tokens, o_in, b_pair, c_pair, smalls, up_row, cot):
    rows = tokens.shape[0]
    return pl.pallas_call(
        feed_first_kernel,
        in_specs=[smem()] + [vmem()] * 9,
        out_specs=[vmem()] * 9,
        out_shape=[
            shape((rows, 512), F32),
            shape((528, rows), BF),
            shape((rows, 2048), BF),
            shape((16, 16, 2048), BF),
            shape((16, 16, 2048), F32),
            shape((512, 512), BF),
            shape((512, 2048), BF),
            shape((rows, 2048), BF),
            shape((2048, 512), BF),
        ],
        scratch_shapes=[
            pltpu.VMEM((rows, 512), BF),
            pltpu.VMEM((512, 512), F32),
        ],
        compiler_params=pltpu.CompilerParams(vmem_limit_bytes=14 * MIB),
        cost_estimate=cost(18),
        name="feed_first",
    )(me, tokens, o_in, *b_pair, *c_pair, smalls, up_row, cot)


def feed_second_kernel(me_ref, normed_t, grad_pre, u_send, u_keep, up_bias_grad, stage):
    me = me_ref[0]
    width = 1024

    def one_chunk(chunk, carry):
        span = block_of(chunk, width)
        stage[...] = dot(normed_t[...], grad_pre[:, span])
        up_bias_grad[:, span] = stage[512:513, :]
        scatter_blocks(me, stage, 16, 0, 32, u_send, u_keep, span)
        return carry

    lax.fori_loop(0, 2048 // width, one_chunk, 0)


def feed_second(me, normed_t, grad_pre):
    return pl.pallas_call(
        feed_second_kernel,
        in_specs=[smem()] + [vmem()] * 2,
        out_specs=[vmem()] * 3,
        out_shape=[
            shape((16, 16, 2048), BF),
            shape((16, 16, 2048), F32),
            shape((1, 2048), F32),
        ],
        scratch_shapes=[pltpu.VMEM((528, 1024), F32)],
        compiler_params=pltpu.CompilerParams(vmem_limit_bytes=12 * MIB),
        cost_estimate=cost(5),
        name="feed_second",
    )(me, normed_t, grad_pre)


def feed_third_kernel(
    middle, grad_pre, mix, up, smalls, cot, ot_in,
    grad_middle, grad_att, mix_grad, small_grads, low_rows,
):
    rows = middle.shape[0]
    block = 512

    def behind(index, carry):
        gain_sum, shift_sum, branch_sum, cot_sum = carry
        span = pl.ds(pl.multiple_of(index * block, block), block)
        centred, scale = row_stats(middle[span, :])
        xh = centred * scale
        h = dot(grad_pre[span, :], up[...], NT)
        hg = h * smalls[1:2, :]
        cot_rows = cot[span, :].astype(F32)
        grad = cot_rows + scale * (
            hg
            - jnp.mean(hg, axis=-1, keepdims=True)
            - xh * jnp.mean(hg * xh, axis=-1, keepdims=True)
        )
        grad_middle[span, :] = grad
        low = grad.astype(BF)
        low_rows[span, :] = low
        grad_att[span, :] = dot(low, mix[...], NT).astype(BF)
        return (
            gain_sum + jnp.sum(h * xh, axis=0, keepdims=True),
            shift_sum + jnp.sum(h, axis=0, keepdims=True),
            branch_sum + jnp.sum(low.astype(F32), axis=0, keepdims=True),
            cot_sum + jnp.sum(cot_rows, axis=0, keepdims=True),
        )

    zero = jnp.zeros((1, 512), F32)
    sums = lax.fori_loop(0, rows // block, behind, (zero, zero, zero, zero))
    for index in range(4):
        small_grads[index : index + 1, :] = sums[index]
    small_grads[4:8, :] = jnp.zeros((4, 512), F32)
    mix_grad[0:256, :] = dot(ot_in[0:256, :], low_rows[...])
    mix_grad[256:512, :] = dot(ot_in[256:512, :], low_rows[...])


def feed_third(middle, grad_pre, mix, up, smalls, cot, ot_in):
    rows = middle.shape[0]
    return pl.pallas_call(
        feed_third_kernel,
        in_specs=[vmem()] * 7,
        out_specs=[vmem()] * 4,
        out_shape=[
            shape((rows, 512), F32),
            shape((rows, 512), BF),
            shape((512, 512), F32),
            shape((8, 512), F32),
        ],
        scratch_shapes=[pltpu.VMEM((rows, 512), BF)],
        compiler_params=pltpu.CompilerParams(vmem_limit_bytes=14 * MIB),
        cost_estimate=cost(8),
        name="feed_third",
    )(middle, grad_pre, mix, up, smalls, cot, ot_in)


def pair_backward(q, k, v, do, ot_in, lse, key_aux, qa, da, dqt, acc_k, acc_v, gm, block):
    k2 = k[0, 0]
    v2 = v[0, 0]
    rows = k2.shape[0]
    kt = k2.T
    lane = lax.broadcasted_iota(jnp.int32, k2.shape, 1)
    zero = jnp.zeros_like(k2)
    keys = []
    vals = []
    for h in range(2):
        own = (lane >= 64) == bool(h)
        keys.append(jnp.concatenate([jnp.where(own, k2, zero), key_aux], axis=1))
        vals.append(jnp.concatenate([jnp.where(own, v2, zero), key_aux], axis=1))
    qt = q[0, 0].T
    dt = do[...].T
    product = dt.astype(F32) * ot_in[...].astype(F32)
    row = lax.broadcasted_iota(jnp.int32, (16, rows), 0)
    for h in range(2):
        qa[h, 0:128, :] = qt
        da[h, 0:128, :] = dt
        delta = jnp.sum(product[64 * h : 64 * h + 64], axis=0, keepdims=True)
        base = qa[h, 128:144, :].astype(F32)
        one, two, three = split_three(-lse[0, h : h + 1, :])
        base = jnp.where(row == 14, one, jnp.where(row == 15, two, base))
        qa[h, 128:144, :] = base.astype(BF)
        qa[h, 144:160, :] = jnp.where(row == 0, three, 0.0).astype(BF)
        one, two, three = split_three(-delta)
        base = jnp.where(row == 14, one, jnp.where(row == 15, two, 0.0))
        da[h, 128:144, :] = base.astype(BF)
        da[h, 144:160, :] = jnp.where(row == 0, three, 0.0).astype(BF)
    small_lane = lax.broadcasted_iota(jnp.int32, (block, 128), 1)
    for index in range(rows // block):
        span = slice(block * index, block * index + block)
        do_rows = do[span, :]
        q_rows = q[0, 0, span, :]
        blank = jnp.zeros_like(do_rows)
        sum_k = None
        sum_v = None
        for h in range(2):
            own = (small_lane >= 64) == bool(h)
            probs = jnp.exp2(dot(keys[h], qa[h, :, span]) * EXP_SCALE)
            grad = (probs * dot(vals[h], da[h, :, span])).astype(BF)
            probs = probs.astype(BF)
            dqt[64 * h : 64 * h + 64, span] = dot(kt[64 * h : 64 * h + 64, :], grad)
            part_k = dot(grad, jnp.where(own, q_rows, blank))
            part_v = dot(probs, jnp.where(own, do_rows, blank))
            sum_k = part_k if sum_k is None else sum_k + part_k
            sum_v = part_v if sum_v is None else sum_v + part_v
        if index == 0:
            acc_k[...] = sum_k
            acc_v[...] = sum_v
        else:
            acc_k[...] += sum_k
            acc_v[...] += sum_v
    gm[:, 0:128] = (dqt[...].T * SCALE).astype(BF)
    gm[:, 128:256] = (acc_k[...] * SCALE).astype(BF)
    gm[:, 256:384] = acc_v[...].astype(BF)


def backward_kernel(
    me_ref, q, k, v, do, ot_in, lse, weight, key_aux, query_aux, normed_t, smalls, small_grads,
    up_bias_grad, mix_term, gm, send, keep,
    qa, da, dqt, acc_k, acc_v, gm_pair, stage, sums, vectors, columns,
):
    me = me_ref[0]
    pair = pl.program_id(0)

    @pl.when(pair == 0)
    def _():
        for h in range(2):
            qa[h, 128:256, :] = query_aux[...]
            da[h, 128:256, :] = jnp.zeros((128, da.shape[2]), BF)
        vectors[...] = jnp.zeros_like(vectors)
        scatter_blocks(me, mix_term, 16, 0, 32, send, keep, slice(1536, 2048))

    pair_backward(q, k, v, do, ot_in, lse, key_aux[...], qa, da, dqt, acc_k, acc_v, gm_pair, 512)
    span = block_of(pair, 384)
    gm[:, span] = gm_pair[...]
    stage[...] = dot(normed_t[...], gm_pair[...])
    total = stage[512:513, :]
    sums[:, span] = jnp.broadcast_to(total, (8, 384))
    scatter_blocks(me, stage, 16, 0, 32, send, keep, span)
    wide = weight[...].astype(F32)
    for index, product in enumerate((stage[0:512, :] * wide, wide * total)):
        vectors[index] += product[:, 0:128] + product[:, 128:256] + product[:, 256:384]

    @pl.when(pair == 3)
    def _():
        columns[...] = jnp.zeros_like(columns)
        columns[1:2, :] = small_grads[0:1, :]
        columns[3:4, :] = small_grads[1:2, :]
        for index in range(4):
            cols = slice(128 * index, 128 * index + 128)
            columns[4:5, cols] = sums[0:1, 384 * index : 384 * index + 128]
            columns[5:6, cols] = sums[0:1, 384 * index + 256 : 384 * index + 384]
        columns[6:7, :] = small_grads[2:3, :]
        columns[7:8, :] = small_grads[3:4, :]
        columns[8:9, :] = smalls[0:1, :]
        columns[9:10, :] = smalls[2:3, :]
        tile = columns[...].T
        plain = jnp.sum(vectors[1], axis=1, keepdims=True)
        weighted = jnp.sum(vectors[0], axis=1, keepdims=True)
        gain_sum = (weighted - tile[:, 9:10] * plain) / tile[:, 8:9]
        lanes = lax.broadcasted_iota(jnp.int32, (512, 128), 1)
        stage[0:512, 0:128] = jnp.where(lanes == 0, gain_sum, jnp.where(lanes == 2, plain, tile))
        lane = lax.broadcasted_iota(jnp.int32, (1, 128), 1)
        for a in range(16):
            piece = up_bias_grad[:, 128 * a : 128 * a + 128]
            rolled = pltpu.roll(jnp.broadcast_to(piece, (8, 128)), 64, 1)[0:1, :]
            for half, values in enumerate((rolled, piece)):
                row = 32 * a + 16 * half
                old = stage[row : row + 1, 0:128]
                stage[row : row + 1, 0:128] = jnp.where(lane < 64, old, values)
        core = me & 1
        for half in range(16):
            r = (me ^ (2 * half)) >> 1
            place = ((r & 3) << 2) | (r >> 2)
            kept = pl.multiple_of(32 * half + core * 16, 16)
            sent = pl.multiple_of(32 * half + (1 - core) * 16, 16)
            keep[place, :, 2048:2176] = stage[pl.ds(kept, 16), 0:128]
            send[place, :, 2048:2176] = stage[pl.ds(sent, 16), 0:128].astype(BF)


def backward(me, qkv_rows, do, ot, lse, weight, *rest):
    rows = do.shape[0]
    parts = [pl.BlockSpec((1, 1, rows, 128), lambda i, part=part: (i, part, 0, 0)) for part in range(3)]
    return pl.pallas_call(
        backward_kernel,
        grid=(4,),
        in_specs=[smem()]
        + parts
        + [
            pl.BlockSpec((rows, 128), lambda i: (0, i)),
            pl.BlockSpec((128, rows), lambda i: (i, 0)),
            pl.BlockSpec((1, 2, rows), lambda i: (i, 0, 0)),
            pl.BlockSpec((512, 384), lambda i: (0, i)),
        ]
        + [vmem()] * 7,
        out_specs=[vmem()] * 3,
        out_shape=[
            shape((rows, 1536), BF),
            shape((16, 16, 2176), BF),
            shape((16, 16, 2176), F32),
        ],
        scratch_shapes=[
            pltpu.VMEM((2, 256, rows), BF),
            pltpu.VMEM((2, 256, rows), BF),
            pltpu.VMEM((128, rows), F32),
            pltpu.VMEM((rows, 128), F32),
            pltpu.VMEM((rows, 128), F32),
            pltpu.VMEM((rows, 384), BF),
            pltpu.VMEM((528, 384), F32),
            pltpu.VMEM((8, 1536), F32),
            pltpu.VMEM((2, 512, 128), F32),
            pltpu.VMEM((128, 512), F32),
        ],
        compiler_params=pltpu.CompilerParams(vmem_limit_bytes=20 * MIB),
        cost_estimate=cost(25),
        name="attend_back",
    )(me, qkv_rows, qkv_rows, qkv_rows, do, ot, lse, weight, *rest)


def input_kernel(
    tokens, gm, weight, smalls, grad_middle, act, down, middle, input_grad, output
):
    block = 256

    def behind(index, carry):
        span = pl.ds(pl.multiple_of(index * block, block), block)
        centred, scale = row_stats(tokens[span, :].astype(F32))
        xh = centred * scale
        total = middle[span, :] + dot(act[span, :], down[...]) + smalls[7:8, :]
        output[span, :] = total.astype(BF)
        hg = dot(gm[span, :], weight[...], NT) * smalls[0:1, :]
        input_grad[span, :] = grad_middle[span, :] + scale * (
            hg
            - jnp.mean(hg, axis=-1, keepdims=True)
            - xh * jnp.mean(hg * xh, axis=-1, keepdims=True)
        )
        return carry

    lax.fori_loop(0, tokens.shape[0] // block, behind, 0)


def input_terms(operands):
    rows = operands[0].shape[0]
    return pl.pallas_call(
        input_kernel,
        in_specs=[vmem()] * 8,
        out_specs=[vmem()] * 2,
        out_shape=[shape((rows, 512), F32), shape((rows, 512), BF)],
        compiler_params=pltpu.CompilerParams(vmem_limit_bytes=12 * MIB),
        cost_estimate=cost(8),
        name="input_terms",
    )(*operands)


def combine_kernel(counts, pieces, *refs):
    total_in = sum(counts) + len(counts)
    outs = refs[total_in:]
    position = 0
    base = 0
    for count in counts:
        own, incoming = refs[position], refs[position + 1 : position + 1 + count]
        position += 1 + count
        width = own.shape[2]
        rows = own.shape[0] // pieces
        for index in range(pieces):
            span = slice(rows * index, rows * index + rows)
            total = own[span]
            for ref in incoming:
                total = total + ref[span].astype(F32)
            outs[index][:, :, base : base + width] = total.astype(outs[index].dtype)
        base += width


def combine(name, pieces, *sums):
    slot_count = sums[0][0].shape[0] // pieces
    width = sum(own.shape[2] for own, _ in sums)
    operands = [part for own, received in sums for part in (own, *received)]
    dims = (slot_count, 16, width)
    first, *rest = pl.pallas_call(
        functools.partial(combine_kernel, [len(received) for _, received in sums], pieces),
        in_specs=[vmem()] * len(operands),
        out_specs=[vmem()] * pieces,
        out_shape=[shape(dims, F32)] + [shape(dims, BF)] * (pieces - 1),
        compiler_params=pltpu.CompilerParams(vmem_limit_bytes=8 * MIB),
        cost_estimate=cost(1.5),
        name=name,
    )(*operands)
    return first, rest


def last_kernel(g_own, g0, g1, g2, du_own, du_recv, own, du_first, p0, p1, p2):
    width = g_own.shape[2]
    for index in range(4):
        total = g_own[index]
        for ref in (g0, g1, g2):
            total = total + ref[index].astype(F32)
        if index == 0:
            own[0] = total
        else:
            (p0, p1, p2)[index - 1][0, :, 0:width] = total.astype(BF)
    du_first[0] = du_own[0] + du_recv[0].astype(F32)
    p0[0, :, width:] = (du_own[1] + du_recv[1].astype(F32)).astype(BF)


def last_sums(g_own, g_recv, du_own, du_recv):
    width, wide = g_own.shape[2], du_own.shape[2]
    own, du_first, *parts = pl.pallas_call(
        last_kernel,
        in_specs=[vmem()] * 6,
        out_specs=[vmem()] * 5,
        out_shape=[shape((1, 16, width), F32), shape((1, 16, wide), F32)]
        + [shape((1, 16, width + wide), BF)]
        + [shape((1, 16, width), BF)] * 2,
        compiler_params=pltpu.CompilerParams(vmem_limit_bytes=8 * MIB),
        cost_estimate=cost(1.5),
        name="last_sums",
    )(g_own, *g_recv, du_own, du_recv)
    return own, du_first, parts


def finish_kernel(
    own, r0, r1, r2, du_own,
    qkv_grad, mix_grad, up_grad, down_grad, gain, shift, qv, proj, bias,
):
    total = own[0] + r0[0, :, 0:2176].astype(F32)
    for ref in (r1, r2):
        total = total + ref[0].astype(F32)
    mix_grad[...] = total[:, 1536:2048]
    for pair in range(4):
        for part in range(3):
            base = 384 * pair + 128 * part
            column = 512 * part + 128 * pair
            qkv_grad[:, column : column + 128] = total[:, base : base + 128]
    tile = total[:, 2048:2176]
    wide = jnp.concatenate([tile, jnp.zeros((112, 128), F32)], axis=0).T
    for index, ref in enumerate((gain, shift, qv, proj)):
        ref[...] = wide[2 * index : 2 * index + 2, 0:16]
    bias[...] = tile[0:1, 64:128]
    total = du_own[0] + r0[0, :, 2176:].astype(F32)
    for part in range(4):
        down_grad[16 * part : 16 * part + 16, :] = total[:, 512 * part : 512 * part + 512]
    up_grad[...] = total[:, 2048:4096]


def finish(own, received, du_own):
    return pl.pallas_call(
        finish_kernel,
        in_specs=[vmem()] * 5,
        out_specs=[vmem()] * 9,
        out_shape=[
            shape((16, 1536), F32),
            shape((16, 512), F32),
            shape((16, 2048), F32),
            shape((64, 512), F32),
        ]
        + [shape((2, 16), F32)] * 4
        + [shape((1, 64), F32)],
        compiler_params=pltpu.CompilerParams(vmem_limit_bytes=6 * MIB),
        cost_estimate=cost(1.5),
        name="finish",
    )(own, *received, du_own)


def swap(value, mask, count):
    return lax.ppermute(value, AXES, [(d, d ^ mask) for d in range(count)])


Z_MASKS = (8, 16, 24)
PLANE_MASKS = (2, 4, 6)


def swaps(value, masks, count):
    return [swap(value, mask, count) for mask in masks]


def point(values, *tokens):
    return lax.optimization_barrier((values, tokens))[0]


def after(value, *tokens):
    return lax.optimization_barrier((value, tokens))[0]


def exchange(parts, masks, count):
    return [swap(part, mask, count) for part, mask in zip(parts, masks, strict=True)]


def group(own, others):
    joined = jnp.stack([own] + others)
    return joined.reshape((-1,) + joined.shape[-2:])


def pack_whole(qkv, mix, up, down, gain, shift, qv, proj, up_bias):
    pieces = []
    for pair in range(4):
        for part in range(3):
            base = 512 * part + 128 * pair
            pieces.append(qkv[:, base : base + 128])
    rows = jnp.concatenate([gain, shift, qv, proj], axis=0)
    tile = jnp.pad(rows.T, ((0, 0), (0, 120))).reshape(32, 16, 128)
    tile = tile.at[:, 0, 64:128].set(up_bias.reshape(32, 64))
    a0 = jnp.concatenate([jnp.concatenate(pieces, 1).reshape(32, 16, 1536), tile], axis=2)
    b0 = jnp.concatenate([mix, up], axis=1).reshape(32, 16, 2560)
    b1 = down.reshape(32, 4, 16, 512).swapaxes(1, 2).reshape(32, 16, 2048)
    return a0, b0, b1


def relative_halves(blocks):
    parts = blocks.reshape((4, 4, 2) + blocks.shape[1:])
    parts = parts.transpose((2, 1, 0) + tuple(range(3, parts.ndim)))
    return parts[0].reshape((16,) + blocks.shape[1:]), parts[1].reshape((16,) + blocks.shape[1:])


def whole_blocks(send, keep):
    parts = jnp.stack([keep, send.astype(F32)]).reshape((2, 4, 4) + keep.shape[1:])
    parts = parts.transpose((2, 1, 0) + tuple(range(3, parts.ndim)))
    return parts.reshape((32,) + keep.shape[1:])


def body(cubic, count, tokens, chain_ids, qkv, mix, up, down, gain, shift, qv, proj, up_bias, cot):
    params = (qkv, mix, up, down, gain, shift, qv, proj, up_bias)
    if cubic:
        index = lax.axis_index(AXES).astype(jnp.int32)
        me = jnp.stack([index, index & ~6])
        own, c_own = pack(*params)
        recv = swaps(own, Z_MASKS, count)
        c_recv = swaps(c_own, PLANE_MASKS, count)
        recv = point(recv)
        a_col = jnp.stack([part[:, :1664] for part in (own, *recv)])
        c_plane = group(c_own, after(c_recv, a_col))
        c_recv = swap(c_plane, 16, count)
        a_mine = lax.all_gather(after(a_col, c_plane), "plane").reshape(16, 16, -1)
        a_mine, c_recv = point((a_mine, c_recv))
        a_other = swap(a_mine, 1, count)
        own, *recv = after((own, *recv), a_mine)
        b_col = jnp.stack([part[:, 1664:] for part in (own, *recv)])
        b_recv = swaps(b_col, PLANE_MASKS, count)
        c_half = group(c_plane, [c_recv])
        c_recv = swap(c_half, 8, count)
        a_mine, a_other = after((a_mine, a_other), b_col, c_half)
    else:
        me = jnp.zeros((2,), jnp.int32)
        dims = (0, 0, 0, 0, 1, 1, 1, 1, 0)
        whole = [
            lax.all_gather(value, AXES, axis=dim, tiled=True)
            for value, dim in zip(params, dims, strict=True)
        ]
        a_parts, b_parts, c_parts = pack_whole(*whole)
        a_mine, a_other = relative_halves(a_parts)
        b_pair = relative_halves(b_parts)
        c_pair = [
            half.reshape(4, 2, 2, 16, 2048).transpose(2, 1, 0, 3, 4).reshape(16, 16, 2048)
            for half in relative_halves(c_parts)
        ]
    (
        qkv_rows, normed_t, weight, o, ot, lse, smalls, up_row, key_aux, query_aux,
    ) = forward(me, tokens, chain_ids, a_mine, a_other)
    if cubic:
        b_recv, c_recv, lse = point((b_recv, c_recv, lse))
        b_mine = group(b_col, b_recv)
        c_mine = group(c_half, [c_recv])
        b_pair = (b_mine, swap(b_mine, 1, count))
        c_pair = (c_mine, swap(c_mine, 1, count))
    (
        middle, normed_two_t, grad_pre, d_send, d_keep, mix_whole, up_whole, act_rows, down_whole,
    ) = feed_first(me, tokens, o, b_pair, c_pair, smalls, up_row, cot)
    if cubic:
        d_recv = swap(d_send, 1, count)
    u_send, u_keep, up_bias_grad = feed_second(me, normed_two_t, grad_pre)
    if cubic:
        u_recv = swap(u_send, 1, count)
    grad_middle, grad_att, mix_term, small_grads = feed_third(
        middle, grad_pre, mix_whole, up_whole, smalls, cot, ot
    )
    if cubic:
        d_recv, u_recv, small_grads = point((d_recv, u_recv, small_grads))
        du_own, du_parts = combine("feed_sum", 4, (d_keep, [d_recv]), (u_keep, [u_recv]))
        du_recv = exchange(du_parts, PLANE_MASKS, count)
        lse = after(lse, du_own)
    gm, g_send, g_keep = backward(
        me, qkv_rows, grad_att, ot, lse, weight, key_aux, query_aux, normed_t, smalls, small_grads,
        up_bias_grad, mix_term,
    )
    if cubic:
        du_recv, g_send, gm = point((du_recv, g_send, gm))
        g_recv = swap(g_send, 1, count)
        du_own, du_parts = combine("feed_sum_two", 2, (du_own, du_recv))
        du_recv = exchange(du_parts, (16,), count)
        g_own, g_parts = combine("last_sum", 4, (g_keep, [after(g_recv, du_own)]))
        g_recv = exchange(g_parts, PLANE_MASKS, count)
        smalls = after(smalls, g_own)
    input_grad, output = input_terms(
        [tokens, gm, weight, smalls, grad_middle, act_rows, down_whole, middle]
    )
    if cubic:
        g_recv, du_recv, input_grad = point((g_recv, du_recv, input_grad))
        own, du_own, parts = last_sums(g_own, g_recv, du_own, *du_recv)
        g_recv = exchange(parts, Z_MASKS, count)
        qkv_grad, mix_grad, up_grad, down_grad, *vectors, bias_grad = finish(own, g_recv, du_own)
        return (
            output, input_grad, qkv_grad, mix_grad, up_grad, down_grad, *vectors,
            bias_grad.reshape(64),
        )
    pairs = ((d_send, d_keep), (u_send, u_keep), (g_send, g_keep))
    blocks = [whole_blocks(s, r) for s, r in pairs]
    tiles = blocks[2][:, :, 2048:2176]
    joined = blocks[2].reshape(512, 2176)
    wholes = (
        blocks[0].reshape(32, 16, 4, 512).swapaxes(1, 2).reshape(2048, 512),
        blocks[1].reshape(512, 2048),
        joined[:, 1536:2048],
        joined[:, :1536].reshape(512, 4, 3, 128).swapaxes(1, 2).reshape(512, 1536),
        tiles[:, 0, 64:128].reshape(2048),
    )
    down_grad, up_grad, mix_grad, qkv_grad, bias_grad = [
        lax.psum_scatter(value, AXES, scatter_dimension=0, tiled=True) for value in wholes
    ]
    vectors = lax.psum_scatter(
        tiles[:, :, 0:8].reshape(512, 8).T, AXES, scatter_dimension=1, tiled=True
    )
    return (
        output, input_grad, qkv_grad, mix_grad, up_grad, down_grad,
        vectors[0:2], vectors[2:4], vectors[4:6], vectors[6:8], bias_grad,
    )


def solution(mesh):
    groups = mesh.shape["dp"]
    count = groups * mesh.shape["fsdp"]
    inner = jax.sharding.Mesh(mesh.devices.reshape(groups, -1, 2), AXES)
    cubic = inner.devices.shape == (4, 4, 2)

    def entry(*operands):
        return body(cubic, count, *operands)

    rows = P(AXES, None)
    columns = P(None, AXES)
    flat = P(AXES)
    return jax.shard_map(
        entry,
        mesh=inner,
        in_specs=(rows,) * 6 + (columns,) * 4 + (flat, rows),
        out_specs=(rows,) * 6 + (columns,) * 4 + (flat,),
        check_vma=False,
    )
```

```python
import functools
import math

import jax
import jax.numpy as jnp
from jax import lax
from jax.experimental import pallas as pl
from jax.experimental.pallas import tpu as pltpu
from jax.sharding import PartitionSpec as P

AXES = ("dp", "plane", "core")
HEADS = 8
EPS = 1e-05
SCALE = 0.125
EXP_SCALE = SCALE * math.log2(math.e)
HIDE = -(2.0**60)
MIB = 2**20

BF = jnp.bfloat16
F32 = jnp.float32
NN = (((1,), (0,)), ((), ()))
NT = (((1,), (1,)), ((), ()))
TN = (((0,), (0,)), ((), ()))


def dot(a, b, dims=NN):
    return lax.dot_general(a, b, dims, preferred_element_type=F32)


def vmem():
    return pl.BlockSpec(memory_space=pltpu.VMEM)


def smem():
    return pl.BlockSpec(memory_space=pltpu.SMEM)


def shape(dims, dtype):
    return jax.ShapeDtypeStruct(dims, dtype)


def block_of(index, block):
    return pl.ds(pl.multiple_of(index * block, block), block)


def cost(us):
    return pl.CostEstimate(flops=int(us * 1.1e9), bytes_accessed=0, transcendentals=0)


TALL_ORDER = (0, 2, 1, 3)


def slots():
    return [(c, j, i) for c in range(2) for j in range(4) for i in range(4)]


def block_row(me, c, j, i, rows):
    return pl.multiple_of((me ^ (c | (j << 1) | (i << 3))) * rows, rows)


def row_stats(rows_in):
    mean = jnp.mean(rows_in, axis=-1, keepdims=True)
    centred = rows_in - mean
    spread = jnp.mean(centred * centred, axis=-1, keepdims=True)
    return centred, lax.rsqrt(spread + EPS)


def split_three(row):
    first = row.astype(BF).astype(F32)
    rest = row - first
    second = rest.astype(BF).astype(F32)
    return first, second, rest - second


def pack_kernel(qkv, mix, up, down, gain, shift, qv, proj, up_bias, a0, c0, rows128):
    for pair in range(4):
        for part in range(3):
            base = 384 * pair + 128 * part
            a0[:, base : base + 128] = qkv[:, 512 * part + 128 * pair : 512 * part + 128 * pair + 128]
    rows128[...] = jnp.zeros_like(rows128)
    for index, ref in enumerate((gain, shift, qv, proj)):
        rows128[2 * index : 2 * index + 2, :] = ref[...].astype(F32)
    eye = (
        lax.broadcasted_iota(jnp.int32, (16, 16), 0) == lax.broadcasted_iota(jnp.int32, (16, 16), 1)
    ).astype(F32)
    columns = dot(eye.astype(BF), rows128[...].astype(BF), NT)
    bias = jnp.concatenate([jnp.zeros((1, 64), F32), up_bias[...].astype(F32)], axis=1)
    row = lax.broadcasted_iota(jnp.int32, (16, 128), 0)
    lane = lax.broadcasted_iota(jnp.int32, (16, 128), 1)
    a0[:, 1536:1664] = jnp.where((row == 0) & (lane >= 64), bias, columns).astype(BF)
    a0[:, 1664:2176] = mix[...]
    a0[:, 2176:4224] = up[...]
    for part in range(4):
        c0[:, 512 * part : 512 * part + 512] = down[16 * part : 16 * part + 16, :]


def pack(qkv, mix, up, down, gain, shift, qv, proj, up_bias):
    return pl.pallas_call(
        pack_kernel,
        in_specs=[vmem()] * 9,
        out_specs=[vmem()] * 2,
        out_shape=[shape((16, 4224), BF), shape((16, 2048), BF)],
        scratch_shapes=[pltpu.VMEM((128, 16), F32)],
        cost_estimate=cost(1.5),
        name="pack",
    )(qkv, mix, up, down, gain, shift, qv, proj, up_bias.reshape(1, 64))


def aux_rows(chain):
    row = lax.broadcasted_iota(jnp.int32, (128, chain.shape[1]), 0)
    low_bits = jnp.where(row < 7, (chain >> jnp.minimum(row, 6)) & 1, 0)
    high_bits = jnp.where(
        (row >= 7) & (row < 14), 1 - ((chain >> jnp.minimum(jnp.maximum(row - 7, 0), 6)) & 1), 0
    )
    bits = low_bits + high_bits
    query_side = bits.astype(F32) * HIDE
    key_side = jnp.where(row < 14, 1 - bits, jnp.where(row < 17, 1, 0)).astype(F32)
    return query_side.astype(BF), key_side.T.astype(BF)


def longest_pair(q2_t, k2):
    wide_q = q2_t.astype(F32)
    wide_k = k2.astype(F32)
    longest_q = jnp.max(jnp.sum(wide_q * wide_q, axis=0, keepdims=True))
    longest_k = jnp.max(jnp.sum(wide_k * wide_k, axis=1, keepdims=True))
    return longest_q * longest_k


def pair_forward(normed, weight, bias_q, bias_v, key_aux, qa, ot, outs, pair, block):
    qkv_out, o_out, ot_out, lse_out = outs
    rows = normed.shape[0]
    cols = block_of(pair, 128)
    q2 = (dot(normed, weight[:, 0:128]) + bias_q).astype(BF)
    k2 = dot(normed, weight[:, 128:256]).astype(BF)
    v2 = (dot(normed, weight[:, 256:384]) + bias_v).astype(BF)
    for index, value in enumerate((q2, k2, v2)):
        qkv_out[pair, index] = value
    qa[0:128, :] = q2.T
    vt = v2.T
    ones = (lax.broadcasted_iota(jnp.int32, (16, rows), 0) == 0).astype(F32).astype(BF)
    lane = lax.broadcasted_iota(jnp.int32, k2.shape, 1)
    zero = jnp.zeros_like(k2)
    keys = [
        jnp.concatenate([jnp.where((lane >= 64) == bool(h), k2, zero), key_aux], axis=1)
        for h in range(2)
    ]
    vts = [jnp.concatenate([vt[64 * h : 64 * h + 64], ones], axis=0) for h in range(2)]
    count = rows // block

    def score(index):
        q_cols = qa[:, block * index : block * index + block]
        return [dot(keys[h], q_cols) for h in range(2)]

    def attend(shifted):
        ahead = score(0)
        for index in range(count):
            scores = ahead
            if index + 1 < count:
                ahead = score(index + 1)
            span = slice(block * index, block * index + block)
            for h in range(2):
                if shifted:
                    peak = jnp.max(scores[h], axis=0, keepdims=True)
                    probs = jnp.exp2((scores[h] - peak) * EXP_SCALE).astype(BF)
                else:
                    peak = 0.0
                    probs = jnp.exp2(scores[h] * EXP_SCALE).astype(BF)
                mixed = dot(vts[h], probs)
                total = mixed[64:65]
                ot[64 * h : 64 * h + 64, span] = mixed[:64] * (1.0 / total)
                lse_out[pair, h : h + 1, span] = peak + jnp.log(total) * (1.0 / SCALE)

    bound = longest_pair(qa[0:128, :], k2) * (EXP_SCALE * EXP_SCALE)
    small = bound < 90.0 * 90.0

    @pl.when(small)
    def _():
        attend(False)

    @pl.when(jnp.logical_not(small))
    def _():
        attend(True)

    ot_out[cols, :] = ot[...].astype(BF)
    o_out[:, cols] = ot[...].T.astype(BF)


def forward_kernel(me_ref, tokens, chain, mine, other, *refs):
    qkv_hbm, normed_t_hbm, weight_hbm, o_out, ot_out, lse_out = refs[:6]
    smalls, up_row, key_aux_out, query_aux_out = refs[6:10]
    qa, ot, columns, qkv_out, normed_out, normed_t, weight, sems = refs[10:]
    me = me_ref[1]
    for c, j, i in slots():
        source = (mine, other)[c]
        row = block_row(me, c, j, i, 16)
        weight[pl.ds(row, 16), :] = source[4 * j + i, :, 0:1536]
        columns[pl.ds(row, 16), :] = source[4 * j + i, :, 1536:1664].astype(F32)
    smalls[...] = columns[...].T[0:8, :]
    lane = lax.broadcasted_iota(jnp.int32, (1, 128), 1)
    for a in range(16):
        even = pltpu.roll(columns[32 * a : 32 * a + 8, :], 64, 1)[0:1, :]
        odd = columns[32 * a + 16 : 32 * a + 17, :]
        up_row[:, 128 * a : 128 * a + 128] = jnp.where(lane < 64, even, odd)
    query_side, key_side = aux_rows(chain[...])
    qa[128:256, :] = query_side
    query_aux_out[...] = query_side
    key_aux_out[...] = key_side

    def norm_block(index, carry):
        span = block_of(index, 512)
        centred, scale = row_stats(tokens[span, :].astype(F32))
        normed_out[span, :] = (centred * scale * smalls[0:1, :] + smalls[2:3, :]).astype(BF)
        return carry

    lax.fori_loop(0, tokens.shape[0] // 512, norm_block, 0)
    normed = normed_out[...]
    normed_t[0:512, :] = normed.T
    ones_row = lax.broadcasted_iota(jnp.int32, (16, normed.shape[0]), 0) == 0
    normed_t[512:528, :] = ones_row.astype(F32).astype(BF)
    copies = [
        pltpu.make_async_copy(normed_t, normed_t_hbm, sems.at[4]),
        pltpu.make_async_copy(weight, weight_hbm, sems.at[5]),
    ]
    for copy in copies:
        copy.start()
    outs = (qkv_out, o_out, ot_out, lse_out)

    def one_pair(pair, carry):
        cols = block_of(pair, 128)
        pair_forward(
            normed_out[...], weight[:, block_of(pair, 384)], smalls[4:5, cols], smalls[5:6, cols],
            key_aux_out[...], qa, ot, outs, pair, 512,
        )
        pltpu.make_async_copy(qkv_out.at[pair], qkv_hbm.at[pair], sems.at[pair]).start()
        return carry

    lax.fori_loop(0, 4, one_pair, 0)
    for pair in range(4):
        pltpu.make_async_copy(qkv_out.at[pair], qkv_hbm.at[pair], sems.at[pair]).wait()
    for copy in copies:
        copy.wait()


def hbm():
    return pl.BlockSpec(memory_space=pltpu.HBM)


def forward(me, tokens, chain, mine, other):
    rows = tokens.shape[0]
    return pl.pallas_call(
        forward_kernel,
        in_specs=[smem()] + [vmem()] * 4,
        out_specs=[hbm()] * 3 + [vmem()] * 7,
        out_shape=[
            shape((4, 3, rows, 128), BF),
            shape((528, rows), BF),
            shape((512, 1536), BF),
            shape((rows, 512), BF),
            shape((512, rows), BF),
            shape((4, 2, rows), F32),
            shape((8, 512), F32),
            shape((1, 2048), F32),
            shape((rows, 128), BF),
            shape((128, rows), BF),
        ],
        scratch_shapes=[
            pltpu.VMEM((256, rows), BF),
            pltpu.VMEM((128, rows), F32),
            pltpu.VMEM((512, 128), F32),
            pltpu.VMEM((4, 3, rows, 128), BF),
            pltpu.VMEM((rows, 512), BF),
            pltpu.VMEM((528, rows), BF),
            pltpu.VMEM((512, 1536), BF),
            pltpu.SemaphoreType.DMA((6,)),
        ],
        compiler_params=pltpu.CompilerParams(vmem_limit_bytes=20 * MIB),
        cost_estimate=cost(15),
        name="attend",
    )(me, tokens, chain, mine, other)


def gelu_parts(u):
    half_cdf = 0.5 + 0.5 * lax.erf(u * math.sqrt(0.5))
    density = jnp.exp2(u * u * (-0.5 * math.log2(math.e))) * (1.0 / math.sqrt(2.0 * math.pi))
    return u * half_cdf, half_cdf + u * density


def scatter_tall(me, source, base_block, send, keep):
    core = me & 1
    for half in range(4):
        r = (me ^ (base_block + 2 * half)) >> 1
        place = ((r & 3) << 2) | (r >> 2)
        for part in range(4):
            row = 128 * half + 16 * part
            span = slice(512 * part, 512 * part + 512)
            keep[place, :, span] = source[pl.ds(pl.multiple_of(row + core * 64, 16), 16), :]
            sent = source[pl.ds(pl.multiple_of(row + (1 - core) * 64, 16), 16), :]
            send[place, :, span] = sent.astype(BF)


def scatter_blocks(me, source, rows, base_block, blocks, send, keep, span):
    core = me & 1
    for half in range(blocks // 2):
        first = base_block + 2 * half
        row = 2 * half * rows
        r = (me ^ first) >> 1
        place = ((r & 3) << 2) | (r >> 2)
        kept = source[pl.ds(pl.multiple_of(row + core * rows, rows), rows), :]
        sent = source[pl.ds(pl.multiple_of(row + (1 - core) * rows, rows), rows), :]
        keep[place, :, span] = kept
        send[place, :, span] = sent.astype(BF)


def feed_first_kernel(
    me_ref, tokens, o_in, mine, other, mine_tall, other_tall, smalls, up_row, cot,
    middle, normed_t, grad_pre_out, d_send, d_keep, mix, up, act_rows, down,
    normed, stage,
):
    me = me_ref[0]
    for c, j, i in slots():
        source = (mine, other)[c]
        row = block_row(me, c, j, i, 16)
        mix[pl.ds(row, 16), :] = source[4 * j + i, :, 0:512]
        up[pl.ds(row, 16), :] = source[4 * j + i, :, 512:2560]
        source = (mine_tall, other_tall)[c]
        for part in range(4):
            row = pl.multiple_of(block_row(me, c, j, i, 64) + 16 * part, 16)
            span = slice(512 * part, 512 * part + 512)
            down[pl.ds(row, 16), :] = source[4 * TALL_ORDER[i] + j, :, span]
    rows = tokens.shape[0]
    block = 512

    def ahead(index, carry):
        span = pl.ds(pl.multiple_of(index * block, block), block)
        mid = tokens[span, :].astype(F32) + dot(o_in[span, :], mix[...]) + smalls[6:7, :]
        middle[span, :] = mid
        centred, scale = row_stats(mid)
        normed[span, :] = (centred * scale * smalls[1:2, :] + smalls[3:4, :]).astype(BF)
        return carry

    lax.fori_loop(0, rows // block, ahead, 0)
    normed_t[0:512, :] = normed[...].T
    ones_row = lax.broadcasted_iota(jnp.int32, (16, rows), 0) == 0
    normed_t[512:528, :] = ones_row.astype(F32).astype(BF)
    width = 512

    def one_chunk(chunk, carry):
        span = block_of(chunk, width)
        down_part = down[span, :]
        act, slope = gelu_parts(dot(normed[...], up[:, span]) + up_row[:, span])
        act_low = act.astype(BF)
        grad_pre_out[:, span] = (dot(cot[...], down_part, NT) * slope).astype(BF)
        act_rows[:, span] = act_low
        stage[...] = dot(act_low, cot[...], TN)
        scatter_tall(me, stage, chunk * (width // 64), d_send, d_keep)
        return carry

    lax.fori_loop(0, 2048 // width, one_chunk, 0)


def feed_first(me, tokens, o_in, b_pair, c_pair, smalls, up_row, cot):
    rows = tokens.shape[0]
    return pl.pallas_call(
        feed_first_kernel,
        in_specs=[smem()] + [vmem()] * 9,
        out_specs=[vmem()] * 9,
        out_shape=[
            shape((rows, 512), F32),
            shape((528, rows), BF),
            shape((rows, 2048), BF),
            shape((16, 16, 2048), BF),
            shape((16, 16, 2048), F32),
            shape((512, 512), BF),
            shape((512, 2048), BF),
            shape((rows, 2048), BF),
            shape((2048, 512), BF),
        ],
        scratch_shapes=[
            pltpu.VMEM((rows, 512), BF),
            pltpu.VMEM((512, 512), F32),
        ],
        compiler_params=pltpu.CompilerParams(vmem_limit_bytes=14 * MIB),
        cost_estimate=cost(18),
        name="feed_first",
    )(me, tokens, o_in, *b_pair, *c_pair, smalls, up_row, cot)


def feed_second_kernel(me_ref, normed_t, grad_pre, u_send, u_keep, up_bias_grad, stage):
    me = me_ref[0]
    width = 1024

    def one_chunk(chunk, carry):
        span = block_of(chunk, width)
        stage[...] = dot(normed_t[...], grad_pre[:, span])
        up_bias_grad[:, span] = stage[512:513, :]
        scatter_blocks(me, stage, 16, 0, 32, u_send, u_keep, span)
        return carry

    lax.fori_loop(0, 2048 // width, one_chunk, 0)


def feed_second(me, normed_t, grad_pre):
    return pl.pallas_call(
        feed_second_kernel,
        in_specs=[smem()] + [vmem()] * 2,
        out_specs=[vmem()] * 3,
        out_shape=[
            shape((16, 16, 2048), BF),
            shape((16, 16, 2048), F32),
            shape((1, 2048), F32),
        ],
        scratch_shapes=[pltpu.VMEM((528, 1024), F32)],
        compiler_params=pltpu.CompilerParams(vmem_limit_bytes=12 * MIB),
        cost_estimate=cost(5),
        name="feed_second",
    )(me, normed_t, grad_pre)


def feed_third_kernel(
    middle, grad_pre, mix, up, smalls, cot, ot_in,
    grad_middle, grad_att, mix_grad, small_grads, low_rows,
):
    rows = middle.shape[0]
    block = 512

    def behind(index, carry):
        gain_sum, shift_sum, branch_sum, cot_sum = carry
        span = pl.ds(pl.multiple_of(index * block, block), block)
        centred, scale = row_stats(middle[span, :])
        xh = centred * scale
        h = dot(grad_pre[span, :], up[...], NT)
        hg = h * smalls[1:2, :]
        cot_rows = cot[span, :].astype(F32)
        grad = cot_rows + scale * (
            hg
            - jnp.mean(hg, axis=-1, keepdims=True)
            - xh * jnp.mean(hg * xh, axis=-1, keepdims=True)
        )
        grad_middle[span, :] = grad
        low = grad.astype(BF)
        low_rows[span, :] = low
        grad_att[span, :] = dot(low, mix[...], NT).astype(BF)
        return (
            gain_sum + jnp.sum(h * xh, axis=0, keepdims=True),
            shift_sum + jnp.sum(h, axis=0, keepdims=True),
            branch_sum + jnp.sum(low.astype(F32), axis=0, keepdims=True),
            cot_sum + jnp.sum(cot_rows, axis=0, keepdims=True),
        )

    zero = jnp.zeros((1, 512), F32)
    sums = lax.fori_loop(0, rows // block, behind, (zero, zero, zero, zero))
    for index in range(4):
        small_grads[index : index + 1, :] = sums[index]
    small_grads[4:8, :] = jnp.zeros((4, 512), F32)
    mix_grad[0:256, :] = dot(ot_in[0:256, :], low_rows[...])
    mix_grad[256:512, :] = dot(ot_in[256:512, :], low_rows[...])


def feed_third(middle, grad_pre, mix, up, smalls, cot, ot_in):
    rows = middle.shape[0]
    return pl.pallas_call(
        feed_third_kernel,
        in_specs=[vmem()] * 7,
        out_specs=[vmem()] * 4,
        out_shape=[
            shape((rows, 512), F32),
            shape((rows, 512), BF),
            shape((512, 512), F32),
            shape((8, 512), F32),
        ],
        scratch_shapes=[pltpu.VMEM((rows, 512), BF)],
        compiler_params=pltpu.CompilerParams(vmem_limit_bytes=14 * MIB),
        cost_estimate=cost(8),
        name="feed_third",
    )(middle, grad_pre, mix, up, smalls, cot, ot_in)


def pair_backward(q, k, v, do, ot_in, lse, key_aux, qa, da, dqt, acc_k, acc_v, gm, block):
    k2 = k[0, 0]
    v2 = v[0, 0]
    rows = k2.shape[0]
    kt = k2.T
    lane = lax.broadcasted_iota(jnp.int32, k2.shape, 1)
    zero = jnp.zeros_like(k2)
    keys = []
    vals = []
    for h in range(2):
        own = (lane >= 64) == bool(h)
        keys.append(jnp.concatenate([jnp.where(own, k2, zero), key_aux], axis=1))
        vals.append(jnp.concatenate([jnp.where(own, v2, zero), key_aux], axis=1))
    qt = q[0, 0].T
    dt = do[...].T
    product = dt.astype(F32) * ot_in[...].astype(F32)
    row = lax.broadcasted_iota(jnp.int32, (16, rows), 0)
    for h in range(2):
        qa[h, 0:128, :] = qt
        da[h, 0:128, :] = dt
        delta = jnp.sum(product[64 * h : 64 * h + 64], axis=0, keepdims=True)
        base = qa[h, 128:144, :].astype(F32)
        one, two, three = split_three(-lse[0, h : h + 1, :])
        base = jnp.where(row == 14, one, jnp.where(row == 15, two, base))
        qa[h, 128:144, :] = base.astype(BF)
        qa[h, 144:160, :] = jnp.where(row == 0, three, 0.0).astype(BF)
        one, two, three = split_three(-delta)
        base = jnp.where(row == 14, one, jnp.where(row == 15, two, 0.0))
        da[h, 128:144, :] = base.astype(BF)
        da[h, 144:160, :] = jnp.where(row == 0, three, 0.0).astype(BF)
    small_lane = lax.broadcasted_iota(jnp.int32, (block, 128), 1)
    for index in range(rows // block):
        span = slice(block * index, block * index + block)
        do_rows = do[span, :]
        q_rows = q[0, 0, span, :]
        blank = jnp.zeros_like(do_rows)
        sum_k = None
        sum_v = None
        for h in range(2):
            own = (small_lane >= 64) == bool(h)
            probs = jnp.exp2(dot(keys[h], qa[h, :, span]) * EXP_SCALE)
            grad = (probs * dot(vals[h], da[h, :, span])).astype(BF)
            probs = probs.astype(BF)
            dqt[64 * h : 64 * h + 64, span] = dot(kt[64 * h : 64 * h + 64, :], grad)
            part_k = dot(grad, jnp.where(own, q_rows, blank))
            part_v = dot(probs, jnp.where(own, do_rows, blank))
            sum_k = part_k if sum_k is None else sum_k + part_k
            sum_v = part_v if sum_v is None else sum_v + part_v
        if index == 0:
            acc_k[...] = sum_k
            acc_v[...] = sum_v
        else:
            acc_k[...] += sum_k
            acc_v[...] += sum_v
    gm[:, 0:128] = (dqt[...].T * SCALE).astype(BF)
    gm[:, 128:256] = (acc_k[...] * SCALE).astype(BF)
    gm[:, 256:384] = acc_v[...].astype(BF)


def backward_kernel(
    me_ref, q, k, v, do, ot_in, lse, weight, key_aux, query_aux, normed_t, smalls, small_grads,
    up_bias_grad, mix_term, gm, send, keep,
    qa, da, dqt, acc_k, acc_v, gm_pair, stage, sums, vectors, columns,
):
    me = me_ref[0]
    pair = pl.program_id(0)

    @pl.when(pair == 0)
    def _():
        for h in range(2):
            qa[h, 128:256, :] = query_aux[...]
            da[h, 128:256, :] = jnp.zeros((128, da.shape[2]), BF)
        vectors[...] = jnp.zeros_like(vectors)
        scatter_blocks(me, mix_term, 16, 0, 32, send, keep, slice(1536, 2048))

    pair_backward(q, k, v, do, ot_in, lse, key_aux[...], qa, da, dqt, acc_k, acc_v, gm_pair, 512)
    span = block_of(pair, 384)
    gm[:, span] = gm_pair[...]
    stage[...] = dot(normed_t[...], gm_pair[...])
    total = stage[512:513, :]
    sums[:, span] = jnp.broadcast_to(total, (8, 384))
    scatter_blocks(me, stage, 16, 0, 32, send, keep, span)
    wide = weight[...].astype(F32)
    for index, product in enumerate((stage[0:512, :] * wide, wide * total)):
        vectors[index] += product[:, 0:128] + product[:, 128:256] + product[:, 256:384]

    @pl.when(pair == 3)
    def _():
        columns[...] = jnp.zeros_like(columns)
        columns[1:2, :] = small_grads[0:1, :]
        columns[3:4, :] = small_grads[1:2, :]
        for index in range(4):
            cols = slice(128 * index, 128 * index + 128)
            columns[4:5, cols] = sums[0:1, 384 * index : 384 * index + 128]
            columns[5:6, cols] = sums[0:1, 384 * index + 256 : 384 * index + 384]
        columns[6:7, :] = small_grads[2:3, :]
        columns[7:8, :] = small_grads[3:4, :]
        columns[8:9, :] = smalls[0:1, :]
        columns[9:10, :] = smalls[2:3, :]
        tile = columns[...].T
        plain = jnp.sum(vectors[1], axis=1, keepdims=True)
        weighted = jnp.sum(vectors[0], axis=1, keepdims=True)
        gain_sum = (weighted - tile[:, 9:10] * plain) / tile[:, 8:9]
        lanes = lax.broadcasted_iota(jnp.int32, (512, 128), 1)
        stage[0:512, 0:128] = jnp.where(lanes == 0, gain_sum, jnp.where(lanes == 2, plain, tile))
        lane = lax.broadcasted_iota(jnp.int32, (1, 128), 1)
        for a in range(16):
            piece = up_bias_grad[:, 128 * a : 128 * a + 128]
            rolled = pltpu.roll(jnp.broadcast_to(piece, (8, 128)), 64, 1)[0:1, :]
            for half, values in enumerate((rolled, piece)):
                row = 32 * a + 16 * half
                old = stage[row : row + 1, 0:128]
                stage[row : row + 1, 0:128] = jnp.where(lane < 64, old, values)
        core = me & 1
        for half in range(16):
            r = (me ^ (2 * half)) >> 1
            place = ((r & 3) << 2) | (r >> 2)
            kept = pl.multiple_of(32 * half + core * 16, 16)
            sent = pl.multiple_of(32 * half + (1 - core) * 16, 16)
            keep[place, :, 2048:2176] = stage[pl.ds(kept, 16), 0:128]
            send[place, :, 2048:2176] = stage[pl.ds(sent, 16), 0:128].astype(BF)


def backward(me, qkv_rows, do, ot, lse, weight, *rest):
    rows = do.shape[0]
    parts = [pl.BlockSpec((1, 1, rows, 128), lambda i, part=part: (i, part, 0, 0)) for part in range(3)]
    return pl.pallas_call(
        backward_kernel,
        grid=(4,),
        in_specs=[smem()]
        + parts
        + [
            pl.BlockSpec((rows, 128), lambda i: (0, i)),
            pl.BlockSpec((128, rows), lambda i: (i, 0)),
            pl.BlockSpec((1, 2, rows), lambda i: (i, 0, 0)),
            pl.BlockSpec((512, 384), lambda i: (0, i)),
        ]
        + [vmem()] * 7,
        out_specs=[vmem()] * 3,
        out_shape=[
            shape((rows, 1536), BF),
            shape((16, 16, 2176), BF),
            shape((16, 16, 2176), F32),
        ],
        scratch_shapes=[
            pltpu.VMEM((2, 256, rows), BF),
            pltpu.VMEM((2, 256, rows), BF),
            pltpu.VMEM((128, rows), F32),
            pltpu.VMEM((rows, 128), F32),
            pltpu.VMEM((rows, 128), F32),
            pltpu.VMEM((rows, 384), BF),
            pltpu.VMEM((528, 384), F32),
            pltpu.VMEM((8, 1536), F32),
            pltpu.VMEM((2, 512, 128), F32),
            pltpu.VMEM((128, 512), F32),
        ],
        compiler_params=pltpu.CompilerParams(vmem_limit_bytes=20 * MIB),
        cost_estimate=cost(25),
        name="attend_back",
    )(me, qkv_rows, qkv_rows, qkv_rows, do, ot, lse, weight, *rest)


def input_kernel(
    tokens, gm, weight, smalls, grad_middle, act, down, middle, input_grad, output
):
    block = 256

    def behind(index, carry):
        span = pl.ds(pl.multiple_of(index * block, block), block)
        centred, scale = row_stats(tokens[span, :].astype(F32))
        xh = centred * scale
        total = middle[span, :] + dot(act[span, :], down[...]) + smalls[7:8, :]
        output[span, :] = total.astype(BF)
        hg = dot(gm[span, :], weight[...], NT) * smalls[0:1, :]
        input_grad[span, :] = grad_middle[span, :] + scale * (
            hg
            - jnp.mean(hg, axis=-1, keepdims=True)
            - xh * jnp.mean(hg * xh, axis=-1, keepdims=True)
        )
        return carry

    lax.fori_loop(0, tokens.shape[0] // block, behind, 0)


def input_terms(operands):
    rows = operands[0].shape[0]
    return pl.pallas_call(
        input_kernel,
        in_specs=[vmem()] * 8,
        out_specs=[vmem()] * 2,
        out_shape=[shape((rows, 512), F32), shape((rows, 512), BF)],
        compiler_params=pltpu.CompilerParams(vmem_limit_bytes=12 * MIB),
        cost_estimate=cost(8),
        name="input_terms",
    )(*operands)


def combine_kernel(counts, pieces, *refs):
    total_in = sum(counts) + len(counts)
    outs = refs[total_in:]
    position = 0
    base = 0
    for count in counts:
        own, incoming = refs[position], refs[position + 1 : position + 1 + count]
        position += 1 + count
        width = own.shape[2]
        rows = own.shape[0] // pieces
        for index in range(pieces):
            span = slice(rows * index, rows * index + rows)
            total = own[span]
            for ref in incoming:
                total = total + ref[span].astype(F32)
            outs[index][:, :, base : base + width] = total.astype(outs[index].dtype)
        base += width


def combine(name, pieces, *sums):
    slot_count = sums[0][0].shape[0] // pieces
    width = sum(own.shape[2] for own, _ in sums)
    operands = [part for own, received in sums for part in (own, *received)]
    dims = (slot_count, 16, width)
    first, *rest = pl.pallas_call(
        functools.partial(combine_kernel, [len(received) for _, received in sums], pieces),
        in_specs=[vmem()] * len(operands),
        out_specs=[vmem()] * pieces,
        out_shape=[shape(dims, F32)] + [shape(dims, BF)] * (pieces - 1),
        compiler_params=pltpu.CompilerParams(vmem_limit_bytes=8 * MIB),
        cost_estimate=cost(1.5),
        name=name,
    )(*operands)
    return first, rest


def last_kernel(g_own, g0, g1, g2, du_own, du_recv, own, du_first, p0, p1, p2):
    width = g_own.shape[2]
    for index in range(4):
        total = g_own[index]
        for ref in (g0, g1, g2):
            total = total + ref[index].astype(F32)
        if index == 0:
            own[0] = total
        else:
            (p0, p1, p2)[index - 1][0, :, 0:width] = total.astype(BF)
    du_first[0] = du_own[0] + du_recv[0].astype(F32)
    p0[0, :, width:] = (du_own[1] + du_recv[1].astype(F32)).astype(BF)


def last_sums(g_own, g_recv, du_own, du_recv):
    width, wide = g_own.shape[2], du_own.shape[2]
    own, du_first, *parts = pl.pallas_call(
        last_kernel,
        in_specs=[vmem()] * 6,
        out_specs=[vmem()] * 5,
        out_shape=[shape((1, 16, width), F32), shape((1, 16, wide), F32)]
        + [shape((1, 16, width + wide), BF)]
        + [shape((1, 16, width), BF)] * 2,
        compiler_params=pltpu.CompilerParams(vmem_limit_bytes=8 * MIB),
        cost_estimate=cost(1.5),
        name="last_sums",
    )(g_own, *g_recv, du_own, du_recv)
    return own, du_first, parts


def finish_kernel(
    own, r0, r1, r2, du_own,
    qkv_grad, mix_grad, up_grad, down_grad, gain, shift, qv, proj, bias,
):
    total = own[0] + r0[0, :, 0:2176].astype(F32)
    for ref in (r1, r2):
        total = total + ref[0].astype(F32)
    mix_grad[...] = total[:, 1536:2048]
    for pair in range(4):
        for part in range(3):
            base = 384 * pair + 128 * part
            column = 512 * part + 128 * pair
            qkv_grad[:, column : column + 128] = total[:, base : base + 128]
    tile = total[:, 2048:2176]
    wide = jnp.concatenate([tile, jnp.zeros((112, 128), F32)], axis=0).T
    for index, ref in enumerate((gain, shift, qv, proj)):
        ref[...] = wide[2 * index : 2 * index + 2, 0:16]
    bias[...] = tile[0:1, 64:128]
    total = du_own[0] + r0[0, :, 2176:].astype(F32)
    for part in range(4):
        down_grad[16 * part : 16 * part + 16, :] = total[:, 512 * part : 512 * part + 512]
    up_grad[...] = total[:, 2048:4096]


def finish(own, received, du_own):
    return pl.pallas_call(
        finish_kernel,
        in_specs=[vmem()] * 5,
        out_specs=[vmem()] * 9,
        out_shape=[
            shape((16, 1536), F32),
            shape((16, 512), F32),
            shape((16, 2048), F32),
            shape((64, 512), F32),
        ]
        + [shape((2, 16), F32)] * 4
        + [shape((1, 64), F32)],
        compiler_params=pltpu.CompilerParams(vmem_limit_bytes=6 * MIB),
        cost_estimate=cost(1.5),
        name="finish",
    )(own, *received, du_own)


def swap(value, mask, count):
    return lax.ppermute(value, AXES, [(d, d ^ mask) for d in range(count)])


Z_MASKS = (8, 16, 24)
PLANE_MASKS = (2, 4, 6)


def swaps(value, masks, count):
    return [swap(value, mask, count) for mask in masks]


def point(values, *tokens):
    return lax.optimization_barrier((values, tokens))[0]


def after(value, *tokens):
    return lax.optimization_barrier((value, tokens))[0]


def exchange(parts, masks, count):
    return [swap(part, mask, count) for part, mask in zip(parts, masks, strict=True)]


def group(own, others):
    joined = jnp.stack([own] + others)
    return joined.reshape((-1,) + joined.shape[-2:])


def pack_whole(qkv, mix, up, down, gain, shift, qv, proj, up_bias):
    pieces = []
    for pair in range(4):
        for part in range(3):
            base = 512 * part + 128 * pair
            pieces.append(qkv[:, base : base + 128])
    rows = jnp.concatenate([gain, shift, qv, proj], axis=0)
    tile = jnp.pad(rows.T, ((0, 0), (0, 120))).reshape(32, 16, 128)
    tile = tile.at[:, 0, 64:128].set(up_bias.reshape(32, 64))
    a0 = jnp.concatenate([jnp.concatenate(pieces, 1).reshape(32, 16, 1536), tile], axis=2)
    b0 = jnp.concatenate([mix, up], axis=1).reshape(32, 16, 2560)
    b1 = down.reshape(32, 4, 16, 512).swapaxes(1, 2).reshape(32, 16, 2048)
    return a0, b0, b1


def relative_halves(blocks):
    parts = blocks.reshape((4, 4, 2) + blocks.shape[1:])
    parts = parts.transpose((2, 1, 0) + tuple(range(3, parts.ndim)))
    return parts[0].reshape((16,) + blocks.shape[1:]), parts[1].reshape((16,) + blocks.shape[1:])


def whole_blocks(send, keep):
    parts = jnp.stack([keep, send.astype(F32)]).reshape((2, 4, 4) + keep.shape[1:])
    parts = parts.transpose((2, 1, 0) + tuple(range(3, parts.ndim)))
    return parts.reshape((32,) + keep.shape[1:])


def body(cubic, count, tokens, chain_ids, qkv, mix, up, down, gain, shift, qv, proj, up_bias, cot):
    params = (qkv, mix, up, down, gain, shift, qv, proj, up_bias)
    if cubic:
        index = lax.axis_index(AXES).astype(jnp.int32)
        me = jnp.stack([index, index & ~6])
        own, c_own = pack(*params)
        recv = swaps(own, Z_MASKS, count)
        c_recv = swaps(c_own, PLANE_MASKS, count)
        recv = point(recv)
        a_col = jnp.stack([part[:, :1664] for part in (own, *recv)])
        c_plane = group(c_own, after(c_recv, a_col))
        c_recv = swap(c_plane, 16, count)
        a_mine = lax.all_gather(after(a_col, c_plane), "plane").reshape(16, 16, -1)
        a_mine, c_recv = point((a_mine, c_recv))
        a_other = swap(a_mine, 1, count)
        own, *recv = after((own, *recv), a_mine)
        b_col = jnp.stack([part[:, 1664:] for part in (own, *recv)])
        b_recv = swaps(b_col, PLANE_MASKS, count)
        c_half = group(c_plane, [c_recv])
        c_recv = swap(c_half, 8, count)
        a_mine, a_other = after((a_mine, a_other), b_col, c_half)
    else:
        me = jnp.zeros((2,), jnp.int32)
        dims = (0, 0, 0, 0, 1, 1, 1, 1, 0)
        whole = [
            lax.all_gather(value, AXES, axis=dim, tiled=True)
            for value, dim in zip(params, dims, strict=True)
        ]
        a_parts, b_parts, c_parts = pack_whole(*whole)
        a_mine, a_other = relative_halves(a_parts)
        b_pair = relative_halves(b_parts)
        c_pair = [
            half.reshape(4, 2, 2, 16, 2048).transpose(2, 1, 0, 3, 4).reshape(16, 16, 2048)
            for half in relative_halves(c_parts)
        ]
    (
        qkv_rows, normed_t, weight, o, ot, lse, smalls, up_row, key_aux, query_aux,
    ) = forward(me, tokens, chain_ids, a_mine, a_other)
    if cubic:
        b_recv, c_recv, lse = point((b_recv, c_recv, lse))
        b_mine = group(b_col, b_recv)
        c_mine = group(c_half, [c_recv])
        b_pair = (b_mine, swap(b_mine, 1, count))
        c_pair = (c_mine, swap(c_mine, 1, count))
    (
        middle, normed_two_t, grad_pre, d_send, d_keep, mix_whole, up_whole, act_rows, down_whole,
    ) = feed_first(me, tokens, o, b_pair, c_pair, smalls, up_row, cot)
    if cubic:
        d_recv = swap(d_send, 1, count)
    u_send, u_keep, up_bias_grad = feed_second(me, normed_two_t, grad_pre)
    if cubic:
        u_recv = swap(u_send, 1, count)
    grad_middle, grad_att, mix_term, small_grads = feed_third(
        middle, grad_pre, mix_whole, up_whole, smalls, cot, ot
    )
    if cubic:
        d_recv, u_recv, small_grads = point((d_recv, u_recv, small_grads))
        du_own, du_parts = combine("feed_sum", 4, (d_keep, [d_recv]), (u_keep, [u_recv]))
        du_recv = exchange(du_parts, PLANE_MASKS, count)
        lse = after(lse, du_own)
    gm, g_send, g_keep = backward(
        me, qkv_rows, grad_att, ot, lse, weight, key_aux, query_aux, normed_t, smalls, small_grads,
        up_bias_grad, mix_term,
    )
    if cubic:
        du_recv, g_send, gm = point((du_recv, g_send, gm))
        g_recv = swap(g_send, 1, count)
        du_own, du_parts = combine("feed_sum_two", 2, (du_own, du_recv))
        du_recv = exchange(du_parts, (16,), count)
        g_own, g_parts = combine("last_sum", 4, (g_keep, [after(g_recv, du_own)]))
        g_recv = exchange(g_parts, PLANE_MASKS, count)
        smalls = after(smalls, g_own)
    input_grad, output = input_terms(
        [tokens, gm, weight, smalls, grad_middle, act_rows, down_whole, middle]
    )
    if cubic:
        g_recv, du_recv, input_grad = point((g_recv, du_recv, input_grad))
        own, du_own, parts = last_sums(g_own, g_recv, du_own, *du_recv)
        g_recv = exchange(parts, Z_MASKS, count)
        qkv_grad, mix_grad, up_grad, down_grad, *vectors, bias_grad = finish(own, g_recv, du_own)
        return (
            output, input_grad, qkv_grad, mix_grad, up_grad, down_grad, *vectors,
            bias_grad.reshape(64),
        )
    pairs = ((d_send, d_keep), (u_send, u_keep), (g_send, g_keep))
    blocks = [whole_blocks(s, r) for s, r in pairs]
    tiles = blocks[2][:, :, 2048:2176]
    joined = blocks[2].reshape(512, 2176)
    wholes = (
        blocks[0].reshape(32, 16, 4, 512).swapaxes(1, 2).reshape(2048, 512),
        blocks[1].reshape(512, 2048),
        joined[:, 1536:2048],
        joined[:, :1536].reshape(512, 4, 3, 128).swapaxes(1, 2).reshape(512, 1536),
        tiles[:, 0, 64:128].reshape(2048),
    )
    down_grad, up_grad, mix_grad, qkv_grad, bias_grad = [
        lax.psum_scatter(value, AXES, scatter_dimension=0, tiled=True) for value in wholes
    ]
    vectors = lax.psum_scatter(
        tiles[:, :, 0:8].reshape(512, 8).T, AXES, scatter_dimension=1, tiled=True
    )
    return (
        output, input_grad, qkv_grad, mix_grad, up_grad, down_grad,
        vectors[0:2], vectors[2:4], vectors[4:6], vectors[6:8], bias_grad,
    )


def solution(mesh):
    groups = mesh.shape["dp"]
    count = groups * mesh.shape["fsdp"]
    inner = jax.sharding.Mesh(mesh.devices.reshape(groups, -1, 2), AXES)
    cubic = inner.devices.shape == (4, 4, 2)

    def entry(*operands):
        return body(cubic, count, *operands)

    rows = P(AXES, None)
    columns = P(None, AXES)
    flat = P(AXES)
    return jax.shard_map(
        entry,
        mesh=inner,
        in_specs=(rows,) * 6 + (columns,) * 4 + (flat, rows),
        out_specs=(rows,) * 6 + (columns,) * 4 + (flat,),
        check_vma=False,
    )
```
